512 devices in a mesh: slab: 32 (over z, x), head: 8 (over y_lo, core), cfg: 2 (over y_hi).
Axes of the slice: x: 4, y: 8 (y_hi: 2, y_lo: 4; y = y_hi * 4 + y_lo), z: 8, core: 2. Of those that a mesh axis runs over, the one named last changes fastest.
Arguments:
- tokens: bfloat16 [8192, 3072], P(('cfg', 'slab'), 'head'), parts along dimension 0, may hold values from -20 to 20
- q_weight: bfloat16 [3072, 3072], P('slab', 'head'), may hold values from -0.109375 to 0.109375
- k_weight: bfloat16 [3072, 3072], P('slab', 'head'), may hold values from -0.109375 to 0.109375
- v_weight: bfloat16 [3072, 3072], P('slab', 'head'), may hold values from -0.109375 to 0.109375
- out_weight: bfloat16 [3072, 3072], P('head', 'slab'), may hold values from -0.109375 to 0.109375
- q_gain: float32 [128], replicated, may hold values from 1 to 2.5
- k_gain: float32 [128], replicated, may hold values from 1 to 2.5
- key_tiles: int32 [24, 64, 6], P('head', 'slab'), may hold values from -1 to 63, as said below
Outputs:
- mixed: bfloat16 [8192, 3072], P(('cfg', 'slab'), 'head'), parts along dimension 0
The draws below stay inside these ranges and needn't reach their ends.
There are 2 independent parts, one for each index of `cfg`. The reference program is written for one: setup_inputs(seed, part) draws one part's arguments, and reference() takes and returns one part's arrays. A program takes and returns all parts, laid end to end along the dimension named above; an argument that names none is the same for every part. Nothing has to cross between parts.
Inputs may be any that keep to these rules, and one draw needn't show every extreme that they name: `key_tiles`: for head h and query tile t of frame f, the row lists in increasing order the tiles of frames f - 1, f and f + 1 whose tile row and tile column lie within that head's reach of t's (a reach of its own for each head, for rows and for columns), then -1 in the remaining slots. Tiles are numbered by frame, then tile row, then tile column; every list holds t itself.
All inputs are finite; a program needn't handle non-finite values.
Results may differ from the reference program's by a relative error of at most 0.018.
Values may be sent and summed in bfloat16 or wider, within the bound.
No kernel may reach another device: no remote copies, remote signals or barrier semaphores. Data moves between devices by JAX's collectives and lax.ppermute only.
A program may use at most 64 MiB of HBM per device.

```python
import math
import jax
import jax.numpy as jnp
from jax import lax

HEADS = 24
HDIM = 128
D = 3072
TILE = 64
TH = 2
TW = 1
FRAMES = 32
TOKENS = 4096
TILES = 64
WIN = 6
N_HEAD = 8


def draw_tokens(key, part):
    key = jax.random.fold_in(key, 1)
    key_base, key_rows = jax.random.split(key, 2)
    base = jnp.clip(jax.random.normal(key_base, (TOKENS, D), jnp.float32), -4.0, 4.0)
    row_scale = jnp.exp(jax.random.uniform(key_rows, (TOKENS, 1), jnp.float32, math.log(0.5), math.log(5.0)))
    return (base * row_scale).astype(jnp.bfloat16)


def draw_key_tiles(key, part):
    key = jax.random.fold_in(key, 2)
    key_rows, key_cols = jax.random.split(key)
    tiles_frame = TH * TW
    reach_rows = jax.random.randint(key_rows, (HEADS, 1, 1), 0, TH)
    reach_cols = jax.random.randint(key_cols, (HEADS, 1, 1), 0, TW)
    query = jnp.arange(TILES, dtype=jnp.int32)[None, :, None]
    slot = jnp.arange(WIN, dtype=jnp.int32)[None, None, :]
    frame = query // tiles_frame
    q_row = query % tiles_frame // TW
    q_col = query % TW
    candidate = (frame - 1) * tiles_frame + slot
    c_frame = frame - 1 + slot // tiles_frame
    c_row = slot % tiles_frame // TW
    c_col = slot % TW
    valid = (c_frame >= 0) & (c_frame < FRAMES)
    valid = valid & (jnp.abs(c_row - q_row) <= reach_rows) & (jnp.abs(c_col - q_col) <= reach_cols)
    beyond = TILES * 4
    ordered = jnp.sort(jnp.where(valid, candidate, beyond), axis=-1)
    return jnp.where(ordered == beyond, -1, ordered).astype(jnp.int32)


def steps_of(key, shape, pieces, smallest, top_value):
    def one(axis_at, parts):
        heights = jax.random.uniform(jax.random.fold_in(jax.random.fold_in(key, 6), axis_at), (parts,), jnp.float32, smallest / len(pieces), top_value / len(pieces))
        return jnp.repeat(jnp.exp(heights), shape[axis_at] // parts).reshape((-1,) + (1,) * (len(shape) - axis_at - 1))

    level = one(*pieces[0])
    for cut in pieces[1:]:
        level = level * one(*cut)
    return level


def gaussian(stream_key, shape, scale, most, pieces=(), held_as=jnp.bfloat16):
    entries = jax.random.normal(stream_key, shape, jnp.float32) * scale
    if len(pieces) > 0:
        entries = steps_of(stream_key, shape, pieces, -0.22, 0.18) * entries
    return jnp.clip(entries, min=-most, max=most).astype(held_as)


def setup_inputs(seed: int = 0, part: int = 0) -> dict:
    streams_of = jax.random.split(jax.random.key(seed), 9)
    part_splits = jax.random.split(jax.random.fold_in(streams_of[8], part), 9)
    return {
        "tokens": draw_tokens(jax.random.fold_in(jax.random.fold_in(streams_of[8], part), 71), part),
        "q_weight": gaussian(streams_of[1], (D, D), D ** -0.5, 0.109375, ((0, 32), (1, 8))),
        "k_weight": gaussian(streams_of[2], (D, D), D ** -0.5, 0.109375, ((0, 32), (1, 8))),
        "v_weight": gaussian(streams_of[3], (D, D), D ** -0.5, 0.109375, ((0, 32), (1, 8))),
        "out_weight": gaussian(streams_of[4], (D, D), D ** -0.5, 0.109375, ((0, 8), (1, 32))),
        "q_gain": jnp.clip(jax.random.uniform(streams_of[5], (HDIM,), jnp.float32, 1.0, 2.5), 1.0, 2.5),
        "k_gain": jnp.clip(jax.random.uniform(streams_of[6], (HDIM,), jnp.float32, 1.0, 2.5), 1.0, 2.5),
        "key_tiles": draw_key_tiles(jax.random.fold_in(streams_of[8], 71), part),
    }


def head_norm(matrix, gain):
    shaped = matrix.reshape(matrix.shape[0], -1, HDIM)
    scaled = shaped * lax.rsqrt(lax.optimization_barrier(jnp.mean(shaped * shaped, axis=-1, keepdims=True)) + 1e-06) * gain
    return scaled.reshape(matrix.shape[0], -1).astype(jnp.bfloat16)

def reference(tokens, q_weight, k_weight, v_weight, out_weight, q_gain, k_gain, key_tiles):
    query = jnp.dot(tokens, q_weight, preferred_element_type=jnp.float32)
    key = jnp.dot(tokens, k_weight, preferred_element_type=jnp.float32)
    value = jnp.dot(tokens, v_weight, preferred_element_type=jnp.float32)
    q_norm = head_norm(query, q_gain)
    k_norm = head_norm(key, k_gain)
    v_cast = value.astype(jnp.bfloat16)
    tiles_frame = TH * TW
    rows = tiles_frame * TILE
    k_padded = jnp.pad(k_norm, ((rows, rows), (0, 0)))
    v_padded = jnp.pad(v_cast, ((rows, rows), (0, 0)))
    scale = 1.0 / HDIM ** 0.5
    anchor = jnp.zeros((), jnp.int32)

    def per_head(head):
        head_col = (head * HDIM).astype(jnp.int32)

        def per_frame(frame):
            row_start = (frame * rows).astype(jnp.int32)
            tile_start = (frame * tiles_frame).astype(jnp.int32)
            q_head = lax.dynamic_slice(q_norm, (row_start, head_col), (rows, HDIM))
            k_head = lax.dynamic_slice(k_padded, (row_start, head_col), (3 * rows, HDIM))
            v_head = lax.dynamic_slice(v_padded, (row_start, head_col), (3 * rows, HDIM))
            listed = lax.dynamic_slice(key_tiles, (head.astype(jnp.int32), tile_start, anchor), (1, tiles_frame, WIN))[0]
            near_ids = ((frame - 1) * tiles_frame).astype(jnp.int32) + jnp.arange(3 * tiles_frame, dtype=jnp.int32)
            live = jnp.any(listed[:, :, None] == near_ids[None, None, :], axis=1)
            allowed = jnp.repeat(jnp.repeat(live, TILE, axis=0), TILE, axis=1)
            score = jnp.dot(q_head, k_head.T, preferred_element_type=jnp.float32) * scale
            weight = jnp.where(allowed, jnp.exp(score), jnp.zeros_like(score))
            total = lax.optimization_barrier(jnp.sum(weight, axis=1))
            summed = jnp.dot(weight.astype(jnp.bfloat16), v_head, preferred_element_type=jnp.float32)
            return (summed / total[:, None]).astype(jnp.bfloat16)
        return lax.map(per_frame, jnp.arange(FRAMES, dtype=jnp.int32))
    attended = lax.map(per_head, jnp.arange(HEADS, dtype=jnp.int32))
    attended = attended.transpose(1, 2, 0, 3).reshape(TOKENS, HEADS * HDIM)
    group_width = HEADS // N_HEAD * HDIM
    result = jnp.zeros((TOKENS, D), jnp.float32)
    for group in range(N_HEAD):
        partial_sum = jnp.dot(attended[:, group * group_width:(group + 1) * group_width], out_weight[group * group_width:(group + 1) * group_width, :], preferred_element_type=jnp.float32).astype(jnp.bfloat16)
        partial_sum = lax.optimization_barrier(partial_sum)
        result = result + partial_sum.astype(jnp.float32)
    return result.astype(jnp.bfloat16)
```

```python
import jax
import jax.numpy as jnp
from jax import lax
from jax.sharding import Mesh
from jax.sharding import PartitionSpec as P

HDIM = 128
TILE = 64
HEAD = ("y", "core")
SLAB = ("z", "x")


def head_norm(shaped, gain):
    scaled = shaped * lax.rsqrt(jnp.mean(shaped * shaped, axis=-1, keepdims=True) + 1e-06) * gain
    return scaled.astype(jnp.bfloat16)


def neighbours(block):
    count = lax.axis_size(SLAB)
    forward = [(i, i + 1) for i in range(count - 1)]
    backward = [(i + 1, i) for i in range(count - 1)]
    low = lax.ppermute(block, SLAB, forward)
    high = lax.ppermute(block, SLAB, backward)
    return jnp.concatenate([low, block, high], axis=0)


def allowed_mask(key_tiles, tiles_here):
    slab_pos = lax.axis_index(SLAB)
    near_ids = (slab_pos - 1) * tiles_here + jnp.arange(3 * tiles_here, dtype=jnp.int32)
    live = jnp.any(key_tiles[:, :, :, None] == near_ids[None, None, None, :], axis=2)
    return jnp.repeat(jnp.repeat(live, TILE, axis=1), TILE, axis=2)


def attention(q_norm, k_all, v_all, allowed):
    score = jnp.einsum("qhd,khd->hqk", q_norm, k_all, preferred_element_type=jnp.float32)
    score = score * (1.0 / HDIM**0.5)
    weight = jnp.where(allowed, jnp.exp(score), jnp.zeros_like(score))
    summed = jnp.einsum(
        "hqk,khd->hqd", weight.astype(jnp.bfloat16), v_all, preferred_element_type=jnp.float32
    )
    total = jnp.sum(weight, axis=2)
    return (summed / total[:, :, None]).astype(jnp.bfloat16)


def on_device(tokens, q_weight, k_weight, v_weight, out_weight, q_gain, k_gain, key_tiles):
    rows, width = tokens.shape
    heads = width // HDIM
    n_x = lax.axis_size("x")
    n_z = lax.axis_size("z")
    n_head = lax.axis_size(HEAD)
    part = width // n_x

    stacked = jnp.concatenate([q_weight, k_weight, v_weight], axis=1)
    weights = lax.all_gather(stacked, "z", axis=0, tiled=True)

    pieces = tokens.reshape(rows, n_x, part).transpose(1, 0, 2)
    pieces = lax.all_to_all(pieces, "x", split_axis=0, concat_axis=0, tiled=True)
    pieces = lax.all_gather(pieces.reshape(n_x * rows, part), HEAD, axis=0, tiled=False)
    group = pieces.transpose(1, 0, 2).reshape(n_x * rows, n_head * part)

    turned = [(z * n_head + h, h * n_z + z) for z in range(n_z) for h in range(n_head)]
    columns = lax.ppermute(out_weight.T, ("z",) + HEAD, turned)
    columns = lax.all_gather(columns, "x", axis=0, tiled=True).T
    projection = lax.all_gather(columns, "z", axis=0, tiled=True)
    weights, _ = lax.optimization_barrier((weights, columns))

    partial = jnp.dot(group, weights, preferred_element_type=jnp.float32).astype(jnp.bfloat16)
    partial = lax.all_to_all(
        partial.reshape(n_x, rows, 3 * width), "x", split_axis=0, concat_axis=0, tiled=True
    )
    whole = jnp.sum(partial.astype(jnp.float32), axis=0).reshape(rows, 3, heads, HDIM)
    q_norm = head_norm(whole[:, 0], q_gain)
    k_norm = head_norm(whole[:, 1], k_gain)
    v_cast = whole[:, 2].astype(jnp.bfloat16)
    near = neighbours(jnp.stack([k_norm, v_cast], axis=1))
    allowed = allowed_mask(key_tiles, rows // TILE)
    attended = attention(q_norm, near[:, 0], near[:, 1], allowed)
    attended = attended.transpose(1, 0, 2).reshape(rows, width)
    everyone = lax.all_gather(attended, HEAD, axis=1, tiled=True)
    return jnp.dot(everyone, projection, preferred_element_type=jnp.float32).astype(jnp.bfloat16)


def solution(mesh):
    n_slab, n_head, n_cfg = (mesh.shape[a] for a in ("slab", "head", "cfg"))
    fine = Mesh(
        mesh.devices.reshape(n_slab // 4, 4, n_head // 2, 2, n_cfg), ("z", "x", "y", "core", "cfg")
    )
    placed = (
        P(("cfg", "z", "x"), HEAD),
        P(SLAB, HEAD),
        P(SLAB, HEAD),
        P(SLAB, HEAD),
        P(HEAD, SLAB),
        P(),
        P(),
        P(HEAD, SLAB, None),
    )
    return jax.shard_map(
        on_device, mesh=fine, in_specs=placed, out_specs=P(("cfg", "z", "x"), HEAD), check_vma=False
    )
```

```python
import jax
import jax.numpy as jnp
from jax import lax
from jax.sharding import Mesh
from jax.sharding import PartitionSpec as P

HDIM = 128
TILE = 64
HEAD = ("y", "core")
SLAB = ("z", "x")


def head_norm(shaped, gain):
    scaled = shaped * lax.rsqrt(jnp.mean(shaped * shaped, axis=-1, keepdims=True) + 1e-06) * gain
    return scaled.astype(jnp.bfloat16)


def neighbours(block):
    count = lax.axis_size(SLAB)
    forward = [(i, i + 1) for i in range(count - 1)]
    backward = [(i + 1, i) for i in range(count - 1)]
    low = lax.ppermute(block, SLAB, forward)
    high = lax.ppermute(block, SLAB, backward)
    return jnp.concatenate([low, block, high], axis=0)


def allowed_mask(key_tiles, tiles_here):
    slab_pos = lax.axis_index(SLAB)
    near_ids = (slab_pos - 1) * tiles_here + jnp.arange(3 * tiles_here, dtype=jnp.int32)
    live = jnp.any(key_tiles[:, :, :, None] == near_ids[None, None, None, :], axis=2)
    return jnp.repeat(jnp.repeat(live, TILE, axis=1), TILE, axis=2)


def attention(q_norm, k_all, v_all, allowed):
    score = jnp.einsum("qhd,khd->hqk", q_norm, k_all, preferred_element_type=jnp.float32)
    score = score * (1.0 / HDIM**0.5)
    weight = jnp.where(allowed, jnp.exp(score), jnp.zeros_like(score))
    summed = jnp.einsum(
        "hqk,khd->hqd", weight.astype(jnp.bfloat16), v_all, preferred_element_type=jnp.float32
    )
    total = jnp.sum(weight, axis=2)
    return (summed / total[:, :, None]).astype(jnp.bfloat16)


def on_device(tokens, q_weight, k_weight, v_weight, out_weight, q_gain, k_gain, key_tiles):
    rows, width = tokens.shape
    heads = width // HDIM
    n_x = lax.axis_size("x")
    n_z = lax.axis_size("z")
    n_head = lax.axis_size(HEAD)
    part = width // n_x

    stacked = jnp.concatenate([q_weight, k_weight, v_weight], axis=1)
    weights = lax.all_gather(stacked, "z", axis=0, tiled=True)

    turned = [(z * n_head + h, h * n_z + z) for z in range(n_z) for h in range(n_head)]
    columns = lax.ppermute(out_weight.T, ("z",) + HEAD, turned)

    pieces = tokens.reshape(rows, n_x, part).transpose(1, 0, 2)
    pieces = lax.all_to_all(pieces, "x", split_axis=0, concat_axis=0, tiled=True)
    pieces = lax.all_gather(pieces.reshape(n_x * rows, part), HEAD, axis=0, tiled=False)
    pieces, columns = lax.optimization_barrier((pieces, columns))
    group = pieces.transpose(1, 0, 2).reshape(n_x * rows, n_head * part)

    columns = lax.all_gather(columns, "x", axis=0, tiled=True).T
    projection = lax.all_gather(columns, "z", axis=0, tiled=True)
    weights, group, _ = lax.optimization_barrier((weights, group, columns))

    def shares(piece):
        share = jnp.dot(group, piece, preferred_element_type=jnp.float32).astype(jnp.bfloat16)
        return share.reshape(n_x, rows, -1)

    def owned(share):
        share = lax.all_to_all(share, "x", split_axis=0, concat_axis=0, tiled=True)
        return jnp.sum(share.astype(jnp.float32), axis=0).reshape(rows, -1, heads, HDIM)

    key_value = owned(shares(weights[:, width:]))
    packed = jnp.stack(
        [head_norm(key_value[:, 0], k_gain), key_value[:, 1].astype(jnp.bfloat16)], axis=1
    )
    query = shares(weights[:, :width])
    query, packed = lax.optimization_barrier((query, packed))
    near = neighbours(packed)
    q_norm = head_norm(owned(query)[:, 0], q_gain)
    allowed = allowed_mask(key_tiles, rows // TILE)
    attended = attention(q_norm, near[:, 0], near[:, 1], allowed)
    attended = attended.transpose(1, 0, 2).reshape(rows, width)
    everyone = lax.all_gather(attended, HEAD, axis=1, tiled=True)
    return jnp.dot(everyone, projection, preferred_element_type=jnp.float32).astype(jnp.bfloat16)


def solution(mesh):
    n_slab, n_head, n_cfg = (mesh.shape[a] for a in ("slab", "head", "cfg"))
    fine = Mesh(
        mesh.devices.reshape(n_slab // 4, 4, n_head // 2, 2, n_cfg), ("z", "x", "y", "core", "cfg")
    )
    placed = (
        P(("cfg", "z", "x"), HEAD),
        P(SLAB, HEAD),
        P(SLAB, HEAD),
        P(SLAB, HEAD),
        P(HEAD, SLAB),
        P(),
        P(),
        P(HEAD, SLAB, None),
    )
    return jax.shard_map(
        on_device, mesh=fine, in_specs=placed, out_specs=P(("cfg", "z", "x"), HEAD), check_vma=False
    )
```

```python
import functools

import jax
import jax.numpy as jnp
from jax import lax
from jax.experimental import pallas as pl
from jax.experimental.pallas import tpu as pltpu
from jax.sharding import Mesh
from jax.sharding import PartitionSpec as P

HDIM = 128
TILE = 64
HEAD = ("y", "core")
Z = ("zq", "zp")
SLAB = ("zq", "zp", "x")
MIB = 1024 * 1024


def whole_block(array):
    rank = len(array.shape)
    return pl.BlockSpec(array.shape, lambda *_: (0,) * rank)


def params(mib):
    return pltpu.CompilerParams(vmem_limit_bytes=mib * MIB)


def shares_kernel(group_ref, weight_ref, out_ref):
    share = jnp.dot(group_ref[...], weight_ref[...], preferred_element_type=jnp.float32)
    out_ref[...] = share.astype(jnp.bfloat16).reshape(out_ref.shape)


def shares(group, weights, first, count, n_x):
    rows, depth = group.shape
    wide = 3 * HDIM
    return pl.pallas_call(
        shares_kernel,
        grid=(count,),
        in_specs=[whole_block(group), pl.BlockSpec((depth, wide), lambda i: (0, first + i))],
        out_specs=pl.BlockSpec((n_x, rows // n_x, wide), lambda i: (0, 0, i)),
        out_shape=jax.ShapeDtypeStruct((n_x, rows // n_x, count * wide), jnp.bfloat16),
        compiler_params=params(16),
    )(group, weights)


def normed(total, gain):
    return total * lax.rsqrt(jnp.mean(total * total, axis=-1, keepdims=True) + 1e-06) * gain


def summed(ref, low, high):
    return jnp.sum(ref[:, :, low:high].astype(jnp.float32), axis=0)


def pack_kernel(share_ref, gain_ref, out_ref):
    width = out_ref.shape[1] // 2
    for low in range(0, width, HDIM):
        total = summed(share_ref, low, low + HDIM)
        out_ref[:, low : low + HDIM] = normed(total, gain_ref[...]).astype(jnp.bfloat16)
    out_ref[:, width:] = summed(share_ref, width, 2 * width).astype(jnp.bfloat16)


def pack(share, gain):
    return pl.pallas_call(
        pack_kernel,
        out_shape=jax.ShapeDtypeStruct(share.shape[1:], jnp.bfloat16),
        compiler_params=params(16),
    )(share, gain.reshape(1, HDIM))


def attention_kernel(share_ref, gain_ref, live_ref, before_ref, own_ref, after_ref, out_ref):
    rows, width = out_ref.shape
    near = (before_ref, own_ref, after_ref)
    scale = 1.0 / HDIM**0.5
    for low in range(0, width, HDIM):
        query = normed(summed(share_ref, low, low + HDIM), gain_ref[...]).astype(jnp.bfloat16)
        keys = jnp.concatenate([r[:, low : low + HDIM] for r in near], axis=0)
        values = jnp.concatenate([r[:, width + low : width + low + HDIM] for r in near], axis=0)
        score = lax.dot_general(
            query, keys, (((1,), (1,)), ((), ())), preferred_element_type=jnp.float32
        )
        allowed = jnp.concatenate(
            [
                jnp.broadcast_to(live_ref[pl.ds(low // HDIM * (rows // TILE) + t, 1), :], (TILE, 3 * rows))
                for t in range(rows // TILE)
            ],
            axis=0,
        )
        weight = jnp.where(allowed > 0, jnp.exp(score * scale), 0.0)
        total = jnp.sum(weight, axis=1, keepdims=True)
        mixed = jnp.dot(weight.astype(jnp.bfloat16), values, preferred_element_type=jnp.float32)
        out_ref[:, low : low + HDIM] = (mixed / total).astype(jnp.bfloat16)


def attention(share, gain, live, before, own, after):
    rows, width = share.shape[1:]
    return pl.pallas_call(
        attention_kernel,
        out_shape=jax.ShapeDtypeStruct((rows, width), jnp.bfloat16),
        compiler_params=params(16),
    )(share, gain.reshape(1, HDIM), live, before, own, after)


def project_kernel(steps, left_ref, right_ref, out_ref, total_ref):
    step = pl.program_id(0)
    part = jnp.dot(left_ref[0], right_ref[0], preferred_element_type=jnp.float32)
    for piece in range(1, left_ref.shape[0]):
        part += jnp.dot(left_ref[piece], right_ref[piece], preferred_element_type=jnp.float32)

    @pl.when(step == 0)
    def _():
        total_ref[...] = part

    @pl.when(step > 0)
    def _():
        total_ref[...] += part

    @pl.when(step == steps - 1)
    def _():
        out_ref[...] = total_ref[...].astype(jnp.bfloat16)


def project(left, right):
    pieces, rows, depth = left.shape
    width = right.shape[2]
    steps = 4
    each = pieces // steps
    return pl.pallas_call(
        functools.partial(project_kernel, steps),
        grid=(steps,),
        in_specs=[
            pl.BlockSpec((each, rows, depth), lambda i: (i, 0, 0)),
            pl.BlockSpec((each, depth, width), lambda i: (i, 0, 0)),
        ],
        out_specs=pl.BlockSpec((rows, width), lambda i: (0, 0)),
        out_shape=jax.ShapeDtypeStruct((rows, width), jnp.bfloat16),
        scratch_shapes=[pltpu.VMEM((rows, width), jnp.float32)],
        compiler_params=params(16),
    )(left, right)


def live_rows(key_tiles, tiles_here):
    near_ids = (lax.axis_index(SLAB) - 1) * tiles_here + jnp.arange(3 * tiles_here, dtype=jnp.int32)
    live = jnp.any(key_tiles[:, :, :, None] == near_ids[None, None, None, :], axis=2)
    live = live.reshape(-1, 3 * tiles_here).astype(jnp.float32)
    return jnp.repeat(live, TILE, axis=1)


def on_device(tokens, q_weight, k_weight, v_weight, out_weight, q_gain, k_gain, key_tiles):
    rows, width = tokens.shape
    n_x, n_z, n_head = (lax.axis_size(a) for a in ("x", Z, HEAD))
    part = width // n_x

    stacked = jnp.concatenate([q_weight, k_weight, v_weight], axis=1)
    weights = lax.all_gather(stacked, Z, axis=0, tiled=True)

    turned = [(z * n_head + h, h * n_z + z) for z in range(n_z) for h in range(n_head)]
    columns = lax.ppermute(out_weight.T, Z + HEAD, turned)

    pieces = tokens.reshape(rows, n_x, part).transpose(1, 0, 2)
    pieces = lax.all_to_all(pieces, "x", split_axis=0, concat_axis=0, tiled=True)
    columns = lax.all_to_all(
        jnp.broadcast_to(columns[None], (n_x,) + columns.shape),
        "x",
        split_axis=0,
        concat_axis=0,
        tiled=True,
    )
    pieces, columns = lax.optimization_barrier((pieces, columns))
    pieces = lax.all_gather(pieces.reshape(n_x * rows, part), HEAD, axis=0, tiled=False)
    group = pieces.transpose(1, 0, 2).reshape(n_x * rows, n_head * part)

    columns = columns.reshape(width, width).T
    other = lax.ppermute(columns, "zp", [(0, 1), (1, 0)])
    first = lax.axis_index("zp") == 0
    pair = jnp.stack([jnp.where(first, columns, other), jnp.where(first, other, columns)])
    projection = lax.all_gather(pair, "zq", axis=0, tiled=True)
    weights, group, _ = lax.optimization_barrier((weights, group, pair))

    key_value = shares(group, weights, 1, 2, n_x)
    query = shares(group, weights, 0, 1, n_x)
    key_value = lax.all_to_all(key_value, "x", split_axis=0, concat_axis=0, tiled=True)
    query = lax.all_to_all(query, "x", split_axis=0, concat_axis=0, tiled=True)
    packed = pack(key_value, k_gain)
    count = lax.axis_size(SLAB)
    before = lax.ppermute(packed, SLAB, [(i, i + 1) for i in range(count - 1)])
    after = lax.ppermute(packed, SLAB, [(i + 1, i) for i in range(count - 1)])
    live = live_rows(key_tiles, rows // TILE)
    attended = attention(query, q_gain, live, before, packed, after)
    everyone = lax.all_gather(attended, HEAD, axis=0, tiled=False)
    return project(everyone, projection)


def solution(mesh):
    n_slab, n_head, n_cfg = (mesh.shape[a] for a in ("slab", "head", "cfg"))
    fine = Mesh(
        mesh.devices.reshape(n_slab // 8, 2, 4, n_head // 2, 2, n_cfg),
        ("zq", "zp", "x", "y", "core", "cfg"),
    )
    placed = (
        P(("cfg",) + SLAB, HEAD),
        P(SLAB, HEAD),
        P(SLAB, HEAD),
        P(SLAB, HEAD),
        P(HEAD, SLAB),
        P(),
        P(),
        P(HEAD, SLAB, None),
    )
    return jax.shard_map(
        on_device, mesh=fine, in_specs=placed, out_specs=P(("cfg",) + SLAB, HEAD), check_vma=False
    )
```

```python
import functools

import jax
import jax.numpy as jnp
from jax import lax
from jax.experimental import pallas as pl
from jax.experimental.pallas import tpu as pltpu
from jax.sharding import Mesh
from jax.sharding import PartitionSpec as P

HDIM = 128
TILE = 64
HEAD = ("y", "core")
SLAB = ("z", "x")
MIB = 1024 * 1024


def whole_block(array):
    rank = len(array.shape)
    return pl.BlockSpec(array.shape, lambda *_: (0,) * rank)


def params(mib):
    return pltpu.CompilerParams(vmem_limit_bytes=mib * MIB)


def shares_kernel(group_ref, weight_ref, out_ref):
    share = jnp.dot(group_ref[...], weight_ref[...], preferred_element_type=jnp.float32)
    out_ref[...] = share.astype(jnp.bfloat16).reshape(out_ref.shape)


def shares(group, weights, first, count, n_x):
    rows, depth = group.shape
    wide = 3 * HDIM
    return pl.pallas_call(
        shares_kernel,
        grid=(count,),
        in_specs=[whole_block(group), pl.BlockSpec((depth, wide), lambda i: (0, first + i))],
        out_specs=pl.BlockSpec((n_x, rows // n_x, wide), lambda i: (0, 0, i)),
        out_shape=jax.ShapeDtypeStruct((n_x, rows // n_x, count * wide), jnp.bfloat16),
        compiler_params=params(56),
    )(group, weights)


def turned_shares_kernel(place_ref, group_ref, weight_ref, *out_refs):
    rows = out_refs[0].shape[0]
    for step, out_ref in enumerate(out_refs):
        slab = jnp.bitwise_xor(place_ref[0], step)
        group = group_ref[pl.ds(pl.multiple_of(slab * rows, rows), rows), :]
        share = jnp.dot(group, weight_ref[...], preferred_element_type=jnp.float32)
        out_ref[...] = share.astype(jnp.bfloat16)


def turned_shares(group, weights, n_x):
    rows, depth = group.shape
    wide = 3 * HDIM
    place = lax.axis_index("x").astype(jnp.int32).reshape(1)
    block = (rows // n_x, wide)
    return pl.pallas_call(
        turned_shares_kernel,
        grid_spec=pltpu.PrefetchScalarGridSpec(
            num_scalar_prefetch=1,
            grid=(1,),
            in_specs=[whole_block(group), pl.BlockSpec((depth, wide), lambda i, p: (0, 0))],
            out_specs=[pl.BlockSpec(block, lambda i, p: (0, 0))] * n_x,
        ),
        out_shape=[jax.ShapeDtypeStruct(block, jnp.bfloat16)] * n_x,
        compiler_params=params(56),
    )(place, group, weights)


def normed(total, gain):
    return total * lax.rsqrt(jnp.mean(total * total, axis=-1, keepdims=True) + 1e-06) * gain


def summed(ref, low, high):
    return jnp.sum(ref[:, :, low:high].astype(jnp.float32), axis=0)


def pack_kernel(share_ref, gain_ref, out_ref):
    width = out_ref.shape[1] // 2
    for low in range(0, width, HDIM):
        total = summed(share_ref, low, low + HDIM)
        out_ref[:, low : low + HDIM] = normed(total, gain_ref[...]).astype(jnp.bfloat16)
    out_ref[:, width:] = summed(share_ref, width, 2 * width).astype(jnp.bfloat16)


def pack(share, gain):
    return pl.pallas_call(
        pack_kernel,
        out_shape=jax.ShapeDtypeStruct(share.shape[1:], jnp.bfloat16),
        compiler_params=params(16),
    )(share, gain.reshape(1, HDIM))


def attention_kernel(*refs):
    *share_refs, gain_ref, live_ref, before_ref, own_ref, after_ref, out_ref = refs
    rows, width = out_ref.shape
    near = (before_ref, own_ref, after_ref)
    scale = 1.0 / HDIM**0.5
    for low in range(0, width, HDIM):
        query = sum(r[:, low : low + HDIM].astype(jnp.float32) for r in share_refs)
        query = normed(query, gain_ref[...]).astype(jnp.bfloat16)
        keys = jnp.concatenate([r[:, low : low + HDIM] for r in near], axis=0)
        values = jnp.concatenate([r[:, width + low : width + low + HDIM] for r in near], axis=0)
        score = lax.dot_general(
            query, keys, (((1,), (1,)), ((), ())), preferred_element_type=jnp.float32
        )
        allowed = jnp.concatenate(
            [
                jnp.broadcast_to(live_ref[pl.ds(low // HDIM * (rows // TILE) + t, 1), :], (TILE, 3 * rows))
                for t in range(rows // TILE)
            ],
            axis=0,
        )
        weight = jnp.where(allowed > 0, jnp.exp(score * scale), 0.0)
        total = jnp.sum(weight, axis=1, keepdims=True)
        mixed = jnp.dot(weight.astype(jnp.bfloat16), values, preferred_element_type=jnp.float32)
        out_ref[:, low : low + HDIM] = (mixed / total).astype(jnp.bfloat16)


def attention(query, gain, live, before, own, after):
    rows, width = query[0].shape
    return pl.pallas_call(
        attention_kernel,
        out_shape=jax.ShapeDtypeStruct((rows, width), jnp.bfloat16),
        compiler_params=params(16),
    )(*query, gain.reshape(1, HDIM), live, before, own, after)


def project_kernel(steps, left_ref, right_ref, out_ref, total_ref):
    step = pl.program_id(0)
    part = sum(
        lax.dot_general(
            left_ref[piece],
            right_ref[piece],
            (((1,), (1,)), ((), ())),
            preferred_element_type=jnp.float32,
        )
        for piece in range(left_ref.shape[0])
    )

    @pl.when(step == 0)
    def _():
        total_ref[...] = part

    @pl.when(step > 0)
    def _():
        total_ref[...] += part

    @pl.when(step == steps - 1)
    def _():
        out_ref[...] = total_ref[...].astype(jnp.bfloat16)


def project(left, right):
    pieces, rows, depth = left.shape
    width = right.shape[1]
    steps = 4
    each = pieces // steps
    return pl.pallas_call(
        functools.partial(project_kernel, steps),
        grid=(steps,),
        in_specs=[
            pl.BlockSpec((each, rows, depth), lambda i: (i, 0, 0)),
            pl.BlockSpec((each, width, depth), lambda i: (i, 0, 0)),
        ],
        out_specs=pl.BlockSpec((rows, width), lambda i: (0, 0)),
        out_shape=jax.ShapeDtypeStruct((rows, width), jnp.bfloat16),
        scratch_shapes=[pltpu.VMEM((rows, width), jnp.float32)],
        compiler_params=params(56),
    )(left, right)


def live_rows(key_tiles, tiles_here):
    near_ids = (lax.axis_index(SLAB) - 1) * tiles_here + jnp.arange(3 * tiles_here, dtype=jnp.int32)
    live = jnp.any(key_tiles[:, :, :, None] == near_ids[None, None, None, :], axis=2)
    live = live.reshape(-1, 3 * tiles_here).astype(jnp.float32)
    return jnp.repeat(live, TILE, axis=1)


def on_device(tokens, q_weight, k_weight, v_weight, out_weight, q_gain, k_gain, key_tiles):
    rows, width = tokens.shape
    n_x, n_z, n_head = (lax.axis_size(a) for a in ("x", "z", HEAD))
    part = width // n_x

    stacked = jnp.concatenate([q_weight, k_weight, v_weight], axis=1)
    weights = lax.all_gather(stacked, "z", axis=0, tiled=True)

    turned = [(z * n_head + h, h * n_z + z) for z in range(n_z) for h in range(n_head)]
    columns = lax.ppermute(out_weight.T, ("z",) + HEAD, turned)

    pieces = tokens.reshape(rows, n_x, part).transpose(1, 0, 2)
    pieces = lax.all_to_all(pieces, "x", split_axis=0, concat_axis=0, tiled=True)
    pieces = lax.all_gather(pieces.reshape(n_x * rows, part), HEAD, axis=0, tiled=False)
    pieces, columns = lax.optimization_barrier((pieces, columns))
    group = pieces.transpose(1, 0, 2).reshape(n_x * rows, n_head * part)

    columns = lax.all_gather(columns, "x", axis=0, tiled=True)
    projection = lax.all_gather(columns, "z", axis=0, tiled=False)
    weights, group, _ = lax.optimization_barrier((weights, group, columns))

    key_value = shares(group, weights, 1, 2, n_x)
    key_value = lax.all_to_all(key_value, "x", split_axis=0, concat_axis=0, tiled=True)
    query = turned_shares(group, weights, n_x)
    key_value, *query = lax.optimization_barrier((key_value, *query))
    query = [
        lax.ppermute(share, "x", [(i, i ^ step) for i in range(n_x)]) if step else share
        for step, share in enumerate(query)
    ]
    packed = pack(key_value, k_gain)
    count = lax.axis_size(SLAB)
    before = lax.ppermute(packed, SLAB, [(i, i + 1) for i in range(count - 1)])
    after = lax.ppermute(packed, SLAB, [(i + 1, i) for i in range(count - 1)])
    live = live_rows(key_tiles, rows // TILE)
    attended = attention(query, q_gain, live, before, packed, after)
    everyone = lax.all_gather(attended, HEAD, axis=0, tiled=False)
    return project(everyone, projection)


def solution(mesh):
    n_slab, n_head, n_cfg = (mesh.shape[a] for a in ("slab", "head", "cfg"))
    fine = Mesh(
        mesh.devices.reshape(n_slab // 4, 4, n_head // 2, 2, n_cfg), ("z", "x", "y", "core", "cfg")
    )
    placed = (
        P(("cfg",) + SLAB, HEAD),
        P(SLAB, HEAD),
        P(SLAB, HEAD),
        P(SLAB, HEAD),
        P(HEAD, SLAB),
        P(),
        P(),
        P(HEAD, SLAB, None),
    )
    return jax.shard_map(
        on_device, mesh=fine, in_specs=placed, out_specs=P(("cfg",) + SLAB, HEAD), check_vma=False
    )
```

```python
import functools

import jax
import jax.numpy as jnp
from jax import lax
from jax.experimental import pallas as pl
from jax.experimental.pallas import tpu as pltpu
from jax.sharding import Mesh
from jax.sharding import PartitionSpec as P

HDIM = 128
TILE = 64
HEAD = ("y", "core")
SLAB = ("z", "x")
MIB = 1024 * 1024


def whole_block(array):
    rank = len(array.shape)
    return pl.BlockSpec(array.shape, lambda *_: (0,) * rank)


def params(mib):
    return pltpu.CompilerParams(vmem_limit_bytes=mib * MIB)


def fetches(source, buffer, sems, first):
    wide = buffer.shape[2]
    copies = [
        pltpu.make_async_copy(
            source.at[:, pl.ds(first + n * wide, wide)], buffer.at[n], sems.at[n]
        )
        for n in range(buffer.shape[0])
    ]
    for copy in copies:
        copy.start()
    return copies


def shares_kernel(first, group_ref, weight_ref, out_ref, weights, results, sems, out_sems):
    wide = weights.shape[2]
    stores = []
    for n, copy in enumerate(fetches(weight_ref, weights, sems, first)):
        copy.wait()
        share = jnp.dot(group_ref[...], weights[n], preferred_element_type=jnp.float32)
        results[n] = share.astype(jnp.bfloat16).reshape(results.shape[1:])
        store = pltpu.make_async_copy(
            results.at[n], out_ref.at[:, :, pl.ds(n * wide, wide)], out_sems.at[n]
        )
        store.start()
        stores.append(store)
    for store in stores:
        store.wait()


def shares(group, weights, first, count, n_x):
    rows, depth = group.shape
    wide = 3 * HDIM
    return pl.pallas_call(
        functools.partial(shares_kernel, first * wide),
        in_specs=[whole_block(group), pl.BlockSpec(memory_space=pltpu.HBM)],
        out_specs=pl.BlockSpec(memory_space=pltpu.HBM),
        out_shape=jax.ShapeDtypeStruct((n_x, rows // n_x, count * wide), jnp.bfloat16),
        scratch_shapes=[
            pltpu.VMEM((count, depth, wide), jnp.bfloat16),
            pltpu.VMEM((count, n_x, rows // n_x, wide), jnp.bfloat16),
            pltpu.SemaphoreType.DMA((count,)),
            pltpu.SemaphoreType.DMA((count,)),
        ],
        compiler_params=params(16),
    )(group, weights)


def turned_shares_kernel(place_ref, group_ref, weight_ref, *refs):
    *out_refs, weights, sems = refs
    rows = out_refs[0].shape[0]
    (copy,) = fetches(weight_ref, weights, sems, 0)
    copy.wait()
    for step, out_ref in enumerate(out_refs):
        slab = jnp.bitwise_xor(place_ref[0], step)
        group = group_ref[pl.ds(pl.multiple_of(slab * rows, rows), rows), :]
        share = jnp.dot(group, weights[0], preferred_element_type=jnp.float32)
        out_ref[...] = share.astype(jnp.bfloat16)


def turned_shares(group, weights, n_x):
    rows, depth = group.shape
    wide = 3 * HDIM
    place = lax.axis_index("x").astype(jnp.int32).reshape(1)
    block = (rows // n_x, wide)
    return pl.pallas_call(
        turned_shares_kernel,
        in_specs=[
            pl.BlockSpec(memory_space=pltpu.SMEM),
            whole_block(group),
            pl.BlockSpec(memory_space=pltpu.HBM),
        ],
        out_shape=[jax.ShapeDtypeStruct(block, jnp.bfloat16)] * n_x,
        scratch_shapes=[
            pltpu.VMEM((1, depth, wide), jnp.bfloat16),
            pltpu.SemaphoreType.DMA((1,)),
        ],
        compiler_params=params(16),
    )(place, group, weights)


def normed(total, gain):
    return total * lax.rsqrt(jnp.mean(total * total, axis=-1, keepdims=True) + 1e-06) * gain


def summed(ref, low, high):
    return jnp.sum(ref[:, :, low:high].astype(jnp.float32), axis=0)


def pack_kernel(share_ref, gain_ref, out_ref):
    width = out_ref.shape[1] // 2
    for low in range(0, width, HDIM):
        total = summed(share_ref, low, low + HDIM)
        out_ref[:, low : low + HDIM] = normed(total, gain_ref[...]).astype(jnp.bfloat16)
    out_ref[:, width:] = summed(share_ref, width, 2 * width).astype(jnp.bfloat16)


def pack(share, gain):
    return pl.pallas_call(
        pack_kernel,
        out_shape=jax.ShapeDtypeStruct(share.shape[1:], jnp.bfloat16),
        compiler_params=params(16),
    )(share, gain.reshape(1, HDIM))


def attention_kernel(*refs):
    *share_refs, gain_ref, live_ref, before_ref, own_ref, after_ref, out_ref = refs
    rows, width = out_ref.shape
    near = (before_ref, own_ref, after_ref)
    scale = 1.0 / HDIM**0.5
    for low in range(0, width, HDIM):
        query = sum(r[:, low : low + HDIM].astype(jnp.float32) for r in share_refs)
        query = normed(query, gain_ref[...]).astype(jnp.bfloat16)
        keys = jnp.concatenate([r[:, low : low + HDIM] for r in near], axis=0)
        values = jnp.concatenate([r[:, width + low : width + low + HDIM] for r in near], axis=0)
        score = lax.dot_general(
            query, keys, (((1,), (1,)), ((), ())), preferred_element_type=jnp.float32
        )
        allowed = jnp.concatenate(
            [
                jnp.broadcast_to(live_ref[pl.ds(low // HDIM * (rows // TILE) + t, 1), :], (TILE, 3 * rows))
                for t in range(rows // TILE)
            ],
            axis=0,
        )
        weight = jnp.where(allowed > 0, jnp.exp(score * scale), 0.0)
        total = jnp.sum(weight, axis=1, keepdims=True)
        mixed = jnp.dot(weight.astype(jnp.bfloat16), values, preferred_element_type=jnp.float32)
        out_ref[:, low : low + HDIM] = (mixed / total).astype(jnp.bfloat16)


def attention(query, gain, live, before, own, after):
    rows, width = query[0].shape
    return pl.pallas_call(
        attention_kernel,
        out_shape=jax.ShapeDtypeStruct((rows, width), jnp.bfloat16),
        compiler_params=params(16),
    )(*query, gain.reshape(1, HDIM), live, before, own, after)


def project_kernel(left_ref, right_ref, out_ref, rights, sems):
    copies = [
        pltpu.make_async_copy(right_ref.at[n], rights.at[n], sems.at[n])
        for n in range(left_ref.shape[0])
    ]
    for copy in copies:
        copy.start()
    total = None
    for n, copy in enumerate(copies):
        copy.wait()
        part = lax.dot_general(
            left_ref[n], rights[n], (((1,), (1,)), ((), ())), preferred_element_type=jnp.float32
        )
        total = part if total is None else total + part
    out_ref[...] = total.astype(jnp.bfloat16)


def project(left, right):
    pieces, rows, _ = left.shape
    return pl.pallas_call(
        project_kernel,
        in_specs=[whole_block(left), pl.BlockSpec(memory_space=pltpu.HBM)],
        out_shape=jax.ShapeDtypeStruct((rows, right.shape[1]), jnp.bfloat16),
        scratch_shapes=[
            pltpu.VMEM(right.shape, jnp.bfloat16),
            pltpu.SemaphoreType.DMA((pieces,)),
        ],
        compiler_params=params(16),
    )(left, right)


def live_rows(key_tiles, tiles_here):
    near_ids = (lax.axis_index(SLAB) - 1) * tiles_here + jnp.arange(3 * tiles_here, dtype=jnp.int32)
    live = jnp.any(key_tiles[:, :, :, None] == near_ids[None, None, None, :], axis=2)
    live = live.reshape(-1, 3 * tiles_here).astype(jnp.float32)
    return jnp.repeat(live, TILE, axis=1)


def on_device(tokens, q_weight, k_weight, v_weight, out_weight, q_gain, k_gain, key_tiles):
    rows, width = tokens.shape
    n_x, n_z, n_head = (lax.axis_size(a) for a in ("x", "z", HEAD))
    part = width // n_x

    stacked = jnp.concatenate([q_weight, k_weight, v_weight], axis=1)
    weights = lax.all_gather(stacked, "z", axis=0, tiled=True)

    turned = [(z * n_head + h, h * n_z + z) for z in range(n_z) for h in range(n_head)]
    columns = lax.ppermute(out_weight.T, ("z",) + HEAD, turned)

    pieces = tokens.reshape(rows, n_x, part).transpose(1, 0, 2)
    pieces = lax.all_to_all(pieces, "x", split_axis=0, concat_axis=0, tiled=True)
    pieces = lax.all_gather(pieces.reshape(n_x * rows, part), HEAD, axis=0, tiled=False)
    pieces, columns = lax.optimization_barrier((pieces, columns))
    group = pieces.transpose(1, 0, 2).reshape(n_x * rows, n_head * part)

    columns = lax.all_gather(columns, "x", axis=0, tiled=True)
    projection = lax.all_gather(columns, "z", axis=0, tiled=False)
    weights, group, _ = lax.optimization_barrier((weights, group, columns))

    key_value = shares(group, weights, 1, 2, n_x)
    key_value = lax.all_to_all(key_value, "x", split_axis=0, concat_axis=0, tiled=True)
    query = turned_shares(group, weights, n_x)
    key_value, *_ = lax.optimization_barrier((key_value, *query))
    query = [
        lax.ppermute(share, "x", [(i, i ^ step) for i in range(n_x)]) if step else share
        for step, share in enumerate(query)
    ]
    packed = pack(key_value, k_gain)
    count = lax.axis_size(SLAB)
    before = lax.ppermute(packed, SLAB, [(i, i + 1) for i in range(count - 1)])
    after = lax.ppermute(packed, SLAB, [(i + 1, i) for i in range(count - 1)])
    live = live_rows(key_tiles, rows // TILE)
    attended = attention(query, q_gain, live, before, packed, after)
    everyone = lax.all_gather(attended, HEAD, axis=0, tiled=False)
    return project(everyone, projection)


def solution(mesh):
    n_slab, n_head, n_cfg = (mesh.shape[a] for a in ("slab", "head", "cfg"))
    fine = Mesh(
        mesh.devices.reshape(n_slab // 4, 4, n_head // 2, 2, n_cfg), ("z", "x", "y", "core", "cfg")
    )
    placed = (
        P(("cfg",) + SLAB, HEAD),
        P(SLAB, HEAD),
        P(SLAB, HEAD),
        P(SLAB, HEAD),
        P(HEAD, SLAB),
        P(),
        P(),
        P(HEAD, SLAB, None),
    )
    return jax.shard_map(
        on_device, mesh=fine, in_specs=placed, out_specs=P(("cfg",) + SLAB, HEAD), check_vma=False
    )
```

```python
import jax
import jax.numpy as jnp
from jax import lax
from jax.experimental import pallas as pl
from jax.experimental.pallas import tpu as pltpu
from jax.sharding import Mesh
from jax.sharding import PartitionSpec as P

HDIM = 128
TILE = 64
HEAD = ("y", "core")
SLAB = ("z", "x")
MIB = 1024 * 1024


def whole_block(array):
    rank = len(array.shape)
    return pl.BlockSpec(array.shape, lambda *_: (0,) * rank)


def params(mib):
    return pltpu.CompilerParams(vmem_limit_bytes=mib * MIB)


def normed(total, gain):
    return total * lax.rsqrt(jnp.mean(total * total, axis=-1, keepdims=True) + 1e-06) * gain


def summed(ref, low, high):
    return jnp.sum(ref[:, :, low:high].astype(jnp.float32), axis=0)


def pack_kernel(share_ref, gain_ref, out_ref):
    width = out_ref.shape[1] // 2
    for low in range(0, width, HDIM):
        total = summed(share_ref, low, low + HDIM)
        out_ref[:, low : low + HDIM] = normed(total, gain_ref[...]).astype(jnp.bfloat16)
    out_ref[:, width:] = summed(share_ref, width, 2 * width).astype(jnp.bfloat16)


def pack(share, gain):
    return pl.pallas_call(
        pack_kernel,
        out_shape=jax.ShapeDtypeStruct(share.shape[1:], jnp.bfloat16),
        compiler_params=params(16),
    )(share, gain.reshape(1, HDIM))


def attention_kernel(*refs):
    *share_refs, gain_ref, live_ref, before_ref, own_ref, after_ref, out_ref = refs
    rows, width = out_ref.shape
    near = (before_ref, own_ref, after_ref)
    scale = 1.0 / HDIM**0.5
    for low in range(0, width, HDIM):
        query = sum(r[:, low : low + HDIM].astype(jnp.float32) for r in share_refs)
        query = normed(query, gain_ref[...]).astype(jnp.bfloat16)
        keys = jnp.concatenate([r[:, low : low + HDIM] for r in near], axis=0)
        values = jnp.concatenate([r[:, width + low : width + low + HDIM] for r in near], axis=0)
        score = lax.dot_general(
            query, keys, (((1,), (1,)), ((), ())), preferred_element_type=jnp.float32
        )
        allowed = jnp.concatenate(
            [
                jnp.broadcast_to(live_ref[pl.ds(low // HDIM * (rows // TILE) + t, 1), :], (TILE, 3 * rows))
                for t in range(rows // TILE)
            ],
            axis=0,
        )
        weight = jnp.where(allowed > 0, jnp.exp(score * scale), 0.0)
        total = jnp.sum(weight, axis=1, keepdims=True)
        mixed = jnp.dot(weight.astype(jnp.bfloat16), values, preferred_element_type=jnp.float32)
        out_ref[:, low : low + HDIM] = (mixed / total).astype(jnp.bfloat16)


def attention(query, gain, live, before, own, after):
    rows, width = query[0].shape
    return pl.pallas_call(
        attention_kernel,
        out_shape=jax.ShapeDtypeStruct((rows, width), jnp.bfloat16),
        compiler_params=params(16),
    )(*query, gain.reshape(1, HDIM), live, before, own, after)


def live_rows(key_tiles, tiles_here):
    near_ids = (lax.axis_index(SLAB) - 1) * tiles_here + jnp.arange(3 * tiles_here, dtype=jnp.int32)
    live = jnp.any(key_tiles[:, :, :, None] == near_ids[None, None, None, :], axis=2)
    live = live.reshape(-1, 3 * tiles_here).astype(jnp.float32)
    return jnp.repeat(live, TILE, axis=1)


def on_device(tokens, q_weight, k_weight, v_weight, out_weight, q_gain, k_gain, key_tiles):
    rows, width = tokens.shape
    n_x, n_z, n_head = (lax.axis_size(a) for a in ("x", "z", HEAD))
    part = width // n_x

    stacked = jnp.concatenate([q_weight, k_weight, v_weight], axis=1)
    weights = lax.all_gather(stacked, "z", axis=0, tiled=True)

    turned = [(z * n_head + h, h * n_z + z) for z in range(n_z) for h in range(n_head)]
    columns = lax.ppermute(out_weight.T, ("z",) + HEAD, turned)

    pieces = tokens.reshape(rows, n_x, part).transpose(1, 0, 2)
    pieces = lax.all_to_all(pieces, "x", split_axis=0, concat_axis=0, tiled=True)
    pieces = lax.all_gather(pieces.reshape(n_x * rows, part), HEAD, axis=0, tiled=False)
    pieces, columns = lax.optimization_barrier((pieces, columns))
    group = pieces.transpose(1, 0, 2).reshape(n_x * rows, n_head * part)

    columns = lax.all_gather(columns, "x", axis=0, tiled=True)
    projection = lax.all_gather(columns, "z", axis=0, tiled=False)
    weights, group, _ = lax.optimization_barrier((weights, group, columns))

    def shares(piece):
        share = jnp.dot(group, piece, preferred_element_type=jnp.float32).astype(jnp.bfloat16)
        return share.reshape(n_x, rows, -1)

    key_value = shares(weights[:, width:])
    key_value = lax.all_to_all(key_value, "x", split_axis=0, concat_axis=0, tiled=True)
    turned = shares(weights[:, :width])
    place = lax.axis_index("x")
    query = []
    for step in range(n_x):
        share = lax.dynamic_index_in_dim(turned, place ^ step, 0, keepdims=False)
        pairs = [(i, i ^ step) for i in range(n_x)]
        query.append(lax.ppermute(share, "x", pairs) if step else share)
    key_value, *query = lax.optimization_barrier((key_value, *query))
    packed = pack(key_value, k_gain)
    count = lax.axis_size(SLAB)
    before = lax.ppermute(packed, SLAB, [(i, i + 1) for i in range(count - 1)])
    after = lax.ppermute(packed, SLAB, [(i + 1, i) for i in range(count - 1)])
    live = live_rows(key_tiles, rows // TILE)
    attended = attention(query, q_gain, live, before, packed, after)
    everyone = lax.all_gather(attended, HEAD, axis=0, tiled=False)
    total = jnp.einsum("hrd,hnd->rn", everyone, projection, preferred_element_type=jnp.float32)
    return total.astype(jnp.bfloat16)


def solution(mesh):
    n_slab, n_head, n_cfg = (mesh.shape[a] for a in ("slab", "head", "cfg"))
    fine = Mesh(
        mesh.devices.reshape(n_slab // 4, 4, n_head // 2, 2, n_cfg), ("z", "x", "y", "core", "cfg")
    )
    placed = (
        P(("cfg",) + SLAB, HEAD),
        P(SLAB, HEAD),
        P(SLAB, HEAD),
        P(SLAB, HEAD),
        P(HEAD, SLAB),
        P(),
        P(),
        P(HEAD, SLAB, None),
    )
    return jax.shard_map(
        on_device, mesh=fine, in_specs=placed, out_specs=P(("cfg",) + SLAB, HEAD), check_vma=False
    )
```

```python
import jax
import jax.numpy as jnp
from jax import lax
from jax.experimental import pallas as pl
from jax.experimental.pallas import tpu as pltpu
from jax.sharding import Mesh
from jax.sharding import PartitionSpec as P

HDIM = 128
TILE = 64
HEAD = ("y", "core")
SLAB = ("z", "x")
MIB = 1024 * 1024


def whole_block(array):
    rank = len(array.shape)
    return pl.BlockSpec(array.shape, lambda *_: (0,) * rank)


def params(mib):
    return pltpu.CompilerParams(vmem_limit_bytes=mib * MIB)


def normed(total, gain):
    return total * lax.rsqrt(jnp.mean(total * total, axis=-1, keepdims=True) + 1e-06) * gain


def summed(ref, low, high):
    return jnp.sum(ref[:, :, low:high].astype(jnp.float32), axis=0)


def pack_kernel(share_ref, gain_ref, out_ref):
    width = out_ref.shape[1] // 2
    for low in range(0, width, HDIM):
        total = summed(share_ref, low, low + HDIM)
        out_ref[:, low : low + HDIM] = normed(total, gain_ref[...]).astype(jnp.bfloat16)
    out_ref[:, width:] = summed(share_ref, width, 2 * width).astype(jnp.bfloat16)


def pack(share, gain):
    return pl.pallas_call(
        pack_kernel,
        out_shape=jax.ShapeDtypeStruct(share.shape[1:], jnp.bfloat16),
        compiler_params=params(16),
    )(share, gain.reshape(1, HDIM))


def attention_kernel(share_ref, gain_ref, live_ref, before_ref, own_ref, after_ref, out_ref):
    rows, width = out_ref.shape
    near = (before_ref, own_ref, after_ref)
    scale = 1.0 / HDIM**0.5
    for low in range(0, width, HDIM):
        query = normed(summed(share_ref, low, low + HDIM), gain_ref[...]).astype(jnp.bfloat16)
        keys = jnp.concatenate([r[:, low : low + HDIM] for r in near], axis=0)
        values = jnp.concatenate([r[:, width + low : width + low + HDIM] for r in near], axis=0)
        score = lax.dot_general(
            query, keys, (((1,), (1,)), ((), ())), preferred_element_type=jnp.float32
        )
        allowed = jnp.concatenate(
            [
                jnp.broadcast_to(live_ref[pl.ds(low // HDIM * (rows // TILE) + t, 1), :], (TILE, 3 * rows))
                for t in range(rows // TILE)
            ],
            axis=0,
        )
        weight = jnp.where(allowed > 0, jnp.exp(score * scale), 0.0)
        total = jnp.sum(weight, axis=1, keepdims=True)
        mixed = jnp.dot(weight.astype(jnp.bfloat16), values, preferred_element_type=jnp.float32)
        out_ref[:, low : low + HDIM] = (mixed / total).astype(jnp.bfloat16)


def attention(query, gain, live, before, own, after):
    rows, width = query.shape[1:]
    return pl.pallas_call(
        attention_kernel,
        out_shape=jax.ShapeDtypeStruct((rows, width), jnp.bfloat16),
        compiler_params=params(16),
    )(query, gain.reshape(1, HDIM), live, before, own, after)


def live_rows(key_tiles, tiles_here):
    near_ids = (lax.axis_index(SLAB) - 1) * tiles_here + jnp.arange(3 * tiles_here, dtype=jnp.int32)
    live = jnp.any(key_tiles[:, :, :, None] == near_ids[None, None, None, :], axis=2)
    live = live.reshape(-1, 3 * tiles_here).astype(jnp.float32)
    return jnp.repeat(live, TILE, axis=1)


def on_device(tokens, q_weight, k_weight, v_weight, out_weight, q_gain, k_gain, key_tiles):
    rows, width = tokens.shape
    n_x, n_z, n_head = (lax.axis_size(a) for a in ("x", "z", HEAD))
    part = width // n_x

    stacked = jnp.concatenate([q_weight, k_weight, v_weight], axis=1)
    weights = lax.all_gather(stacked, "z", axis=0, tiled=True)

    turned = [(z * n_head + h, h * n_z + z) for z in range(n_z) for h in range(n_head)]
    columns = lax.ppermute(out_weight.T, ("z",) + HEAD, turned)

    pieces = tokens.reshape(rows, n_x, part).transpose(1, 0, 2)
    pieces = lax.all_to_all(pieces, "x", split_axis=0, concat_axis=0, tiled=True)
    pieces = lax.all_gather(pieces.reshape(n_x * rows, part), HEAD, axis=0, tiled=False)
    pieces, columns = lax.optimization_barrier((pieces, columns))
    group = pieces.transpose(1, 0, 2).reshape(n_x * rows, n_head * part)

    columns = lax.all_gather(columns, "x", axis=0, tiled=True)
    projection = lax.all_gather(columns, "z", axis=0, tiled=False)
    weights, group, _ = lax.optimization_barrier((weights, group, columns))

    def shares(piece):
        share = jnp.dot(group, piece, preferred_element_type=jnp.float32).astype(jnp.bfloat16)
        return share.reshape(n_x, rows, -1)

    key_value = shares(weights[:, width:])
    key_value = lax.all_to_all(key_value, "x", split_axis=0, concat_axis=0, tiled=True)
    query = shares(weights[:, :width])
    query = lax.all_to_all(query, "x", split_axis=0, concat_axis=0, tiled=True)
    packed = pack(key_value, k_gain)
    count = lax.axis_size(SLAB)
    before = lax.ppermute(packed, SLAB, [(i, i + 1) for i in range(count - 1)])
    after = lax.ppermute(packed, SLAB, [(i + 1, i) for i in range(count - 1)])
    live = live_rows(key_tiles, rows // TILE)
    attended = attention(query, q_gain, live, before, packed, after)
    everyone = lax.all_gather(attended, HEAD, axis=0, tiled=False)
    total = jnp.einsum("hrd,hnd->rn", everyone, projection, preferred_element_type=jnp.float32)
    return total.astype(jnp.bfloat16)


def solution(mesh):
    n_slab, n_head, n_cfg = (mesh.shape[a] for a in ("slab", "head", "cfg"))
    fine = Mesh(
        mesh.devices.reshape(n_slab // 4, 4, n_head // 2, 2, n_cfg), ("z", "x", "y", "core", "cfg")
    )
    placed = (
        P(("cfg",) + SLAB, HEAD),
        P(SLAB, HEAD),
        P(SLAB, HEAD),
        P(SLAB, HEAD),
        P(HEAD, SLAB),
        P(),
        P(),
        P(HEAD, SLAB, None),
    )
    return jax.shard_map(
        on_device, mesh=fine, in_specs=placed, out_specs=P(("cfg",) + SLAB, HEAD), check_vma=False
    )
```

```python
import jax
import jax.numpy as jnp
from jax import lax
from jax.experimental import pallas as pl
from jax.experimental.pallas import tpu as pltpu
from jax.sharding import Mesh
from jax.sharding import PartitionSpec as P

HDIM = 128
TILE = 64
HEAD = ("y", "core")
SLAB = ("z", "x")
MIB = 1024 * 1024


def whole_block(array):
    rank = len(array.shape)
    return pl.BlockSpec(array.shape, lambda *_: (0,) * rank)


def params(mib):
    return pltpu.CompilerParams(vmem_limit_bytes=mib * MIB)


def normed(total, gain):
    return total * lax.rsqrt(jnp.mean(total * total, axis=-1, keepdims=True) + 1e-06) * gain


def summed(ref, low, high):
    return jnp.sum(ref[:, :, low:high].astype(jnp.float32), axis=0)


def pack_kernel(share_ref, gain_ref, out_ref):
    width = out_ref.shape[1] // 2
    for low in range(0, width, HDIM):
        total = summed(share_ref, low, low + HDIM)
        out_ref[:, low : low + HDIM] = normed(total, gain_ref[...]).astype(jnp.bfloat16)
    out_ref[:, width:] = summed(share_ref, width, 2 * width).astype(jnp.bfloat16)


def pack(share, gain):
    return pl.pallas_call(
        pack_kernel,
        out_shape=jax.ShapeDtypeStruct(share.shape[1:], jnp.bfloat16),
        compiler_params=params(16),
    )(share, gain.reshape(1, HDIM))


def attention_kernel(share_ref, gain_ref, live_ref, before_ref, own_ref, after_ref, out_ref):
    rows, width = out_ref.shape
    near = (before_ref, own_ref, after_ref)
    scale = 1.0 / HDIM**0.5
    for low in range(0, width, HDIM):
        query = normed(summed(share_ref, low, low + HDIM), gain_ref[...]).astype(jnp.bfloat16)
        keys = jnp.concatenate([r[:, low : low + HDIM] for r in near], axis=0)
        values = jnp.concatenate([r[:, width + low : width + low + HDIM] for r in near], axis=0)
        score = lax.dot_general(
            query, keys, (((1,), (1,)), ((), ())), preferred_element_type=jnp.float32
        )
        allowed = jnp.concatenate(
            [
                jnp.broadcast_to(live_ref[pl.ds(low // HDIM * (rows // TILE) + t, 1), :], (TILE, 3 * rows))
                for t in range(rows // TILE)
            ],
            axis=0,
        )
        weight = jnp.where(allowed > 0, jnp.exp(score * scale), 0.0)
        total = jnp.sum(weight, axis=1, keepdims=True)
        mixed = jnp.dot(weight.astype(jnp.bfloat16), values, preferred_element_type=jnp.float32)
        out_ref[:, low : low + HDIM] = (mixed / total).astype(jnp.bfloat16)


def attention(query, gain, live, before, own, after):
    rows, width = query.shape[1:]
    return pl.pallas_call(
        attention_kernel,
        out_shape=jax.ShapeDtypeStruct((rows, width), jnp.bfloat16),
        compiler_params=params(16),
    )(query, gain.reshape(1, HDIM), live, before, own, after)


def live_rows(key_tiles, tiles_here):
    near_ids = (lax.axis_index(SLAB) - 1) * tiles_here + jnp.arange(3 * tiles_here, dtype=jnp.int32)
    live = jnp.any(key_tiles[:, :, :, None] == near_ids[None, None, None, :], axis=2)
    live = live.reshape(-1, 3 * tiles_here).astype(jnp.float32)
    return jnp.repeat(live, TILE, axis=1)


def on_device(tokens, q_weight, k_weight, v_weight, out_weight, q_gain, k_gain, key_tiles):
    rows, width = tokens.shape
    n_x, n_z, n_head = (lax.axis_size(a) for a in ("x", "z", HEAD))
    part = width // n_x

    stacked = jnp.concatenate([q_weight, k_weight, v_weight], axis=1)
    weights = lax.all_gather(stacked, "z", axis=0, tiled=True)

    turned = [(z * n_head + h, h * n_z + z) for z in range(n_z) for h in range(n_head)]
    columns = lax.ppermute(out_weight.T, ("z",) + HEAD, turned)

    pieces = tokens.reshape(rows, n_x, part).transpose(1, 0, 2)
    pieces = lax.all_to_all(pieces, "x", split_axis=0, concat_axis=0, tiled=True)
    pieces = lax.all_gather(pieces.reshape(n_x * rows, part), HEAD, axis=0, tiled=False)
    pieces, columns = lax.optimization_barrier((pieces, columns))
    group = pieces.transpose(1, 0, 2).reshape(n_x * rows, n_head * part)

    columns = lax.all_gather(columns, "x", axis=0, tiled=True)
    projection = lax.all_gather(columns, "z", axis=0, tiled=False)
    weights, group, _ = lax.optimization_barrier((weights, group, columns))

    def shares(piece):
        share = jnp.dot(group, piece, preferred_element_type=jnp.float32).astype(jnp.bfloat16)
        return share.reshape(n_x, rows, -1)

    query = shares(weights[:, :width])
    query = lax.all_to_all(query, "x", split_axis=0, concat_axis=0, tiled=True)
    key_value = shares(weights[:, width:])
    query, key_value = lax.optimization_barrier((query, key_value))
    key_value = lax.all_to_all(key_value, "x", split_axis=0, concat_axis=0, tiled=True)
    packed = pack(key_value, k_gain)
    count = lax.axis_size(SLAB)
    before = lax.ppermute(packed, SLAB, [(i, i + 1) for i in range(count - 1)])
    after = lax.ppermute(packed, SLAB, [(i + 1, i) for i in range(count - 1)])
    live = live_rows(key_tiles, rows // TILE)
    attended = attention(query, q_gain, live, before, packed, after)
    everyone = lax.all_gather(attended, HEAD, axis=0, tiled=False)
    total = jnp.einsum("hrd,hnd->rn", everyone, projection, preferred_element_type=jnp.float32)
    return total.astype(jnp.bfloat16)


def solution(mesh):
    n_slab, n_head, n_cfg = (mesh.shape[a] for a in ("slab", "head", "cfg"))
    fine = Mesh(
        mesh.devices.reshape(n_slab // 4, 4, n_head // 2, 2, n_cfg), ("z", "x", "y", "core", "cfg")
    )
    placed = (
        P(("cfg",) + SLAB, HEAD),
        P(SLAB, HEAD),
        P(SLAB, HEAD),
        P(SLAB, HEAD),
        P(HEAD, SLAB),
        P(),
        P(),
        P(HEAD, SLAB, None),
    )
    return jax.shard_map(
        on_device, mesh=fine, in_specs=placed, out_specs=P(("cfg",) + SLAB, HEAD), check_vma=False
    )
```

```python
import jax
import jax.numpy as jnp
from jax import lax
from jax.experimental import pallas as pl
from jax.experimental.pallas import tpu as pltpu
from jax.sharding import Mesh
from jax.sharding import PartitionSpec as P

HDIM = 128
TILE = 64
HEAD = ("y", "core")
SLAB = ("z", "x")
MIB = 1024 * 1024


def whole_block(array):
    rank = len(array.shape)
    return pl.BlockSpec(array.shape, lambda *_: (0,) * rank)


def params(mib):
    return pltpu.CompilerParams(vmem_limit_bytes=mib * MIB)


def normed(total, gain):
    return total * lax.rsqrt(jnp.mean(total * total, axis=-1, keepdims=True) + 1e-06) * gain


def summed(ref, low, high):
    return jnp.sum(ref[:, :, low:high].astype(jnp.float32), axis=0)


def pack_kernel(share_ref, gain_ref, out_ref):
    width = out_ref.shape[1] // 2
    for low in range(0, width, HDIM):
        total = summed(share_ref, low, low + HDIM)
        out_ref[:, low : low + HDIM] = normed(total, gain_ref[...]).astype(jnp.bfloat16)
    out_ref[:, width:] = summed(share_ref, width, 2 * width).astype(jnp.bfloat16)


def pack(share, gain):
    return pl.pallas_call(
        pack_kernel,
        out_shape=jax.ShapeDtypeStruct(share.shape[1:], jnp.bfloat16),
        compiler_params=params(16),
    )(share, gain.reshape(1, HDIM))


def attention_kernel(share_ref, gain_ref, live_ref, odd_ref, own_ref, even_ref, out_ref):
    rows, width = out_ref.shape
    near = (odd_ref, own_ref, even_ref)
    scale = 1.0 / HDIM**0.5
    for low in range(0, width, HDIM):
        query = normed(summed(share_ref, low, low + HDIM), gain_ref[...]).astype(jnp.bfloat16)
        keys = jnp.concatenate([r[:, low : low + HDIM] for r in near], axis=0)
        values = jnp.concatenate([r[:, width + low : width + low + HDIM] for r in near], axis=0)
        score = lax.dot_general(
            query, keys, (((1,), (1,)), ((), ())), preferred_element_type=jnp.float32
        )
        allowed = jnp.concatenate(
            [
                jnp.broadcast_to(live_ref[pl.ds(low // HDIM * (rows // TILE) + t, 1), :], (TILE, 3 * rows))
                for t in range(rows // TILE)
            ],
            axis=0,
        )
        weight = jnp.where(allowed > 0, jnp.exp(score * scale), 0.0)
        total = jnp.sum(weight, axis=1, keepdims=True)
        mixed = jnp.dot(weight.astype(jnp.bfloat16), values, preferred_element_type=jnp.float32)
        out_ref[:, low : low + HDIM] = (mixed / total).astype(jnp.bfloat16)


def attention(query, gain, live, odd, own, even):
    rows, width = query.shape[1:]
    return pl.pallas_call(
        attention_kernel,
        out_shape=jax.ShapeDtypeStruct((rows, width), jnp.bfloat16),
        compiler_params=params(16),
    )(query, gain.reshape(1, HDIM), live, odd, own, even)


def live_rows(key_tiles, tiles_here):
    slab = lax.axis_index(SLAB)
    even_at = jnp.where(slab % 2 == 0, slab + 1, slab - 1)
    slabs = jnp.stack([2 * slab - even_at, slab, even_at])
    near_ids = slabs[:, None] * tiles_here + jnp.arange(tiles_here, dtype=jnp.int32)
    near_ids = near_ids.reshape(-1)
    live = jnp.any(key_tiles[:, :, :, None] == near_ids[None, None, None, :], axis=2)
    live = live.reshape(-1, 3 * tiles_here).astype(jnp.float32)
    return jnp.repeat(live, TILE, axis=1)


def on_device(tokens, q_weight, k_weight, v_weight, out_weight, q_gain, k_gain, key_tiles):
    rows, width = tokens.shape
    n_x, n_z, n_head = (lax.axis_size(a) for a in ("x", "z", HEAD))
    part = width // n_x

    stacked = jnp.concatenate([q_weight, k_weight, v_weight], axis=1)
    weights = lax.all_gather(stacked, "z", axis=0, tiled=True)

    turned = [(z * n_head + h, h * n_z + z) for z in range(n_z) for h in range(n_head)]
    columns = lax.ppermute(out_weight.T, ("z",) + HEAD, turned)

    pieces = tokens.reshape(rows, n_x, part).transpose(1, 0, 2)
    pieces = lax.all_to_all(pieces, "x", split_axis=0, concat_axis=0, tiled=True)
    pieces = lax.all_gather(pieces.reshape(n_x * rows, part), HEAD, axis=0, tiled=False)
    pieces, columns = lax.optimization_barrier((pieces, columns))
    group = pieces.transpose(1, 0, 2).reshape(n_x * rows, n_head * part)

    columns = lax.all_gather(columns, "x", axis=0, tiled=True)
    projection = lax.all_gather(columns, "z", axis=0, tiled=False)
    weights, group, _ = lax.optimization_barrier((weights, group, columns))

    def shares(piece):
        share = jnp.dot(group, piece, preferred_element_type=jnp.float32).astype(jnp.bfloat16)
        return share.reshape(n_x, rows, -1)

    key_value = shares(weights[:, width:])
    key_value = lax.all_to_all(key_value, "x", split_axis=0, concat_axis=0, tiled=True)
    query = shares(weights[:, :width])
    query = lax.all_to_all(query, "x", split_axis=0, concat_axis=0, tiled=True)
    packed = pack(key_value, k_gain)
    count = lax.axis_size(SLAB)
    swaps = [
        [pair for i in range(first, count - 1, 2) for pair in ((i, i + 1), (i + 1, i))]
        for first in (1, 0)
    ]
    odd, even = (lax.ppermute(packed, SLAB, pairs) for pairs in swaps)
    live = live_rows(key_tiles, rows // TILE)
    attended = attention(query, q_gain, live, odd, packed, even)
    everyone = lax.all_gather(attended, HEAD, axis=0, tiled=False)
    total = jnp.einsum("hrd,hnd->rn", everyone, projection, preferred_element_type=jnp.float32)
    return total.astype(jnp.bfloat16)


def solution(mesh):
    n_slab, n_head, n_cfg = (mesh.shape[a] for a in ("slab", "head", "cfg"))
    fine = Mesh(
        mesh.devices.reshape(n_slab // 4, 4, n_head // 2, 2, n_cfg), ("z", "x", "y", "core", "cfg")
    )
    placed = (
        P(("cfg",) + SLAB, HEAD),
        P(SLAB, HEAD),
        P(SLAB, HEAD),
        P(SLAB, HEAD),
        P(HEAD, SLAB),
        P(),
        P(),
        P(HEAD, SLAB, None),
    )
    return jax.shard_map(
        on_device, mesh=fine, in_specs=placed, out_specs=P(("cfg",) + SLAB, HEAD), check_vma=False
    )
```

```python
import jax
import jax.numpy as jnp
from jax import lax
from jax.experimental import pallas as pl
from jax.experimental.pallas import tpu as pltpu
from jax.sharding import Mesh
from jax.sharding import PartitionSpec as P

HDIM = 128
TILE = 64
HEAD = ("y", "core")
SLAB = ("z", "x")
MIB = 1024 * 1024


def whole_block(array):
    rank = len(array.shape)
    return pl.BlockSpec(array.shape, lambda *_: (0,) * rank)


def params(mib):
    return pltpu.CompilerParams(vmem_limit_bytes=mib * MIB)


def normed(total, gain):
    return total * lax.rsqrt(jnp.mean(total * total, axis=-1, keepdims=True) + 1e-06) * gain


def summed(ref, low, high):
    return jnp.sum(ref[:, :, low:high].astype(jnp.float32), axis=0)


def pack_kernel(share_ref, gain_ref, out_ref):
    width = out_ref.shape[1] // 2
    for low in range(0, width, HDIM):
        total = summed(share_ref, low, low + HDIM)
        out_ref[:, low : low + HDIM] = normed(total, gain_ref[...]).astype(jnp.bfloat16)
    out_ref[:, width:] = summed(share_ref, width, 2 * width).astype(jnp.bfloat16)


def pack(share, gain):
    return pl.pallas_call(
        pack_kernel,
        out_shape=jax.ShapeDtypeStruct(share.shape[1:], jnp.bfloat16),
        compiler_params=params(16),
    )(share, gain.reshape(1, HDIM))


def attention_kernel(share_ref, gain_ref, live_ref, odd_ref, own_ref, even_ref, out_ref):
    rows, width = out_ref.shape
    near = (odd_ref, own_ref, even_ref)
    scale = 1.0 / HDIM**0.5
    for low in range(0, width, HDIM):
        query = normed(summed(share_ref, low, low + HDIM), gain_ref[...]).astype(jnp.bfloat16)
        keys = jnp.concatenate([r[:, low : low + HDIM] for r in near], axis=0)
        values = jnp.concatenate([r[:, width + low : width + low + HDIM] for r in near], axis=0)
        score = lax.dot_general(
            query, keys, (((1,), (1,)), ((), ())), preferred_element_type=jnp.float32
        )
        allowed = jnp.concatenate(
            [
                jnp.broadcast_to(live_ref[pl.ds(low // HDIM * (rows // TILE) + t, 1), :], (TILE, 3 * rows))
                for t in range(rows // TILE)
            ],
            axis=0,
        )
        weight = jnp.where(allowed > 0, jnp.exp(score * scale), 0.0)
        total = jnp.sum(weight, axis=1, keepdims=True)
        mixed = jnp.dot(weight.astype(jnp.bfloat16), values, preferred_element_type=jnp.float32)
        out_ref[:, low : low + HDIM] = (mixed / total).astype(jnp.bfloat16)


def attention(query, gain, live, odd, own, even):
    rows, width = query.shape[1:]
    return pl.pallas_call(
        attention_kernel,
        out_shape=jax.ShapeDtypeStruct((rows, width), jnp.bfloat16),
        compiler_params=params(16),
    )(query, gain.reshape(1, HDIM), live, odd, own, even)


def live_rows(key_tiles, tiles_here):
    slab = lax.axis_index(SLAB)
    even_at = jnp.where(slab % 2 == 0, slab + 1, slab - 1)
    slabs = jnp.stack([2 * slab - even_at, slab, even_at])
    near_ids = slabs[:, None] * tiles_here + jnp.arange(tiles_here, dtype=jnp.int32)
    near_ids = near_ids.reshape(-1)
    live = jnp.any(key_tiles[:, :, :, None] == near_ids[None, None, None, :], axis=2)
    live = live.reshape(-1, 3 * tiles_here).astype(jnp.float32)
    return jnp.repeat(live, TILE, axis=1)


def on_device(tokens, q_weight, k_weight, v_weight, out_weight, q_gain, k_gain, key_tiles):
    rows, width = tokens.shape
    n_x, n_z, n_head = (lax.axis_size(a) for a in ("x", "z", HEAD))
    part = width // n_x

    stacked = jnp.concatenate([q_weight, k_weight, v_weight], axis=1)
    weights = lax.all_gather(stacked, "z", axis=0, tiled=True)

    turned = [(z * n_head + h, h * n_z + z) for z in range(n_z) for h in range(n_head)]
    columns = lax.ppermute(out_weight.T, ("z",) + HEAD, turned)

    pieces = tokens.reshape(rows, n_x, part).transpose(1, 0, 2)
    pieces = lax.all_to_all(pieces, "x", split_axis=0, concat_axis=0, tiled=True)
    pieces = lax.all_gather(pieces.reshape(n_x * rows, part), HEAD, axis=0, tiled=False)
    pieces, columns = lax.optimization_barrier((pieces, columns))
    group = pieces.transpose(1, 0, 2).reshape(n_x * rows, n_head * part)

    columns = lax.all_gather(columns, "x", axis=0, tiled=True)
    projection = lax.all_gather(columns, "z", axis=0, tiled=False)
    weights, group, _ = lax.optimization_barrier((weights, group, columns))

    def shares(piece):
        share = jnp.dot(group, piece, preferred_element_type=jnp.float32).astype(jnp.bfloat16)
        return share.reshape(n_x, rows, -1)

    key_value = shares(weights[:, width:])
    key_value = lax.all_to_all(key_value, "x", split_axis=0, concat_axis=0, tiled=True)
    query = shares(weights[:, :width])
    packed = pack(key_value, k_gain)
    query, packed = lax.optimization_barrier((query, packed))
    query = lax.all_to_all(query, "x", split_axis=0, concat_axis=0, tiled=True)
    count = lax.axis_size(SLAB)
    swaps = [
        [pair for i in range(first, count - 1, 2) for pair in ((i, i + 1), (i + 1, i))]
        for first in (1, 0)
    ]
    odd, even = (lax.ppermute(packed, SLAB, pairs) for pairs in swaps)
    live = live_rows(key_tiles, rows // TILE)
    attended = attention(query, q_gain, live, odd, packed, even)
    everyone = lax.all_gather(attended, HEAD, axis=0, tiled=False)
    total = jnp.einsum("hrd,hnd->rn", everyone, projection, preferred_element_type=jnp.float32)
    return total.astype(jnp.bfloat16)


def solution(mesh):
    n_slab, n_head, n_cfg = (mesh.shape[a] for a in ("slab", "head", "cfg"))
    fine = Mesh(
        mesh.devices.reshape(n_slab // 4, 4, n_head // 2, 2, n_cfg), ("z", "x", "y", "core", "cfg")
    )
    placed = (
        P(("cfg",) + SLAB, HEAD),
        P(SLAB, HEAD),
        P(SLAB, HEAD),
        P(SLAB, HEAD),
        P(HEAD, SLAB),
        P(),
        P(),
        P(HEAD, SLAB, None),
    )
    return jax.shard_map(
        on_device, mesh=fine, in_specs=placed, out_specs=P(("cfg",) + SLAB, HEAD), check_vma=False
    )
```

```python
import jax
import jax.numpy as jnp
from jax import lax
from jax.experimental import pallas as pl
from jax.experimental.pallas import tpu as pltpu
from jax.sharding import Mesh
from jax.sharding import PartitionSpec as P

HDIM = 128
TILE = 64
HEAD = ("y", "core")
SLAB = ("z", "x")
MIB = 1024 * 1024


def whole_block(array):
    rank = len(array.shape)
    return pl.BlockSpec(array.shape, lambda *_: (0,) * rank)


def params(mib):
    return pltpu.CompilerParams(vmem_limit_bytes=mib * MIB)


def normed(total, gain):
    return total * lax.rsqrt(jnp.mean(total * total, axis=-1, keepdims=True) + 1e-06) * gain


def summed(ref, low, high):
    return jnp.sum(ref[:, :, low:high].astype(jnp.float32), axis=0)


def pack_kernel(share_ref, gain_ref, out_ref):
    width = out_ref.shape[1] // 2
    for low in range(0, width, HDIM):
        total = summed(share_ref, low, low + HDIM)
        out_ref[:, low : low + HDIM] = normed(total, gain_ref[...]).astype(jnp.bfloat16)
    out_ref[:, width:] = summed(share_ref, width, 2 * width).astype(jnp.bfloat16)


def pack(share, gain):
    return pl.pallas_call(
        pack_kernel,
        out_shape=jax.ShapeDtypeStruct(share.shape[1:], jnp.bfloat16),
        compiler_params=params(16),
    )(share, gain.reshape(1, HDIM))


def attention_kernel(kept_ref, came_ref, gain_ref, live_ref, odd_ref, own_ref, even_ref, out_ref):
    rows, width = out_ref.shape
    near = (odd_ref, own_ref, even_ref)
    scale = 1.0 / HDIM**0.5
    for low in range(0, width, HDIM):
        head = slice(low, low + HDIM)
        query = kept_ref[:, head] + came_ref[:, head].astype(jnp.float32)
        query = normed(query, gain_ref[...]).astype(jnp.bfloat16)
        keys = jnp.concatenate([r[:, low : low + HDIM] for r in near], axis=0)
        values = jnp.concatenate([r[:, width + low : width + low + HDIM] for r in near], axis=0)
        score = lax.dot_general(
            query, keys, (((1,), (1,)), ((), ())), preferred_element_type=jnp.float32
        )
        allowed = jnp.concatenate(
            [
                jnp.broadcast_to(live_ref[pl.ds(low // HDIM * (rows // TILE) + t, 1), :], (TILE, 3 * rows))
                for t in range(rows // TILE)
            ],
            axis=0,
        )
        weight = jnp.where(allowed > 0, jnp.exp(score * scale), 0.0)
        total = jnp.sum(weight, axis=1, keepdims=True)
        mixed = jnp.dot(weight.astype(jnp.bfloat16), values, preferred_element_type=jnp.float32)
        out_ref[:, low : low + HDIM] = (mixed / total).astype(jnp.bfloat16)


def attention(kept, came, gain, live, odd, own, even):
    rows, width = kept.shape
    return pl.pallas_call(
        attention_kernel,
        out_shape=jax.ShapeDtypeStruct((rows, width), jnp.bfloat16),
        compiler_params=params(16),
    )(kept, came, gain.reshape(1, HDIM), live, odd, own, even)


def live_rows(key_tiles, tiles_here):
    slab = lax.axis_index(SLAB)
    even_at = jnp.where(slab % 2 == 0, slab + 1, slab - 1)
    slabs = jnp.stack([2 * slab - even_at, slab, even_at])
    near_ids = slabs[:, None] * tiles_here + jnp.arange(tiles_here, dtype=jnp.int32)
    near_ids = near_ids.reshape(-1)
    live = jnp.any(key_tiles[:, :, :, None] == near_ids[None, None, None, :], axis=2)
    live = live.reshape(-1, 3 * tiles_here).astype(jnp.float32)
    return jnp.repeat(live, TILE, axis=1)


def on_device(tokens, q_weight, k_weight, v_weight, out_weight, q_gain, k_gain, key_tiles):
    rows, width = tokens.shape
    n_x, n_z, n_head = (lax.axis_size(a) for a in ("x", "z", HEAD))
    part = width // n_x

    stacked = jnp.concatenate([q_weight, k_weight, v_weight], axis=1)
    weights = lax.all_gather(stacked, "z", axis=0, tiled=True)

    turned = [(z * n_head + h, h * n_z + z) for z in range(n_z) for h in range(n_head)]
    columns = lax.ppermute(out_weight.T, ("z",) + HEAD, turned)

    pieces = tokens.reshape(rows, n_x, part).transpose(1, 0, 2)
    pieces = lax.all_to_all(pieces, "x", split_axis=0, concat_axis=0, tiled=True)
    pieces = lax.all_gather(pieces.reshape(n_x * rows, part), HEAD, axis=0, tiled=False)
    pieces, columns = lax.optimization_barrier((pieces, columns))
    group = pieces.transpose(1, 0, 2).reshape(n_x * rows, n_head * part)

    columns = lax.all_gather(columns, "x", axis=0, tiled=True)
    projection = lax.all_gather(columns, "z", axis=0, tiled=False)
    weights, group, _ = lax.optimization_barrier((weights, group, columns))

    def shares(piece):
        share = jnp.dot(group, piece, preferred_element_type=jnp.float32).astype(jnp.bfloat16)
        return share.reshape(n_x, rows, -1)

    key_value = shares(weights[:, width:])
    key_value = lax.all_to_all(key_value, "x", split_axis=0, concat_axis=0, tiled=True)
    query = shares(weights[:, :width]).reshape(n_x // 2, 2, rows, width)
    place = lax.axis_index("x")
    kept, sent = (
        lax.dynamic_index_in_dim(query, side, 1, keepdims=False)
        for side in (place % 2, 1 - place % 2)
    )
    came = lax.ppermute(sent, "x", [(i, i ^ 1) for i in range(n_x)])
    pair = kept.astype(jnp.float32) + came.astype(jnp.float32)
    kept, sent = (
        lax.dynamic_index_in_dim(pair, side, 0, keepdims=False)
        for side in (place // 2, 1 - place // 2)
    )
    came = lax.ppermute(sent.astype(jnp.bfloat16), "x", [(i, i ^ 2) for i in range(n_x)])
    packed = pack(key_value, k_gain)
    count = lax.axis_size(SLAB)
    swaps = [
        [pair for i in range(first, count - 1, 2) for pair in ((i, i + 1), (i + 1, i))]
        for first in (1, 0)
    ]
    odd, even = (lax.ppermute(packed, SLAB, pairs) for pairs in swaps)
    live = live_rows(key_tiles, rows // TILE)
    attended = attention(kept, came, q_gain, live, odd, packed, even)
    everyone = lax.all_gather(attended, HEAD, axis=0, tiled=False)
    total = jnp.einsum("hrd,hnd->rn", everyone, projection, preferred_element_type=jnp.float32)
    return total.astype(jnp.bfloat16)


def solution(mesh):
    n_slab, n_head, n_cfg = (mesh.shape[a] for a in ("slab", "head", "cfg"))
    fine = Mesh(
        mesh.devices.reshape(n_slab // 4, 4, n_head // 2, 2, n_cfg), ("z", "x", "y", "core", "cfg")
    )
    placed = (
        P(("cfg",) + SLAB, HEAD),
        P(SLAB, HEAD),
        P(SLAB, HEAD),
        P(SLAB, HEAD),
        P(HEAD, SLAB),
        P(),
        P(),
        P(HEAD, SLAB, None),
    )
    return jax.shard_map(
        on_device, mesh=fine, in_specs=placed, out_specs=P(("cfg",) + SLAB, HEAD), check_vma=False
    )
```

```python
import jax
import jax.numpy as jnp
from jax import lax
from jax.experimental import pallas as pl
from jax.experimental.pallas import tpu as pltpu
from jax.sharding import Mesh
from jax.sharding import PartitionSpec as P

HDIM = 128
TILE = 64
HEAD = ("y", "core")
SLAB = ("z", "x")
MIB = 1024 * 1024


def whole_block(array):
    rank = len(array.shape)
    return pl.BlockSpec(array.shape, lambda *_: (0,) * rank)


def params(mib):
    return pltpu.CompilerParams(vmem_limit_bytes=mib * MIB)


def normed(total, gain):
    return total * lax.rsqrt(jnp.mean(total * total, axis=-1, keepdims=True) + 1e-06) * gain


def summed(ref, low, high):
    return jnp.sum(ref[:, :, low:high].astype(jnp.float32), axis=0)


def pack_kernel(share_ref, gain_ref, out_ref):
    width = out_ref.shape[1] // 2
    for low in range(0, width, HDIM):
        total = summed(share_ref, low, low + HDIM)
        out_ref[:, low : low + HDIM] = normed(total, gain_ref[...]).astype(jnp.bfloat16)
    out_ref[:, width:] = summed(share_ref, width, 2 * width).astype(jnp.bfloat16)


def pack(share, gain):
    return pl.pallas_call(
        pack_kernel,
        out_shape=jax.ShapeDtypeStruct(share.shape[1:], jnp.bfloat16),
        compiler_params=params(16),
    )(share, gain.reshape(1, HDIM))


def copy_kernel(source_ref, out_ref):
    out_ref[...] = source_ref[...]


def copied(array):
    return pl.pallas_call(
        copy_kernel,
        out_shape=jax.ShapeDtypeStruct(array.shape, array.dtype),
        compiler_params=params(16),
    )(array)


def attention_kernel(share_ref, gain_ref, live_ref, odd_ref, own_ref, even_ref, out_ref):
    rows, width = out_ref.shape
    near = (odd_ref, own_ref, even_ref)
    scale = 1.0 / HDIM**0.5
    for low in range(0, width, HDIM):
        query = normed(summed(share_ref, low, low + HDIM), gain_ref[...]).astype(jnp.bfloat16)
        keys = jnp.concatenate([r[:, low : low + HDIM] for r in near], axis=0)
        values = jnp.concatenate([r[:, width + low : width + low + HDIM] for r in near], axis=0)
        score = lax.dot_general(
            query, keys, (((1,), (1,)), ((), ())), preferred_element_type=jnp.float32
        )
        allowed = jnp.concatenate(
            [
                jnp.broadcast_to(live_ref[pl.ds(low // HDIM * (rows // TILE) + t, 1), :], (TILE, 3 * rows))
                for t in range(rows // TILE)
            ],
            axis=0,
        )
        weight = jnp.where(allowed > 0, jnp.exp(score * scale), 0.0)
        total = jnp.sum(weight, axis=1, keepdims=True)
        mixed = jnp.dot(weight.astype(jnp.bfloat16), values, preferred_element_type=jnp.float32)
        out_ref[:, low : low + HDIM] = (mixed / total).astype(jnp.bfloat16)


def attention(query, gain, live, odd, own, even):
    rows, width = query.shape[1:]
    return pl.pallas_call(
        attention_kernel,
        out_shape=jax.ShapeDtypeStruct((rows, width), jnp.bfloat16),
        compiler_params=params(16),
    )(query, gain.reshape(1, HDIM), live, odd, own, even)


def live_rows(key_tiles, tiles_here):
    slab = lax.axis_index(SLAB)
    even_at = jnp.where(slab % 2 == 0, slab + 1, slab - 1)
    slabs = jnp.stack([2 * slab - even_at, slab, even_at])
    near_ids = slabs[:, None] * tiles_here + jnp.arange(tiles_here, dtype=jnp.int32)
    near_ids = near_ids.reshape(-1)
    live = jnp.any(key_tiles[:, :, :, None] == near_ids[None, None, None, :], axis=2)
    live = live.reshape(-1, 3 * tiles_here).astype(jnp.float32)
    return jnp.repeat(live, TILE, axis=1)


def on_device(tokens, q_weight, k_weight, v_weight, out_weight, q_gain, k_gain, key_tiles):
    rows, width = tokens.shape
    n_x, n_z, n_head = (lax.axis_size(a) for a in ("x", "z", HEAD))
    part = width // n_x

    stacked = jnp.concatenate([q_weight, k_weight, v_weight], axis=1)
    weights = lax.all_gather(stacked, "z", axis=0, tiled=True)

    turned = [(z * n_head + h, h * n_z + z) for z in range(n_z) for h in range(n_head)]
    columns = lax.ppermute(out_weight.T, ("z",) + HEAD, turned)

    pieces = tokens.reshape(rows, n_x, part).transpose(1, 0, 2)
    pieces = lax.all_to_all(pieces, "x", split_axis=0, concat_axis=0, tiled=True)
    pieces = lax.all_gather(pieces.reshape(n_x * rows, part), HEAD, axis=0, tiled=False)
    pieces, columns = lax.optimization_barrier((pieces, columns))
    group = pieces.transpose(1, 0, 2).reshape(n_x * rows, n_head * part)

    columns = lax.all_gather(columns, "x", axis=0, tiled=True)
    projection = lax.all_gather(columns, "z", axis=0, tiled=False)
    weights, group, _ = lax.optimization_barrier((weights, group, columns))

    def shares(piece):
        share = jnp.dot(group, piece, preferred_element_type=jnp.float32).astype(jnp.bfloat16)
        return share.reshape(n_x, rows, -1)

    key_value = shares(weights[:, width:])
    key_value = lax.all_to_all(key_value, "x", split_axis=0, concat_axis=0, tiled=True)
    query = shares(weights[:, :width])
    packed = pack(key_value, k_gain)
    query, packed = lax.optimization_barrier((query, packed))
    query = lax.all_to_all(query, "x", split_axis=0, concat_axis=0, tiled=True)
    count = lax.axis_size(SLAB)
    swaps = [
        [pair for i in range(first, count - 1, 2) for pair in ((i, i + 1), (i + 1, i))]
        for first in (1, 0)
    ]
    odd = lax.ppermute(packed, SLAB, swaps[0])
    even = lax.ppermute(copied(packed), SLAB, swaps[1])
    live = live_rows(key_tiles, rows // TILE)
    attended = attention(query, q_gain, live, odd, packed, even)
    everyone = lax.all_gather(attended, HEAD, axis=0, tiled=False)
    total = jnp.einsum("hrd,hnd->rn", everyone, projection, preferred_element_type=jnp.float32)
    return total.astype(jnp.bfloat16)


def solution(mesh):
    n_slab, n_head, n_cfg = (mesh.shape[a] for a in ("slab", "head", "cfg"))
    fine = Mesh(
        mesh.devices.reshape(n_slab // 4, 4, n_head // 2, 2, n_cfg), ("z", "x", "y", "core", "cfg")
    )
    placed = (
        P(("cfg",) + SLAB, HEAD),
        P(SLAB, HEAD),
        P(SLAB, HEAD),
        P(SLAB, HEAD),
        P(HEAD, SLAB),
        P(),
        P(),
        P(HEAD, SLAB, None),
    )
    return jax.shard_map(
        on_device, mesh=fine, in_specs=placed, out_specs=P(("cfg",) + SLAB, HEAD), check_vma=False
    )
```

```python
import jax
import jax.numpy as jnp
from jax import lax
from jax.experimental import pallas as pl
from jax.experimental.pallas import tpu as pltpu
from jax.sharding import Mesh
from jax.sharding import PartitionSpec as P

HDIM = 128
TILE = 64
HEAD = ("y", "core")
SLAB = ("z", "x")
MIB = 1024 * 1024


def whole_block(array):
    rank = len(array.shape)
    return pl.BlockSpec(array.shape, lambda *_: (0,) * rank)


def params(mib):
    return pltpu.CompilerParams(vmem_limit_bytes=mib * MIB)


def normed(total, gain):
    return total * lax.rsqrt(jnp.mean(total * total, axis=-1, keepdims=True) + 1e-06) * gain


def summed(ref, low, high):
    return jnp.sum(ref[:, :, low:high].astype(jnp.float32), axis=0)


def pack_kernel(share_ref, gain_ref, out_ref):
    width = out_ref.shape[1] // 2
    for low in range(0, width, HDIM):
        total = summed(share_ref, low, low + HDIM)
        out_ref[:, low : low + HDIM] = normed(total, gain_ref[...]).astype(jnp.bfloat16)
    out_ref[:, width:] = summed(share_ref, width, 2 * width).astype(jnp.bfloat16)


def pack(share, gain):
    return pl.pallas_call(
        pack_kernel,
        out_shape=jax.ShapeDtypeStruct(share.shape[1:], jnp.bfloat16),
        compiler_params=params(16),
    )(share, gain.reshape(1, HDIM))


def copy_kernel(source_ref, out_ref):
    out_ref[...] = source_ref[...]


def copied(array):
    return pl.pallas_call(
        copy_kernel,
        out_shape=jax.ShapeDtypeStruct(array.shape, array.dtype),
        compiler_params=params(16),
    )(array)


def attention_kernel(share_ref, gain_ref, live_ref, odd_ref, own_ref, even_ref, out_ref):
    rows, width = out_ref.shape
    near = (odd_ref, own_ref, even_ref)
    scale = 1.0 / HDIM**0.5
    for low in range(0, width, HDIM):
        query = normed(summed(share_ref, low, low + HDIM), gain_ref[...]).astype(jnp.bfloat16)
        keys = jnp.concatenate([r[:, low : low + HDIM] for r in near], axis=0)
        values = jnp.concatenate([r[:, width + low : width + low + HDIM] for r in near], axis=0)
        score = lax.dot_general(
            query, keys, (((1,), (1,)), ((), ())), preferred_element_type=jnp.float32
        )
        allowed = jnp.concatenate(
            [
                jnp.broadcast_to(live_ref[pl.ds(low // HDIM * (rows // TILE) + t, 1), :], (TILE, 3 * rows))
                for t in range(rows // TILE)
            ],
            axis=0,
        )
        weight = jnp.where(allowed > 0, jnp.exp(score * scale), 0.0)
        total = jnp.sum(weight, axis=1, keepdims=True)
        mixed = jnp.dot(weight.astype(jnp.bfloat16), values, preferred_element_type=jnp.float32)
        out_ref[:, low : low + HDIM] = (mixed / total).astype(jnp.bfloat16)


def attention(query, gain, live, odd, own, even):
    rows, width = query.shape[1:]
    return pl.pallas_call(
        attention_kernel,
        out_shape=jax.ShapeDtypeStruct((rows, width), jnp.bfloat16),
        compiler_params=params(16),
    )(query, gain.reshape(1, HDIM), live, odd, own, even)


def live_rows(key_tiles, tiles_here):
    slab = lax.axis_index(SLAB)
    even_at = jnp.where(slab % 2 == 0, slab + 1, slab - 1)
    slabs = jnp.stack([2 * slab - even_at, slab, even_at])
    near_ids = slabs[:, None] * tiles_here + jnp.arange(tiles_here, dtype=jnp.int32)
    near_ids = near_ids.reshape(-1)
    live = jnp.any(key_tiles[:, :, :, None] == near_ids[None, None, None, :], axis=2)
    live = live.reshape(-1, 3 * tiles_here).astype(jnp.float32)
    return jnp.repeat(live, TILE, axis=1)


def on_device(tokens, q_weight, k_weight, v_weight, out_weight, q_gain, k_gain, key_tiles):
    rows, width = tokens.shape
    n_x, n_z, n_head = (lax.axis_size(a) for a in ("x", "z", HEAD))
    part = width // n_x

    stacked = jnp.concatenate([q_weight, k_weight, v_weight], axis=1)
    weights = lax.all_gather(stacked, "z", axis=0, tiled=True)

    n_core = lax.axis_size("core")
    rank = [h % n_core * (n_head // n_core) + h // n_core for h in range(n_head)]
    turned = [(z * n_head + h, rank[h] * n_z + z) for z in range(n_z) for h in range(n_head)]
    columns = lax.ppermute(out_weight.T, ("z",) + HEAD, turned)

    pieces = tokens.reshape(rows, n_x, part).transpose(1, 0, 2)
    pieces = lax.all_to_all(pieces, "x", split_axis=0, concat_axis=0, tiled=True)
    pieces = lax.all_gather(pieces.reshape(n_x * rows, part), HEAD, axis=0, tiled=False)
    pieces, columns = lax.optimization_barrier((pieces, columns))
    group = pieces.transpose(1, 0, 2).reshape(n_x * rows, n_head * part)

    columns = lax.all_gather(columns, "x", axis=0, tiled=True)
    projection = lax.all_gather(columns, "z", axis=0, tiled=False)
    weights, group, _ = lax.optimization_barrier((weights, group, columns))

    def shares(piece):
        share = jnp.dot(group, piece, preferred_element_type=jnp.float32).astype(jnp.bfloat16)
        return share.reshape(n_x, rows, -1)

    key_value = shares(weights[:, width:])
    key_value = lax.all_to_all(key_value, "x", split_axis=0, concat_axis=0, tiled=True)
    query = shares(weights[:, :width])
    packed = pack(key_value, k_gain)
    query, packed = lax.optimization_barrier((query, packed))
    query = lax.all_to_all(query, "x", split_axis=0, concat_axis=0, tiled=True)
    count = lax.axis_size(SLAB)
    swaps = [
        [pair for i in range(first, count - 1, 2) for pair in ((i, i + 1), (i + 1, i))]
        for first in (1, 0)
    ]
    odd = lax.ppermute(packed, SLAB, swaps[0])
    even = lax.ppermute(copied(packed), SLAB, swaps[1])
    live = live_rows(key_tiles, rows // TILE)
    attended = attention(query, q_gain, live, odd, packed, even)
    everyone = lax.all_gather(attended, ("core", "y"), axis=0, tiled=False)
    total = jnp.einsum("hrd,hnd->rn", everyone, projection, preferred_element_type=jnp.float32)
    return total.astype(jnp.bfloat16)


def solution(mesh):
    n_slab, n_head, n_cfg = (mesh.shape[a] for a in ("slab", "head", "cfg"))
    fine = Mesh(
        mesh.devices.reshape(n_slab // 4, 4, n_head // 2, 2, n_cfg), ("z", "x", "y", "core", "cfg")
    )
    placed = (
        P(("cfg",) + SLAB, HEAD),
        P(SLAB, HEAD),
        P(SLAB, HEAD),
        P(SLAB, HEAD),
        P(HEAD, SLAB),
        P(),
        P(),
        P(HEAD, SLAB, None),
    )
    return jax.shard_map(
        on_device, mesh=fine, in_specs=placed, out_specs=P(("cfg",) + SLAB, HEAD), check_vma=False
    )
```

```python
import jax
import jax.numpy as jnp
from jax import lax
from jax.experimental import pallas as pl
from jax.experimental.pallas import tpu as pltpu
from jax.sharding import Mesh
from jax.sharding import PartitionSpec as P

HDIM = 128
TILE = 64
SLAB = ("z", "x")
MIB = 1024 * 1024


def whole_block(array):
    rank = len(array.shape)
    return pl.BlockSpec(array.shape, lambda *_: (0,) * rank)


def params(mib):
    return pltpu.CompilerParams(vmem_limit_bytes=mib * MIB)


def normed(total, gain):
    return total * lax.rsqrt(jnp.mean(total * total, axis=-1, keepdims=True) + 1e-06) * gain


def summed(ref, low, high):
    return jnp.sum(ref[:, :, low:high].astype(jnp.float32), axis=0)


def pack_kernel(share_ref, gain_ref, out_ref):
    width = out_ref.shape[1] // 2
    for low in range(0, width, HDIM):
        total = summed(share_ref, low, low + HDIM)
        out_ref[:, low : low + HDIM] = normed(total, gain_ref[...]).astype(jnp.bfloat16)
    out_ref[:, width:] = summed(share_ref, width, 2 * width).astype(jnp.bfloat16)


def pack(share, gain):
    return pl.pallas_call(
        pack_kernel,
        out_shape=jax.ShapeDtypeStruct(share.shape[1:], jnp.bfloat16),
        compiler_params=params(16),
    )(share, gain.reshape(1, HDIM))


def copy_kernel(source_ref, out_ref):
    out_ref[...] = source_ref[...]


def copied(array):
    return pl.pallas_call(
        copy_kernel,
        out_shape=jax.ShapeDtypeStruct(array.shape, array.dtype),
        compiler_params=params(16),
    )(array)


def attention_kernel(share_ref, gain_ref, live_ref, odd_ref, own_ref, even_ref, out_ref):
    rows, width = out_ref.shape
    near = (odd_ref, own_ref, even_ref)
    scale = 1.0 / HDIM**0.5
    for low in range(0, width, HDIM):
        query = normed(summed(share_ref, low, low + HDIM), gain_ref[...]).astype(jnp.bfloat16)
        keys = jnp.concatenate([r[:, low : low + HDIM] for r in near], axis=0)
        values = jnp.concatenate([r[:, width + low : width + low + HDIM] for r in near], axis=0)
        score = lax.dot_general(
            query, keys, (((1,), (1,)), ((), ())), preferred_element_type=jnp.float32
        )
        allowed = jnp.concatenate(
            [
                jnp.broadcast_to(live_ref[pl.ds(low // HDIM * (rows // TILE) + t, 1), :], (TILE, 3 * rows))
                for t in range(rows // TILE)
            ],
            axis=0,
        )
        weight = jnp.where(allowed > 0, jnp.exp(score * scale), 0.0)
        total = jnp.sum(weight, axis=1, keepdims=True)
        mixed = jnp.dot(weight.astype(jnp.bfloat16), values, preferred_element_type=jnp.float32)
        out_ref[:, low : low + HDIM] = (mixed / total).astype(jnp.bfloat16)


def attention(query, gain, live, odd, own, even):
    rows, width = query.shape[1:]
    return pl.pallas_call(
        attention_kernel,
        out_shape=jax.ShapeDtypeStruct((rows, width), jnp.bfloat16),
        compiler_params=params(16),
    )(query, gain.reshape(1, HDIM), live, odd, own, even)


def live_rows(key_tiles, tiles_here):
    slab = lax.axis_index(SLAB)
    even_at = jnp.where(slab % 2 == 0, slab + 1, slab - 1)
    slabs = jnp.stack([2 * slab - even_at, slab, even_at])
    near_ids = slabs[:, None] * tiles_here + jnp.arange(tiles_here, dtype=jnp.int32)
    near_ids = near_ids.reshape(-1)
    live = jnp.any(key_tiles[:, :, :, None] == near_ids[None, None, None, :], axis=2)
    live = live.reshape(-1, 3 * tiles_here).astype(jnp.float32)
    return jnp.repeat(live, TILE, axis=1)


def on_device(tokens, q_weight, k_weight, v_weight, out_weight, q_gain, k_gain, key_tiles):
    rows, width = tokens.shape
    n_x, n_z, n_head = (lax.axis_size(a) for a in ("x", "z", "head"))
    part = width // n_x

    stacked = jnp.concatenate([q_weight, k_weight, v_weight], axis=1)
    weights = lax.all_gather(stacked, "z", axis=0, tiled=True)

    ring = [*range(0, n_head, 2), *range(n_head - 1, 0, -2)]
    turned = [(z * n_head + h, ring.index(h) * n_z + z) for z in range(n_z) for h in range(n_head)]
    columns = lax.ppermute(out_weight.T, ("z", "head"), turned)

    pieces = tokens.reshape(rows, n_x, part).transpose(1, 0, 2)
    pieces = lax.all_to_all(pieces, "x", split_axis=0, concat_axis=0, tiled=True)
    pieces = lax.all_gather(pieces.reshape(n_x * rows, part), "head", axis=0, tiled=False)
    pieces, columns = lax.optimization_barrier((pieces, columns))
    group = pieces.transpose(1, 0, 2).reshape(n_x * rows, n_head * part)

    columns = lax.all_gather(columns, "x", axis=0, tiled=True)
    projection = lax.all_gather(columns, "z", axis=0, tiled=False)
    weights, group, _ = lax.optimization_barrier((weights, group, columns))

    def shares(piece):
        share = jnp.dot(group, piece, preferred_element_type=jnp.float32).astype(jnp.bfloat16)
        return share.reshape(n_x, rows, -1)

    key_value = shares(weights[:, width:])
    key_value = lax.all_to_all(key_value, "x", split_axis=0, concat_axis=0, tiled=True)
    query = shares(weights[:, :width])
    packed = pack(key_value, k_gain)
    query, packed = lax.optimization_barrier((query, packed))
    query = lax.all_to_all(query, "x", split_axis=0, concat_axis=0, tiled=True)
    count = lax.axis_size(SLAB)
    swaps = [
        [pair for i in range(first, count - 1, 2) for pair in ((i, i + 1), (i + 1, i))]
        for first in (1, 0)
    ]
    odd = lax.ppermute(packed, SLAB, swaps[0])
    even = lax.ppermute(copied(packed), SLAB, swaps[1])
    live = live_rows(key_tiles, rows // TILE)
    attended = attention(query, q_gain, live, odd, packed, even)
    everyone = lax.all_gather(attended, "head", axis=0, tiled=False, axis_index_groups=[ring])
    total = jnp.einsum("hrd,hnd->rn", everyone, projection, preferred_element_type=jnp.float32)
    return total.astype(jnp.bfloat16)


def solution(mesh):
    n_slab, n_head, n_cfg = (mesh.shape[a] for a in ("slab", "head", "cfg"))
    fine = Mesh(
        mesh.devices.reshape(n_slab // 4, 4, n_head, n_cfg), ("z", "x", "head", "cfg")
    )
    placed = (
        P(("cfg",) + SLAB, "head"),
        P(SLAB, "head"),
        P(SLAB, "head"),
        P(SLAB, "head"),
        P("head", SLAB),
        P(),
        P(),
        P("head", SLAB, None),
    )
    return jax.shard_map(
        on_device, mesh=fine, in_specs=placed, out_specs=P(("cfg",) + SLAB, "head"), check_vma=False
    )
```

```python
import jax
import jax.numpy as jnp
from jax import lax
from jax.experimental import pallas as pl
from jax.experimental.pallas import tpu as pltpu
from jax.sharding import Mesh
from jax.sharding import PartitionSpec as P

HDIM = 128
TILE = 64
HEAD = ("y", "core")
SLAB = ("z", "x")
MIB = 1024 * 1024


def whole_block(array):
    rank = len(array.shape)
    return pl.BlockSpec(array.shape, lambda *_: (0,) * rank)


def params(mib):
    return pltpu.CompilerParams(vmem_limit_bytes=mib * MIB)


def normed(total, gain):
    return total * lax.rsqrt(jnp.mean(total * total, axis=-1, keepdims=True) + 1e-06) * gain


def summed(ref, low, high):
    return jnp.sum(ref[:, :, low:high].astype(jnp.float32), axis=0)


def pack_kernel(share_ref, gain_ref, out_ref):
    width = out_ref.shape[1] // 2
    for low in range(0, width, HDIM):
        total = summed(share_ref, low, low + HDIM)
        out_ref[:, low : low + HDIM] = normed(total, gain_ref[...]).astype(jnp.bfloat16)
    out_ref[:, width:] = summed(share_ref, width, 2 * width).astype(jnp.bfloat16)


def pack(share, gain):
    return pl.pallas_call(
        pack_kernel,
        out_shape=jax.ShapeDtypeStruct(share.shape[1:], jnp.bfloat16),
        compiler_params=params(16),
    )(share, gain.reshape(1, HDIM))


def copy_kernel(source_ref, out_ref):
    out_ref[...] = source_ref[...]


def copied(array):
    return pl.pallas_call(
        copy_kernel,
        out_shape=jax.ShapeDtypeStruct(array.shape, array.dtype),
        compiler_params=params(16),
    )(array)


def attention_kernel(share_ref, gain_ref, live_ref, odd_ref, own_ref, even_ref, out_ref):
    rows, width = out_ref.shape[1:]
    near = (odd_ref, own_ref, even_ref)
    scale = 1.0 / HDIM**0.5
    for low in range(0, width, HDIM):
        query = normed(summed(share_ref, low, low + HDIM), gain_ref[...]).astype(jnp.bfloat16)
        keys = jnp.concatenate([r[:, low : low + HDIM] for r in near], axis=0)
        values = jnp.concatenate([r[:, width + low : width + low + HDIM] for r in near], axis=0)
        score = lax.dot_general(
            query, keys, (((1,), (1,)), ((), ())), preferred_element_type=jnp.float32
        )
        allowed = jnp.concatenate(
            [
                jnp.broadcast_to(live_ref[pl.ds(low // HDIM * (rows // TILE) + t, 1), :], (TILE, 3 * rows))
                for t in range(rows // TILE)
            ],
            axis=0,
        )
        weight = jnp.where(allowed > 0, jnp.exp(score * scale), 0.0)
        total = jnp.sum(weight, axis=1, keepdims=True)
        mixed = jnp.dot(weight.astype(jnp.bfloat16), values, preferred_element_type=jnp.float32)
        mixed = (mixed / total).astype(jnp.bfloat16)
        for copy in range(out_ref.shape[0]):
            out_ref[copy, :, low : low + HDIM] = mixed


def attention(copies, query, gain, live, odd, own, even):
    rows, width = query.shape[1:]
    return pl.pallas_call(
        attention_kernel,
        out_shape=jax.ShapeDtypeStruct((copies, rows, width), jnp.bfloat16),
        compiler_params=params(16),
    )(query, gain.reshape(1, HDIM), live, odd, own, even)


def live_rows(key_tiles, tiles_here):
    slab = lax.axis_index(SLAB)
    even_at = jnp.where(slab % 2 == 0, slab + 1, slab - 1)
    slabs = jnp.stack([2 * slab - even_at, slab, even_at])
    near_ids = slabs[:, None] * tiles_here + jnp.arange(tiles_here, dtype=jnp.int32)
    near_ids = near_ids.reshape(-1)
    live = jnp.any(key_tiles[:, :, :, None] == near_ids[None, None, None, :], axis=2)
    live = live.reshape(-1, 3 * tiles_here).astype(jnp.float32)
    return jnp.repeat(live, TILE, axis=1)


def on_device(tokens, q_weight, k_weight, v_weight, out_weight, q_gain, k_gain, key_tiles):
    rows, width = tokens.shape
    n_x, n_z, n_head = (lax.axis_size(a) for a in ("x", "z", HEAD))
    part = width // n_x

    stacked = jnp.concatenate([q_weight, k_weight, v_weight], axis=1)
    weights = lax.all_gather(stacked, "z", axis=0, tiled=True)

    n_core = lax.axis_size("core")
    rank = [h % n_core * (n_head // n_core) + h // n_core for h in range(n_head)]
    turned = [(z * n_head + h, rank[h] * n_z + z) for z in range(n_z) for h in range(n_head)]
    columns = lax.ppermute(out_weight.T, ("z",) + HEAD, turned)

    pieces = tokens.reshape(rows, n_x, part).transpose(1, 0, 2)
    pieces = lax.all_to_all(pieces, "x", split_axis=0, concat_axis=0, tiled=True)
    pieces = lax.all_gather(pieces.reshape(n_x * rows, part), HEAD, axis=0, tiled=False)
    pieces, columns = lax.optimization_barrier((pieces, columns))
    group = pieces.transpose(1, 0, 2).reshape(n_x * rows, n_head * part)

    columns = lax.all_gather(columns, "x", axis=0, tiled=True)
    projection = lax.all_gather(columns, "z", axis=0, tiled=False)
    weights, group, _ = lax.optimization_barrier((weights, group, columns))

    def shares(piece):
        share = jnp.dot(group, piece, preferred_element_type=jnp.float32).astype(jnp.bfloat16)
        return share.reshape(n_x, rows, -1)

    key_value = shares(weights[:, width:])
    key_value = lax.all_to_all(key_value, "x", split_axis=0, concat_axis=0, tiled=True)
    query = shares(weights[:, :width])
    packed = pack(key_value, k_gain)
    query, packed = lax.optimization_barrier((query, packed))
    query = lax.all_to_all(query, "x", split_axis=0, concat_axis=0, tiled=True)
    count = lax.axis_size(SLAB)
    swaps = [
        [pair for i in range(first, count - 1, 2) for pair in ((i, i + 1), (i + 1, i))]
        for first in (1, 0)
    ]
    odd = lax.ppermute(packed, SLAB, swaps[0])
    even = lax.ppermute(copied(packed), SLAB, swaps[1])
    live = live_rows(key_tiles, rows // TILE)
    attended = attention(n_head // n_core, query, q_gain, live, odd, packed, even)
    everyone = lax.all_to_all(attended, "y", split_axis=0, concat_axis=0, tiled=True)
    everyone = lax.all_gather(everyone, "core", axis=0, tiled=True)
    total = jnp.einsum("hrd,hnd->rn", everyone, projection, preferred_element_type=jnp.float32)
    return total.astype(jnp.bfloat16)


def solution(mesh):
    n_slab, n_head, n_cfg = (mesh.shape[a] for a in ("slab", "head", "cfg"))
    fine = Mesh(
        mesh.devices.reshape(n_slab // 4, 4, n_head // 2, 2, n_cfg), ("z", "x", "y", "core", "cfg")
    )
    placed = (
        P(("cfg",) + SLAB, HEAD),
        P(SLAB, HEAD),
        P(SLAB, HEAD),
        P(SLAB, HEAD),
        P(HEAD, SLAB),
        P(),
        P(),
        P(HEAD, SLAB, None),
    )
    return jax.shard_map(
        on_device, mesh=fine, in_specs=placed, out_specs=P(("cfg",) + SLAB, HEAD), check_vma=False
    )
```

```python
import jax
import jax.numpy as jnp
from jax import lax
from jax.experimental import pallas as pl
from jax.experimental.pallas import tpu as pltpu
from jax.sharding import Mesh
from jax.sharding import PartitionSpec as P

HDIM = 128
TILE = 64
HEAD = ("y", "core")
SLAB = ("z", "x")
MIB = 1024 * 1024


def whole_block(array):
    rank = len(array.shape)
    return pl.BlockSpec(array.shape, lambda *_: (0,) * rank)


def params(mib):
    return pltpu.CompilerParams(vmem_limit_bytes=mib * MIB)


def normed(total, gain):
    return total * lax.rsqrt(jnp.mean(total * total, axis=-1, keepdims=True) + 1e-06) * gain


def summed(ref, low, high):
    return jnp.sum(ref[:, :, low:high].astype(jnp.float32), axis=0)


def pack_kernel(share_ref, gain_ref, out_ref):
    width = out_ref.shape[1] // 2
    for low in range(0, width, HDIM):
        total = summed(share_ref, low, low + HDIM)
        out_ref[:, low : low + HDIM] = normed(total, gain_ref[...]).astype(jnp.bfloat16)
    out_ref[:, width:] = summed(share_ref, width, 2 * width).astype(jnp.bfloat16)


def pack(share, gain):
    return pl.pallas_call(
        pack_kernel,
        out_shape=jax.ShapeDtypeStruct(share.shape[1:], jnp.bfloat16),
        compiler_params=params(16),
    )(share, gain.reshape(1, HDIM))


def copy_kernel(source_ref, out_ref):
    out_ref[...] = source_ref[...]


def copied(array):
    return pl.pallas_call(
        copy_kernel,
        out_shape=jax.ShapeDtypeStruct(array.shape, array.dtype),
        compiler_params=params(16),
    )(array)


def attention_kernel(share_ref, gain_ref, live_ref, odd_ref, own_ref, even_ref, out_ref):
    rows, width = out_ref.shape[1:]
    near = (odd_ref, own_ref, even_ref)
    scale = 1.0 / HDIM**0.5
    for low in range(0, width, HDIM):
        query = normed(summed(share_ref, low, low + HDIM), gain_ref[...]).astype(jnp.bfloat16)
        keys = jnp.concatenate([r[:, low : low + HDIM] for r in near], axis=0)
        values = jnp.concatenate([r[:, width + low : width + low + HDIM] for r in near], axis=0)
        score = lax.dot_general(
            query, keys, (((1,), (1,)), ((), ())), preferred_element_type=jnp.float32
        )
        allowed = jnp.concatenate(
            [
                jnp.broadcast_to(live_ref[pl.ds(low // HDIM * (rows // TILE) + t, 1), :], (TILE, 3 * rows))
                for t in range(rows // TILE)
            ],
            axis=0,
        )
        weight = jnp.where(allowed > 0, jnp.exp(score * scale), 0.0)
        total = jnp.sum(weight, axis=1, keepdims=True)
        mixed = jnp.dot(weight.astype(jnp.bfloat16), values, preferred_element_type=jnp.float32)
        mixed = (mixed / total).astype(jnp.bfloat16)
        for copy in range(out_ref.shape[0]):
            out_ref[copy, :, low : low + HDIM] = mixed


def attention(copies, query, gain, live, odd, own, even):
    rows, width = query.shape[1:]
    return pl.pallas_call(
        attention_kernel,
        out_shape=jax.ShapeDtypeStruct((copies, rows, width), jnp.bfloat16),
        compiler_params=params(16),
    )(query, gain.reshape(1, HDIM), live, odd, own, even)


def live_rows(key_tiles, tiles_here):
    slab = lax.axis_index(SLAB)
    even_at = jnp.where(slab % 2 == 0, slab + 1, slab - 1)
    slabs = jnp.stack([2 * slab - even_at, slab, even_at])
    near_ids = slabs[:, None] * tiles_here + jnp.arange(tiles_here, dtype=jnp.int32)
    near_ids = near_ids.reshape(-1)
    live = jnp.any(key_tiles[:, :, :, None] == near_ids[None, None, None, :], axis=2)
    live = live.reshape(-1, 3 * tiles_here).astype(jnp.float32)
    return jnp.repeat(live, TILE, axis=1)


def on_device(tokens, q_weight, k_weight, v_weight, out_weight, q_gain, k_gain, key_tiles):
    rows, width = tokens.shape
    n_x, n_z, n_head = (lax.axis_size(a) for a in ("x", "z", HEAD))
    part = width // n_x

    stacked = jnp.concatenate([q_weight, k_weight, v_weight], axis=1)
    weights = lax.all_gather(stacked, "z", axis=0, tiled=True)

    n_core = lax.axis_size("core")
    rank = [h % n_core * (n_head // n_core) + h // n_core for h in range(n_head)]
    turned = [(z * n_head + h, rank[h] * n_z + z) for z in range(n_z) for h in range(n_head)]
    columns = lax.ppermute(out_weight.T, ("z",) + HEAD, turned)

    pieces = tokens.reshape(rows, n_x, part).transpose(1, 0, 2)
    pieces = lax.all_to_all(pieces, "x", split_axis=0, concat_axis=0, tiled=True)
    pieces = lax.all_gather(pieces.reshape(n_x * rows, part), HEAD, axis=0, tiled=False)
    pieces, columns = lax.optimization_barrier((pieces, columns))
    group = pieces.transpose(1, 0, 2).reshape(n_x * rows, n_head * part)

    columns = lax.all_gather(columns, "x", axis=0, tiled=True)
    projection = lax.all_gather(columns, "z", axis=0, tiled=False)
    weights, group, _ = lax.optimization_barrier((weights, group, columns))

    def shares(piece):
        share = jnp.dot(group, piece, preferred_element_type=jnp.float32).astype(jnp.bfloat16)
        return share.reshape(n_x, rows, -1)

    key_value = shares(weights[:, width:])
    key_value = lax.all_to_all(key_value, "x", split_axis=0, concat_axis=0, tiled=True)
    query = shares(weights[:, :width])
    packed = pack(key_value, k_gain)
    query, packed = lax.optimization_barrier((query, packed))
    query = lax.all_to_all(query, "x", split_axis=0, concat_axis=0, tiled=True)
    count = lax.axis_size(SLAB)
    swaps = [
        [pair for i in range(first, count - 1, 2) for pair in ((i, i + 1), (i + 1, i))]
        for first in (1, 0)
    ]
    odd = lax.ppermute(packed, SLAB, swaps[0])
    even = lax.ppermute(copied(packed), SLAB, swaps[1])
    live = live_rows(key_tiles, rows // TILE)
    attended = attention(n_head // n_core, query, q_gain, live, odd, packed, even)
    everyone = lax.all_to_all(attended, "y", split_axis=0, concat_axis=0, tiled=True)
    everyone, projection = lax.optimization_barrier((everyone, projection))
    everyone = lax.all_gather(everyone, "core", axis=0, tiled=True)
    total = jnp.einsum("hrd,hnd->rn", everyone, projection, preferred_element_type=jnp.float32)
    return total.astype(jnp.bfloat16)


def solution(mesh):
    n_slab, n_head, n_cfg = (mesh.shape[a] for a in ("slab", "head", "cfg"))
    fine = Mesh(
        mesh.devices.reshape(n_slab // 4, 4, n_head // 2, 2, n_cfg), ("z", "x", "y", "core", "cfg")
    )
    placed = (
        P(("cfg",) + SLAB, HEAD),
        P(SLAB, HEAD),
        P(SLAB, HEAD),
        P(SLAB, HEAD),
        P(HEAD, SLAB),
        P(),
        P(),
        P(HEAD, SLAB, None),
    )
    return jax.shard_map(
        on_device, mesh=fine, in_specs=placed, out_specs=P(("cfg",) + SLAB, HEAD), check_vma=False
    )
```

```python
import jax
import jax.numpy as jnp
from jax import lax
from jax.experimental import pallas as pl
from jax.experimental.pallas import tpu as pltpu
from jax.sharding import Mesh
from jax.sharding import PartitionSpec as P

HDIM = 128
TILE = 64
HEAD = ("y", "core")
SLAB = ("z", "x")
MIB = 1024 * 1024


def whole_block(array):
    rank = len(array.shape)
    return pl.BlockSpec(array.shape, lambda *_: (0,) * rank)


def params(mib):
    return pltpu.CompilerParams(vmem_limit_bytes=mib * MIB)


def normed(total, gain):
    return total * lax.rsqrt(jnp.mean(total * total, axis=-1, keepdims=True) + 1e-06) * gain


def summed(ref, low, high):
    return jnp.sum(ref[:, :, low:high].astype(jnp.float32), axis=0)


def pack_kernel(share_ref, gain_ref, out_ref):
    width = out_ref.shape[1] // 2
    for low in range(0, width, HDIM):
        total = summed(share_ref, low, low + HDIM)
        out_ref[:, low : low + HDIM] = normed(total, gain_ref[...]).astype(jnp.bfloat16)
    out_ref[:, width:] = summed(share_ref, width, 2 * width).astype(jnp.bfloat16)


def pack(share, gain):
    return pl.pallas_call(
        pack_kernel,
        out_shape=jax.ShapeDtypeStruct(share.shape[1:], jnp.bfloat16),
        compiler_params=params(16),
    )(share, gain.reshape(1, HDIM))


def copy_kernel(source_ref, out_ref):
    out_ref[...] = source_ref[...]


def copied(array):
    return pl.pallas_call(
        copy_kernel,
        out_shape=jax.ShapeDtypeStruct(array.shape, array.dtype),
        compiler_params=params(16),
    )(array)


def attention_kernel(share_ref, gain_ref, live_ref, odd_ref, own_ref, even_ref, out_ref):
    rows, width = out_ref.shape[1:]
    near = (odd_ref, own_ref, even_ref)
    scale = 1.0 / HDIM**0.5
    for low in range(0, width, HDIM):
        query = normed(summed(share_ref, low, low + HDIM), gain_ref[...]).astype(jnp.bfloat16)
        keys = jnp.concatenate([r[:, low : low + HDIM] for r in near], axis=0)
        values = jnp.concatenate([r[:, width + low : width + low + HDIM] for r in near], axis=0)
        score = lax.dot_general(
            query, keys, (((1,), (1,)), ((), ())), preferred_element_type=jnp.float32
        )
        allowed = jnp.concatenate(
            [
                jnp.broadcast_to(live_ref[pl.ds(low // HDIM * (rows // TILE) + t, 1), :], (TILE, 3 * rows))
                for t in range(rows // TILE)
            ],
            axis=0,
        )
        weight = jnp.where(allowed > 0, jnp.exp(score * scale), 0.0)
        total = jnp.sum(weight, axis=1, keepdims=True)
        mixed = jnp.dot(weight.astype(jnp.bfloat16), values, preferred_element_type=jnp.float32)
        mixed = (mixed / total).astype(jnp.bfloat16)
        for copy in range(out_ref.shape[0]):
            out_ref[copy, :, low : low + HDIM] = mixed


def attention(copies, query, gain, live, odd, own, even):
    rows, width = query.shape[1:]
    return pl.pallas_call(
        attention_kernel,
        out_shape=jax.ShapeDtypeStruct((copies, rows, width), jnp.bfloat16),
        compiler_params=params(16),
    )(query, gain.reshape(1, HDIM), live, odd, own, even)


def live_rows(key_tiles, tiles_here):
    slab = lax.axis_index(SLAB)
    even_at = jnp.where(slab % 2 == 0, slab + 1, slab - 1)
    slabs = jnp.stack([2 * slab - even_at, slab, even_at])
    near_ids = slabs[:, None] * tiles_here + jnp.arange(tiles_here, dtype=jnp.int32)
    near_ids = near_ids.reshape(-1)
    live = jnp.any(key_tiles[:, :, :, None] == near_ids[None, None, None, :], axis=2)
    live = live.reshape(-1, 3 * tiles_here).astype(jnp.float32)
    return jnp.repeat(live, TILE, axis=1)


def on_device(tokens, q_weight, k_weight, v_weight, out_weight, q_gain, k_gain, key_tiles):
    rows, width = tokens.shape
    n_x, n_z, n_head = (lax.axis_size(a) for a in ("x", "z", HEAD))
    part = width // n_x

    stacked = jnp.concatenate([q_weight, k_weight, v_weight], axis=1)
    weights = lax.all_gather(stacked, "z", axis=0, tiled=True)

    n_core = lax.axis_size("core")
    n_y = n_head // n_core

    def place_of(head, column):
        return (head % n_core + column) % n_core * n_y + head // n_core

    turned = [
        (z * n_head + h, place_of(h, z) * n_z + z) for z in range(n_z) for h in range(n_head)
    ]
    columns = lax.ppermute(out_weight.T, ("z",) + HEAD, turned)

    pieces = tokens.reshape(rows, n_x, part).transpose(1, 0, 2)
    pieces = lax.all_to_all(pieces, "x", split_axis=0, concat_axis=0, tiled=True)
    pieces = lax.all_gather(pieces.reshape(n_x * rows, part), HEAD, axis=0, tiled=False)
    pieces, columns = lax.optimization_barrier((pieces, columns))
    group = pieces.transpose(1, 0, 2).reshape(n_x * rows, n_head * part)

    columns = lax.all_gather(columns, "x", axis=0, tiled=True)
    projection = lax.all_gather(columns, "z", axis=0, tiled=False)
    weights, group, _ = lax.optimization_barrier((weights, group, columns))

    def shares(piece):
        share = jnp.dot(group, piece, preferred_element_type=jnp.float32).astype(jnp.bfloat16)
        return share.reshape(n_x, rows, -1)

    key_value = shares(weights[:, width:])
    key_value = lax.all_to_all(key_value, "x", split_axis=0, concat_axis=0, tiled=True)
    query = shares(weights[:, :width])
    packed = pack(key_value, k_gain)
    query, packed = lax.optimization_barrier((query, packed))
    query = lax.all_to_all(query, "x", split_axis=0, concat_axis=0, tiled=True)
    count = lax.axis_size(SLAB)
    swaps = [
        [pair for i in range(first, count - 1, 2) for pair in ((i, i + 1), (i + 1, i))]
        for first in (1, 0)
    ]
    odd = lax.ppermute(packed, SLAB, swaps[0])
    even = lax.ppermute(copied(packed), SLAB, swaps[1])
    live = live_rows(key_tiles, rows // TILE)
    attended = attention(n_y, query, q_gain, live, odd, packed, even)
    mine = lax.all_to_all(attended, "y", split_axis=0, concat_axis=0, tiled=True)
    other = lax.ppermute(mine, "core", [(i, (i + 1) % n_core) for i in range(n_core)])

    def projected(part, rows_of):
        return jnp.einsum("hrd,hnd->rn", part, rows_of, preferred_element_type=jnp.float32)

    total = projected(mine, projection[:n_y]) + projected(other, projection[n_y:])
    return total.astype(jnp.bfloat16)


def solution(mesh):
    n_slab, n_head, n_cfg = (mesh.shape[a] for a in ("slab", "head", "cfg"))
    fine = Mesh(
        mesh.devices.reshape(n_slab // 4, 4, n_head // 2, 2, n_cfg), ("z", "x", "y", "core", "cfg")
    )
    placed = (
        P(("cfg",) + SLAB, HEAD),
        P(SLAB, HEAD),
        P(SLAB, HEAD),
        P(SLAB, HEAD),
        P(HEAD, SLAB),
        P(),
        P(),
        P(HEAD, SLAB, None),
    )
    return jax.shard_map(
        on_device, mesh=fine, in_specs=placed, out_specs=P(("cfg",) + SLAB, HEAD), check_vma=False
    )
```

```python
import jax
import jax.numpy as jnp
from jax import lax
from jax.experimental import pallas as pl
from jax.experimental.pallas import tpu as pltpu
from jax.sharding import Mesh
from jax.sharding import PartitionSpec as P

HDIM = 128
TILE = 64
HEAD = ("y", "core")
SLAB = ("z", "x")
MIB = 1024 * 1024


def whole_block(array):
    rank = len(array.shape)
    return pl.BlockSpec(array.shape, lambda *_: (0,) * rank)


def params(mib):
    return pltpu.CompilerParams(vmem_limit_bytes=mib * MIB)


def normed(total, gain):
    return total * lax.rsqrt(jnp.mean(total * total, axis=-1, keepdims=True) + 1e-06) * gain


def summed(ref, low, high):
    return jnp.sum(ref[:, :, low:high].astype(jnp.float32), axis=0)


def pack_kernel(share_ref, gain_ref, out_ref):
    width = out_ref.shape[1] // 2
    for low in range(0, width, HDIM):
        total = summed(share_ref, low, low + HDIM)
        out_ref[:, low : low + HDIM] = normed(total, gain_ref[...]).astype(jnp.bfloat16)
    out_ref[:, width:] = summed(share_ref, width, 2 * width).astype(jnp.bfloat16)


def pack(share, gain):
    return pl.pallas_call(
        pack_kernel,
        out_shape=jax.ShapeDtypeStruct(share.shape[1:], jnp.bfloat16),
        compiler_params=params(16),
    )(share, gain.reshape(1, HDIM))


def copy_kernel(source_ref, out_ref):
    out_ref[...] = source_ref[...]


def copied(array):
    return pl.pallas_call(
        copy_kernel,
        out_shape=jax.ShapeDtypeStruct(array.shape, array.dtype),
        compiler_params=params(16),
    )(array)


def attention_kernel(share_ref, gain_ref, live_ref, odd_ref, own_ref, even_ref, out_ref):
    rows, width = out_ref.shape[1:]
    near = (odd_ref, own_ref, even_ref)
    scale = 1.0 / HDIM**0.5
    for low in range(0, width, HDIM):
        query = normed(summed(share_ref, low, low + HDIM), gain_ref[...]).astype(jnp.bfloat16)
        keys = jnp.concatenate([r[:, low : low + HDIM] for r in near], axis=0)
        values = jnp.concatenate([r[:, width + low : width + low + HDIM] for r in near], axis=0)
        score = lax.dot_general(
            query, keys, (((1,), (1,)), ((), ())), preferred_element_type=jnp.float32
        )
        allowed = jnp.concatenate(
            [
                jnp.broadcast_to(live_ref[pl.ds(low // HDIM * (rows // TILE) + t, 1), :], (TILE, 3 * rows))
                for t in range(rows // TILE)
            ],
            axis=0,
        )
        weight = jnp.where(allowed > 0, jnp.exp(score * scale), 0.0)
        total = jnp.sum(weight, axis=1, keepdims=True)
        mixed = jnp.dot(weight.astype(jnp.bfloat16), values, preferred_element_type=jnp.float32)
        mixed = (mixed / total).astype(jnp.bfloat16)
        for copy in range(out_ref.shape[0]):
            out_ref[copy, :, low : low + HDIM] = mixed


def attention(copies, query, gain, live, odd, own, even):
    rows, width = query.shape[1:]
    return pl.pallas_call(
        attention_kernel,
        out_shape=jax.ShapeDtypeStruct((copies, rows, width), jnp.bfloat16),
        compiler_params=params(16),
    )(query, gain.reshape(1, HDIM), live, odd, own, even)


def live_rows(key_tiles, tiles_here):
    slab = lax.axis_index(SLAB)
    even_at = jnp.where(slab % 2 == 0, slab + 1, slab - 1)
    slabs = jnp.stack([2 * slab - even_at, slab, even_at])
    near_ids = slabs[:, None] * tiles_here + jnp.arange(tiles_here, dtype=jnp.int32)
    near_ids = near_ids.reshape(-1)
    live = jnp.any(key_tiles[:, :, :, None] == near_ids[None, None, None, :], axis=2)
    live = live.reshape(-1, 3 * tiles_here).astype(jnp.float32)
    return jnp.repeat(live, TILE, axis=1)


def on_device(tokens, q_weight, k_weight, v_weight, out_weight, q_gain, k_gain, key_tiles):
    rows, width = tokens.shape
    n_x, n_z, n_head = (lax.axis_size(a) for a in ("x", "z", HEAD))
    part = width // n_x

    stacked = jnp.concatenate([q_weight, k_weight, v_weight], axis=1)
    weights = lax.all_gather(stacked, "z", axis=0, tiled=True)

    n_core = lax.axis_size("core")
    rank = [h % n_core * (n_head // n_core) + h // n_core for h in range(n_head)]
    turned = [(z * n_head + h, rank[h] * n_z + z) for z in range(n_z) for h in range(n_head)]
    columns = lax.ppermute(out_weight.T, ("z",) + HEAD, turned)

    pieces = tokens.reshape(rows, n_x, part).transpose(1, 0, 2)
    pieces = lax.all_to_all(pieces, "x", split_axis=0, concat_axis=0, tiled=True)
    pieces = lax.all_gather(pieces.reshape(n_x * rows, part), HEAD, axis=0, tiled=False)
    pieces, columns = lax.optimization_barrier((pieces, columns))
    group = pieces.transpose(1, 0, 2).reshape(n_x * rows, n_head * part)

    columns = lax.all_gather(columns, "x", axis=0, tiled=True)
    projection = lax.all_gather(columns, "z", axis=0, tiled=False)
    weights, group, _ = lax.optimization_barrier((weights, group, columns))

    def shares(piece):
        share = jnp.dot(group, piece, preferred_element_type=jnp.float32).astype(jnp.bfloat16)
        return share.reshape(n_x, rows, -1)

    key_value = shares(weights[:, width:])
    key_value = lax.all_to_all(key_value, "x", split_axis=0, concat_axis=0, tiled=True)
    query = shares(weights[:, :width])
    query = lax.all_to_all(query, "x", split_axis=0, concat_axis=0, tiled=True)
    packed = pack(key_value, k_gain)
    count = lax.axis_size(SLAB)
    swaps = [
        [pair for i in range(first, count - 1, 2) for pair in ((i, i + 1), (i + 1, i))]
        for first in (1, 0)
    ]
    odd = lax.ppermute(packed, SLAB, swaps[0])
    even = lax.ppermute(copied(packed), SLAB, swaps[1])
    live = live_rows(key_tiles, rows // TILE)
    attended = attention(n_head // n_core, query, q_gain, live, odd, packed, even)
    everyone = lax.all_to_all(attended, "y", split_axis=0, concat_axis=0, tiled=True)
    everyone = lax.all_gather(everyone, "core", axis=0, tiled=True)
    total = jnp.einsum("hrd,hnd->rn", everyone, projection, preferred_element_type=jnp.float32)
    return total.astype(jnp.bfloat16)


def solution(mesh):
    n_slab, n_head, n_cfg = (mesh.shape[a] for a in ("slab", "head", "cfg"))
    fine = Mesh(
        mesh.devices.reshape(n_slab // 4, 4, n_head // 2, 2, n_cfg), ("z", "x", "y", "core", "cfg")
    )
    placed = (
        P(("cfg",) + SLAB, HEAD),
        P(SLAB, HEAD),
        P(SLAB, HEAD),
        P(SLAB, HEAD),
        P(HEAD, SLAB),
        P(),
        P(),
        P(HEAD, SLAB, None),
    )
    return jax.shard_map(
        on_device, mesh=fine, in_specs=placed, out_specs=P(("cfg",) + SLAB, HEAD), check_vma=False
    )
```

```python
import jax
import jax.numpy as jnp
from jax import lax
from jax.experimental import pallas as pl
from jax.experimental.pallas import tpu as pltpu
from jax.sharding import Mesh
from jax.sharding import PartitionSpec as P

HDIM = 128
TILE = 64
HEAD = ("y", "core")
SLAB = ("z", "x")
MIB = 1024 * 1024


def whole_block(array):
    rank = len(array.shape)
    return pl.BlockSpec(array.shape, lambda *_: (0,) * rank)


def params(mib):
    return pltpu.CompilerParams(vmem_limit_bytes=mib * MIB)


def normed(total, gain):
    return total * lax.rsqrt(jnp.mean(total * total, axis=-1, keepdims=True) + 1e-06) * gain


def summed(ref, low, high):
    return jnp.sum(ref[:, :, low:high].astype(jnp.float32), axis=0)


def pack_kernel(share_ref, gain_ref, out_ref):
    width = out_ref.shape[1] // 2
    for low in range(0, width, HDIM):
        total = summed(share_ref, low, low + HDIM)
        out_ref[:, low : low + HDIM] = normed(total, gain_ref[...]).astype(jnp.bfloat16)
    out_ref[:, width:] = summed(share_ref, width, 2 * width).astype(jnp.bfloat16)


def pack(share, gain):
    return pl.pallas_call(
        pack_kernel,
        out_shape=jax.ShapeDtypeStruct(share.shape[1:], jnp.bfloat16),
        compiler_params=params(16),
    )(share, gain.reshape(1, HDIM))


def copy_kernel(source_ref, out_ref):
    out_ref[...] = source_ref[...]


def copied(array):
    return pl.pallas_call(
        copy_kernel,
        out_shape=jax.ShapeDtypeStruct(array.shape, array.dtype),
        compiler_params=params(16),
    )(array)


def attention_kernel(share_ref, gain_ref, live_ref, odd_ref, own_ref, even_ref, out_ref):
    rows, width = out_ref.shape[1:]
    near = (odd_ref, own_ref, even_ref)
    scale = 1.0 / HDIM**0.5
    for low in range(0, width, HDIM):
        query = normed(summed(share_ref, low, low + HDIM), gain_ref[...]).astype(jnp.bfloat16)
        keys = jnp.concatenate([r[:, low : low + HDIM] for r in near], axis=0)
        values = jnp.concatenate([r[:, width + low : width + low + HDIM] for r in near], axis=0)
        score = lax.dot_general(
            query, keys, (((1,), (1,)), ((), ())), preferred_element_type=jnp.float32
        )
        allowed = jnp.concatenate(
            [
                jnp.broadcast_to(live_ref[pl.ds(low // HDIM * (rows // TILE) + t, 1), :], (TILE, 3 * rows))
                for t in range(rows // TILE)
            ],
            axis=0,
        )
        weight = jnp.where(allowed > 0, jnp.exp(score * scale), 0.0)
        total = jnp.sum(weight, axis=1, keepdims=True)
        mixed = jnp.dot(weight.astype(jnp.bfloat16), values, preferred_element_type=jnp.float32)
        mixed = (mixed / total).astype(jnp.bfloat16)
        for copy in range(out_ref.shape[0]):
            out_ref[copy, :, low : low + HDIM] = mixed


def attention(copies, query, gain, live, odd, own, even):
    rows, width = query.shape[1:]
    return pl.pallas_call(
        attention_kernel,
        out_shape=jax.ShapeDtypeStruct((copies, rows, width), jnp.bfloat16),
        compiler_params=params(16),
    )(query, gain.reshape(1, HDIM), live, odd, own, even)


def live_rows(key_tiles, tiles_here):
    slab = lax.axis_index(SLAB)
    even_at = jnp.where(slab % 2 == 0, slab + 1, slab - 1)
    slabs = jnp.stack([2 * slab - even_at, slab, even_at])
    near_ids = slabs[:, None] * tiles_here + jnp.arange(tiles_here, dtype=jnp.int32)
    near_ids = near_ids.reshape(-1)
    live = jnp.any(key_tiles[:, :, :, None] == near_ids[None, None, None, :], axis=2)
    live = live.reshape(-1, 3 * tiles_here).astype(jnp.float32)
    return jnp.repeat(live, TILE, axis=1)


def on_device(tokens, q_weight, k_weight, v_weight, out_weight, q_gain, k_gain, key_tiles):
    rows, width = tokens.shape
    n_x, n_z, n_head = (lax.axis_size(a) for a in ("x", "z", HEAD))
    part = width // n_x

    stacked = jnp.concatenate([q_weight, k_weight, v_weight], axis=1)
    weights = lax.all_gather(stacked, "z", axis=0, tiled=True)

    n_core = lax.axis_size("core")
    rank = [h % n_core * (n_head // n_core) + h // n_core for h in range(n_head)]
    turned = [(z * n_head + h, rank[h] * n_z + z) for z in range(n_z) for h in range(n_head)]
    columns = lax.ppermute(out_weight.T, ("z",) + HEAD, turned)

    pieces = tokens.reshape(rows, n_x, part).transpose(1, 0, 2)
    pieces = lax.all_to_all(pieces, "x", split_axis=0, concat_axis=0, tiled=True)
    pieces = lax.all_gather(pieces.reshape(n_x * rows, part), HEAD, axis=0, tiled=False)
    pieces, columns = lax.optimization_barrier((pieces, columns))
    group = pieces.transpose(1, 0, 2).reshape(n_x * rows, n_head * part)

    columns = lax.all_gather(columns, "x", axis=0, tiled=True)
    projection = lax.all_gather(columns, "z", axis=0, tiled=False)
    weights, group, _ = lax.optimization_barrier((weights, group, columns))

    def shares(piece):
        share = jnp.dot(group, piece, preferred_element_type=jnp.float32).astype(jnp.bfloat16)
        return share.reshape(n_x, rows, -1)

    key_value = shares(weights[:, width:])
    key_value = lax.all_to_all(key_value, "x", split_axis=0, concat_axis=0, tiled=True)
    query = shares(weights[:, :width])
    packed = pack(key_value, k_gain)
    query, packed = lax.optimization_barrier((query, packed))
    query = lax.all_to_all(query, "x", split_axis=0, concat_axis=0, tiled=True)
    count = lax.axis_size(SLAB)
    swaps = [
        [pair for i in range(first, count - 1, 2) for pair in ((i, i + 1), (i + 1, i))]
        for first in (1, 0)
    ]
    odd = lax.ppermute(packed, SLAB, swaps[0])
    even = lax.ppermute(copied(packed), SLAB, swaps[1])
    live = live_rows(key_tiles, rows // TILE)
    attended = attention(1, query, q_gain, live, odd, packed, even)
    everyone = lax.all_gather(attended, "y", axis=0, tiled=True)
    everyone = lax.all_gather(everyone, "core", axis=0, tiled=True)
    total = jnp.einsum("hrd,hnd->rn", everyone, projection, preferred_element_type=jnp.float32)
    return total.astype(jnp.bfloat16)


def solution(mesh):
    n_slab, n_head, n_cfg = (mesh.shape[a] for a in ("slab", "head", "cfg"))
    fine = Mesh(
        mesh.devices.reshape(n_slab // 4, 4, n_head // 2, 2, n_cfg), ("z", "x", "y", "core", "cfg")
    )
    placed = (
        P(("cfg",) + SLAB, HEAD),
        P(SLAB, HEAD),
        P(SLAB, HEAD),
        P(SLAB, HEAD),
        P(HEAD, SLAB),
        P(),
        P(),
        P(HEAD, SLAB, None),
    )
    return jax.shard_map(
        on_device, mesh=fine, in_specs=placed, out_specs=P(("cfg",) + SLAB, HEAD), check_vma=False
    )
```

```python
import jax
import jax.numpy as jnp
from jax import lax
from jax.experimental import pallas as pl
from jax.experimental.pallas import tpu as pltpu
from jax.sharding import Mesh
from jax.sharding import PartitionSpec as P

HDIM = 128
TILE = 64
HEAD = ("y", "core")
SLAB = ("z", "x")
MIB = 1024 * 1024


def whole_block(array):
    rank = len(array.shape)
    return pl.BlockSpec(array.shape, lambda *_: (0,) * rank)


def params(mib):
    return pltpu.CompilerParams(vmem_limit_bytes=mib * MIB)


def normed(total, gain):
    return total * lax.rsqrt(jnp.mean(total * total, axis=-1, keepdims=True) + 1e-06) * gain


def summed(ref, low, high):
    return jnp.sum(ref[:, :, low:high].astype(jnp.float32), axis=0)


def pack_kernel(share_ref, gain_ref, out_ref):
    width = out_ref.shape[1] // 2
    for low in range(0, width, HDIM):
        total = summed(share_ref, low, low + HDIM)
        out_ref[:, low : low + HDIM] = normed(total, gain_ref[...]).astype(jnp.bfloat16)
    out_ref[:, width:] = summed(share_ref, width, 2 * width).astype(jnp.bfloat16)


def pack(share, gain):
    return pl.pallas_call(
        pack_kernel,
        out_shape=jax.ShapeDtypeStruct(share.shape[1:], jnp.bfloat16),
        compiler_params=params(16),
    )(share, gain.reshape(1, HDIM))


def turn_kernel(source_ref, out_ref):
    out_ref[...] = source_ref[...].T


def turned_over(array):
    return pl.pallas_call(
        turn_kernel,
        out_shape=jax.ShapeDtypeStruct(array.shape[::-1], array.dtype),
        compiler_params=params(16),
    )(array)


def query_kernel(share_ref, gain_ref, out_ref):
    for low in range(0, out_ref.shape[1], HDIM):
        total = summed(share_ref, low, low + HDIM)
        out_ref[:, low : low + HDIM] = normed(total, gain_ref[...]).astype(jnp.bfloat16)


def normed_query(share, gain):
    return pl.pallas_call(
        query_kernel,
        out_shape=jax.ShapeDtypeStruct(share.shape[1:], jnp.bfloat16),
        compiler_params=params(16),
    )(share, gain.reshape(1, HDIM))


def copy_kernel(source_ref, out_ref):
    out_ref[...] = source_ref[...]


def copied(array):
    return pl.pallas_call(
        copy_kernel,
        out_shape=jax.ShapeDtypeStruct(array.shape, array.dtype),
        compiler_params=params(16),
    )(array)


def attention_kernel(query_ref, live_ref, odd_ref, own_ref, even_ref, out_ref):
    rows, width = out_ref.shape[1:]
    near = (odd_ref, own_ref, even_ref)
    scale = 1.0 / HDIM**0.5
    for low in range(0, width, HDIM):
        query = query_ref[:, low : low + HDIM]
        keys = jnp.concatenate([r[:, low : low + HDIM] for r in near], axis=0)
        values = jnp.concatenate([r[:, width + low : width + low + HDIM] for r in near], axis=0)
        score = lax.dot_general(
            query, keys, (((1,), (1,)), ((), ())), preferred_element_type=jnp.float32
        )
        allowed = jnp.concatenate(
            [
                jnp.broadcast_to(live_ref[pl.ds(low // HDIM * (rows // TILE) + t, 1), :], (TILE, 3 * rows))
                for t in range(rows // TILE)
            ],
            axis=0,
        )
        weight = jnp.where(allowed > 0, jnp.exp(score * scale), 0.0)
        total = jnp.sum(weight, axis=1, keepdims=True)
        mixed = jnp.dot(weight.astype(jnp.bfloat16), values, preferred_element_type=jnp.float32)
        mixed = (mixed / total).astype(jnp.bfloat16)
        for copy in range(out_ref.shape[0]):
            out_ref[copy, :, low : low + HDIM] = mixed


def attention(copies, query, live, odd, own, even):
    rows, width = query.shape
    return pl.pallas_call(
        attention_kernel,
        out_shape=jax.ShapeDtypeStruct((copies, rows, width), jnp.bfloat16),
        compiler_params=params(16),
    )(query, live, odd, own, even)


def live_rows(key_tiles, tiles_here):
    slab = lax.axis_index(SLAB)
    even_at = jnp.where(slab % 2 == 0, slab + 1, slab - 1)
    slabs = jnp.stack([2 * slab - even_at, slab, even_at])
    near_ids = slabs[:, None] * tiles_here + jnp.arange(tiles_here, dtype=jnp.int32)
    near_ids = near_ids.reshape(-1)
    live = jnp.any(key_tiles[:, :, :, None] == near_ids[None, None, None, :], axis=2)
    live = live.reshape(-1, 3 * tiles_here).astype(jnp.float32)
    return jnp.repeat(live, TILE, axis=1)


def on_device(tokens, q_weight, k_weight, v_weight, out_weight, q_gain, k_gain, key_tiles):
    rows, width = tokens.shape
    n_x, n_z, n_head = (lax.axis_size(a) for a in ("x", "z", HEAD))
    part = width // n_x

    stacked = jnp.concatenate([q_weight, k_weight, v_weight], axis=1)
    weights = lax.all_gather(stacked, "z", axis=0, tiled=True)

    n_core = lax.axis_size("core")
    rank = [h % n_core * (n_head // n_core) + h // n_core for h in range(n_head)]
    turned = [(z * n_head + h, rank[h] * n_z + z) for z in range(n_z) for h in range(n_head)]
    columns = lax.ppermute(out_weight.T, ("z",) + HEAD, turned)

    pieces = tokens.reshape(rows, n_x, part).transpose(1, 0, 2)
    pieces = lax.all_to_all(pieces, "x", split_axis=0, concat_axis=0, tiled=True)
    pieces = lax.all_gather(pieces.reshape(n_x * rows, part), HEAD, axis=0, tiled=False)
    pieces, columns = lax.optimization_barrier((pieces, columns))
    group = pieces.transpose(1, 0, 2).reshape(n_x * rows, n_head * part)

    columns = turned_over(lax.all_gather(columns, "x", axis=0, tiled=True))
    projection = lax.all_gather(columns, "z", axis=0, tiled=False)
    weights, group, _ = lax.optimization_barrier((weights, group, columns))

    def shares(piece):
        share = jnp.dot(group, piece, preferred_element_type=jnp.float32).astype(jnp.bfloat16)
        return share.reshape(n_x, rows, -1)

    key_value = shares(weights[:, width:])
    key_value = lax.all_to_all(key_value, "x", split_axis=0, concat_axis=0, tiled=True)
    query = shares(weights[:, :width])
    packed = pack(key_value, k_gain)
    query, packed = lax.optimization_barrier((query, packed))
    query = lax.all_to_all(query, "x", split_axis=0, concat_axis=0, tiled=True)
    count = lax.axis_size(SLAB)
    swaps = [
        [pair for i in range(first, count - 1, 2) for pair in ((i, i + 1), (i + 1, i))]
        for first in (1, 0)
    ]
    odd = lax.ppermute(packed, SLAB, swaps[0])
    even = lax.ppermute(copied(packed), SLAB, swaps[1])
    live = live_rows(key_tiles, rows // TILE)
    attended = attention(n_head // n_core, normed_query(query, q_gain), live, odd, packed, even)
    everyone = lax.all_to_all(attended, "y", split_axis=0, concat_axis=0, tiled=True)
    everyone = lax.all_gather(everyone, "core", axis=0, tiled=True)
    total = jnp.einsum("hrd,hdn->rn", everyone, projection, preferred_element_type=jnp.float32)
    return total.astype(jnp.bfloat16)


def solution(mesh):
    n_slab, n_head, n_cfg = (mesh.shape[a] for a in ("slab", "head", "cfg"))
    fine = Mesh(
        mesh.devices.reshape(n_slab // 4, 4, n_head // 2, 2, n_cfg), ("z", "x", "y", "core", "cfg")
    )
    placed = (
        P(("cfg",) + SLAB, HEAD),
        P(SLAB, HEAD),
        P(SLAB, HEAD),
        P(SLAB, HEAD),
        P(HEAD, SLAB),
        P(),
        P(),
        P(HEAD, SLAB, None),
    )
    return jax.shard_map(
        on_device, mesh=fine, in_specs=placed, out_specs=P(("cfg",) + SLAB, HEAD), check_vma=False
    )
```

```python
import jax
import jax.numpy as jnp
from jax import lax
from jax.experimental import pallas as pl
from jax.experimental.pallas import tpu as pltpu
from jax.sharding import Mesh
from jax.sharding import PartitionSpec as P

HDIM = 128
TILE = 64
HEAD = ("y", "core")
SLAB = ("z", "x")
MIB = 1024 * 1024


def whole_block(array):
    rank = len(array.shape)
    return pl.BlockSpec(array.shape, lambda *_: (0,) * rank)


def params(mib):
    return pltpu.CompilerParams(vmem_limit_bytes=mib * MIB)


def normed(total, gain):
    return total * lax.rsqrt(jnp.mean(total * total, axis=-1, keepdims=True) + 1e-06) * gain


def summed(ref, low, high):
    return jnp.sum(ref[:, :, low:high].astype(jnp.float32), axis=0)


def pack_kernel(share_ref, gain_ref, out_ref):
    width = out_ref.shape[1] // 2
    for low in range(0, width, HDIM):
        total = summed(share_ref, low, low + HDIM)
        out_ref[:, low : low + HDIM] = normed(total, gain_ref[...]).astype(jnp.bfloat16)
    out_ref[:, width:] = summed(share_ref, width, 2 * width).astype(jnp.bfloat16)


def pack(share, gain):
    return pl.pallas_call(
        pack_kernel,
        out_shape=jax.ShapeDtypeStruct(share.shape[1:], jnp.bfloat16),
        compiler_params=params(16),
    )(share, gain.reshape(1, HDIM))


def turn_kernel(source_ref, out_ref):
    out_ref[...] = source_ref[...].T


def turned_over(array):
    return pl.pallas_call(
        turn_kernel,
        out_shape=jax.ShapeDtypeStruct(array.shape[::-1], array.dtype),
        compiler_params=params(16),
    )(array)


def query_kernel(share_ref, gain_ref, out_ref):
    for low in range(0, out_ref.shape[1], HDIM):
        total = summed(share_ref, low, low + HDIM)
        out_ref[:, low : low + HDIM] = normed(total, gain_ref[...]).astype(jnp.bfloat16)


def normed_query(share, gain):
    return pl.pallas_call(
        query_kernel,
        out_shape=jax.ShapeDtypeStruct(share.shape[1:], jnp.bfloat16),
        compiler_params=params(16),
    )(share, gain.reshape(1, HDIM))


def copy_kernel(source_ref, out_ref):
    out_ref[...] = source_ref[...]


def copied(array):
    return pl.pallas_call(
        copy_kernel,
        out_shape=jax.ShapeDtypeStruct(array.shape, array.dtype),
        compiler_params=params(16),
    )(array)


def attention_kernel(query_ref, live_ref, odd_ref, own_ref, even_ref, out_ref):
    rows, width = out_ref.shape[1:]
    near = (odd_ref, own_ref, even_ref)
    tiles = rows // TILE
    scale = 1.0 / HDIM**0.5
    lows = range(0, width, HDIM)

    def weight_of(low, place):
        score = lax.dot_general(
            query_ref[:, low : low + HDIM],
            near[place][:, low : low + HDIM],
            (((1,), (1,)), ((), ())),
            preferred_element_type=jnp.float32,
        )
        allowed = [
            jnp.broadcast_to(
                live_ref[pl.ds(low // HDIM * tiles + t, 1), place * rows : (place + 1) * rows],
                (TILE, rows),
            )
            for t in range(tiles)
        ]
        return jnp.where(jnp.concatenate(allowed, axis=0) > 0, jnp.exp(score * scale), 0.0)

    weights = [[weight_of(low, place) for place in range(len(near))] for low in lows]
    for low, each in zip(lows, weights):
        total = jnp.sum(sum(each), axis=1, keepdims=True)
        mixed = sum(
            jnp.dot(
                weight.astype(jnp.bfloat16),
                ref[:, width + low : width + low + HDIM],
                preferred_element_type=jnp.float32,
            )
            for weight, ref in zip(each, near)
        )
        mixed = (mixed / total).astype(jnp.bfloat16)
        for copy in range(out_ref.shape[0]):
            out_ref[copy, :, low : low + HDIM] = mixed


def attention(copies, query, live, odd, own, even):
    rows, width = query.shape
    return pl.pallas_call(
        attention_kernel,
        out_shape=jax.ShapeDtypeStruct((copies, rows, width), jnp.bfloat16),
        compiler_params=params(16),
    )(query, live, odd, own, even)


def live_rows(key_tiles, tiles_here):
    slab = lax.axis_index(SLAB)
    even_at = jnp.where(slab % 2 == 0, slab + 1, slab - 1)
    slabs = jnp.stack([2 * slab - even_at, slab, even_at])
    near_ids = slabs[:, None] * tiles_here + jnp.arange(tiles_here, dtype=jnp.int32)
    near_ids = near_ids.reshape(-1)
    live = jnp.any(key_tiles[:, :, :, None] == near_ids[None, None, None, :], axis=2)
    live = live.reshape(-1, 3 * tiles_here).astype(jnp.float32)
    return jnp.repeat(live, TILE, axis=1)


def on_device(tokens, q_weight, k_weight, v_weight, out_weight, q_gain, k_gain, key_tiles):
    rows, width = tokens.shape
    n_x, n_z, n_head = (lax.axis_size(a) for a in ("x", "z", HEAD))
    part = width // n_x

    stacked = jnp.concatenate([q_weight, k_weight, v_weight], axis=1)
    weights = lax.all_gather(stacked, "z", axis=0, tiled=True)

    n_core = lax.axis_size("core")
    rank = [h % n_core * (n_head // n_core) + h // n_core for h in range(n_head)]
    turned = [(z * n_head + h, rank[h] * n_z + z) for z in range(n_z) for h in range(n_head)]
    columns = lax.ppermute(out_weight.T, ("z",) + HEAD, turned)

    pieces = tokens.reshape(rows, n_x, part).transpose(1, 0, 2)
    pieces = lax.all_to_all(pieces, "x", split_axis=0, concat_axis=0, tiled=True)
    pieces = lax.all_gather(pieces.reshape(n_x * rows, part), HEAD, axis=0, tiled=False)
    pieces, columns = lax.optimization_barrier((pieces, columns))
    group = pieces.transpose(1, 0, 2).reshape(n_x * rows, n_head * part)

    columns = turned_over(lax.all_gather(columns, "x", axis=0, tiled=True))
    projection = lax.all_gather(columns, "z", axis=0, tiled=False)
    weights, group, _ = lax.optimization_barrier((weights, group, columns))

    def shares(piece):
        share = jnp.dot(group, piece, preferred_element_type=jnp.float32).astype(jnp.bfloat16)
        return share.reshape(n_x, rows, -1)

    key_value = shares(weights[:, width:])
    key_value = lax.all_to_all(key_value, "x", split_axis=0, concat_axis=0, tiled=True)
    query = shares(weights[:, :width])
    packed = pack(key_value, k_gain)
    query, packed = lax.optimization_barrier((query, packed))
    query = lax.all_to_all(query, "x", split_axis=0, concat_axis=0, tiled=True)
    count = lax.axis_size(SLAB)
    swaps = [
        [pair for i in range(first, count - 1, 2) for pair in ((i, i + 1), (i + 1, i))]
        for first in (1, 0)
    ]
    odd = lax.ppermute(packed, SLAB, swaps[0])
    even = lax.ppermute(copied(packed), SLAB, swaps[1])
    live = live_rows(key_tiles, rows // TILE)
    attended = attention(n_head // n_core, normed_query(query, q_gain), live, odd, packed, even)
    everyone = lax.all_to_all(attended, "y", split_axis=0, concat_axis=0, tiled=True)
    everyone = lax.all_gather(everyone, "core", axis=0, tiled=True)
    total = jnp.einsum("hrd,hdn->rn", everyone, projection, preferred_element_type=jnp.float32)
    return total.astype(jnp.bfloat16)


def solution(mesh):
    n_slab, n_head, n_cfg = (mesh.shape[a] for a in ("slab", "head", "cfg"))
    fine = Mesh(
        mesh.devices.reshape(n_slab // 4, 4, n_head // 2, 2, n_cfg), ("z", "x", "y", "core", "cfg")
    )
    placed = (
        P(("cfg",) + SLAB, HEAD),
        P(SLAB, HEAD),
        P(SLAB, HEAD),
        P(SLAB, HEAD),
        P(HEAD, SLAB),
        P(),
        P(),
        P(HEAD, SLAB, None),
    )
    return jax.shard_map(
        on_device, mesh=fine, in_specs=placed, out_specs=P(("cfg",) + SLAB, HEAD), check_vma=False
    )
```

```python
import jax
import jax.numpy as jnp
from jax import lax
from jax.experimental import pallas as pl
from jax.experimental.pallas import tpu as pltpu
from jax.sharding import Mesh
from jax.sharding import PartitionSpec as P

HDIM = 128
TILE = 64
HEAD = ("y", "core")
SLAB = ("z", "x")
MIB = 1024 * 1024


def whole_block(array):
    rank = len(array.shape)
    return pl.BlockSpec(array.shape, lambda *_: (0,) * rank)


def params(mib):
    return pltpu.CompilerParams(vmem_limit_bytes=mib * MIB)


def normed(total, gain):
    return total * lax.rsqrt(jnp.mean(total * total, axis=-1, keepdims=True) + 1e-06) * gain


def summed(ref, low, high):
    return jnp.sum(ref[:, :, low:high].astype(jnp.float32), axis=0)


def pack_kernel(share_ref, gain_ref, out_ref):
    width = out_ref.shape[1] // 2
    for low in range(0, width, HDIM):
        total = summed(share_ref, low, low + HDIM)
        out_ref[:, low : low + HDIM] = normed(total, gain_ref[...]).astype(jnp.bfloat16)
    out_ref[:, width:] = summed(share_ref, width, 2 * width).astype(jnp.bfloat16)


def pack(share, gain):
    return pl.pallas_call(
        pack_kernel,
        out_shape=jax.ShapeDtypeStruct(share.shape[1:], jnp.bfloat16),
        compiler_params=params(16),
    )(share, gain.reshape(1, HDIM))


def turn_kernel(source_ref, out_ref):
    out_ref[...] = source_ref[...].T


def turned_over(array):
    return pl.pallas_call(
        turn_kernel,
        out_shape=jax.ShapeDtypeStruct(array.shape[::-1], array.dtype),
        compiler_params=params(16),
    )(array)


def query_kernel(share_ref, gain_ref, out_ref):
    for low in range(0, out_ref.shape[1], HDIM):
        total = summed(share_ref, low, low + HDIM)
        out_ref[:, low : low + HDIM] = normed(total, gain_ref[...]).astype(jnp.bfloat16)


def normed_query(share, gain):
    return pl.pallas_call(
        query_kernel,
        out_shape=jax.ShapeDtypeStruct(share.shape[1:], jnp.bfloat16),
        compiler_params=params(16),
    )(share, gain.reshape(1, HDIM))


def copy_kernel(source_ref, out_ref):
    out_ref[...] = source_ref[...]


def copied(array):
    return pl.pallas_call(
        copy_kernel,
        out_shape=jax.ShapeDtypeStruct(array.shape, array.dtype),
        compiler_params=params(16),
    )(array)


def attention_kernel(query_ref, live_ref, odd_ref, own_ref, even_ref, out_ref):
    rows, width = out_ref.shape[1:]
    near = (odd_ref, own_ref, even_ref)
    tiles = rows // TILE
    scale = 1.0 / HDIM**0.5
    lows = range(0, width, HDIM)

    def weight_of(low, place):
        score = lax.dot_general(
            query_ref[:, low : low + HDIM],
            near[place][:, low : low + HDIM],
            (((1,), (1,)), ((), ())),
            preferred_element_type=jnp.float32,
        )
        allowed = [
            jnp.broadcast_to(
                live_ref[pl.ds(low // HDIM * tiles + t, 1), place * rows : (place + 1) * rows],
                (TILE, rows),
            )
            for t in range(tiles)
        ]
        return jnp.where(jnp.concatenate(allowed, axis=0) > 0, jnp.exp(score * scale), 0.0)

    weights = [[weight_of(low, place) for place in range(len(near))] for low in lows]
    for low, each in zip(lows, weights):
        total = jnp.sum(sum(each), axis=1, keepdims=True)
        mixed = sum(
            jnp.dot(
                weight.astype(jnp.bfloat16),
                ref[:, width + low : width + low + HDIM],
                preferred_element_type=jnp.float32,
            )
            for weight, ref in zip(each, near)
        )
        mixed = (mixed / total).astype(jnp.bfloat16)
        for copy in range(out_ref.shape[0]):
            out_ref[copy, :, low : low + HDIM] = mixed


def attention(copies, query, live, odd, own, even):
    rows, width = query.shape
    return pl.pallas_call(
        attention_kernel,
        out_shape=jax.ShapeDtypeStruct((copies, rows, width), jnp.bfloat16),
        compiler_params=params(16),
    )(query, live, odd, own, even)


def live_rows(key_tiles, tiles_here):
    slab = lax.axis_index(SLAB)
    even_at = jnp.where(slab % 2 == 0, slab + 1, slab - 1)
    slabs = jnp.stack([2 * slab - even_at, slab, even_at])
    near_ids = slabs[:, None] * tiles_here + jnp.arange(tiles_here, dtype=jnp.int32)
    near_ids = near_ids.reshape(-1)
    live = jnp.any(key_tiles[:, :, :, None] == near_ids[None, None, None, :], axis=2)
    live = live.reshape(-1, 3 * tiles_here).astype(jnp.float32)
    return jnp.repeat(live, TILE, axis=1)


def on_device(tokens, q_weight, k_weight, v_weight, out_weight, q_gain, k_gain, key_tiles):
    rows, width = tokens.shape
    n_x, n_z, n_head = (lax.axis_size(a) for a in ("x", "z", HEAD))
    part = width // n_x

    stacked = jnp.concatenate([q_weight, k_weight, v_weight], axis=1)
    weights = lax.all_gather(stacked, "z", axis=0, tiled=True)

    n_core = lax.axis_size("core")
    rank = [h % n_core * (n_head // n_core) + h // n_core for h in range(n_head)]
    turned = [(z * n_head + h, rank[h] * n_z + z) for z in range(n_z) for h in range(n_head)]
    columns = lax.ppermute(out_weight.T, ("z",) + HEAD, turned)

    pieces = tokens.reshape(rows, n_x, part).transpose(1, 0, 2)
    pieces = lax.all_to_all(pieces, "x", split_axis=0, concat_axis=0, tiled=True)
    pieces = lax.all_gather(pieces.reshape(n_x * rows, part), HEAD, axis=0, tiled=False)
    pieces, columns = lax.optimization_barrier((pieces, columns))
    group = pieces.transpose(1, 0, 2).reshape(n_x * rows, n_head * part)

    columns = turned_over(lax.all_gather(columns, "x", axis=0, tiled=True))
    projection = lax.all_gather(columns, "z", axis=0, tiled=False)
    weights, group, _ = lax.optimization_barrier((weights, group, columns))

    def shares(piece):
        share = jnp.dot(group, piece, preferred_element_type=jnp.float32).astype(jnp.bfloat16)
        return share.reshape(n_x, rows, -1)

    both = shares(weights)
    query, key_value = lax.optimization_barrier((both[:, :, :width], both[:, :, width:]))
    key_value = lax.all_to_all(key_value, "x", split_axis=0, concat_axis=0, tiled=True)
    packed = pack(key_value, k_gain)
    query, packed = lax.optimization_barrier((query, packed))
    query = lax.all_to_all(query, "x", split_axis=0, concat_axis=0, tiled=True)
    count = lax.axis_size(SLAB)
    swaps = [
        [pair for i in range(first, count - 1, 2) for pair in ((i, i + 1), (i + 1, i))]
        for first in (1, 0)
    ]
    odd = lax.ppermute(packed, SLAB, swaps[0])
    even = lax.ppermute(copied(packed), SLAB, swaps[1])
    live = live_rows(key_tiles, rows // TILE)
    attended = attention(n_head // n_core, normed_query(query, q_gain), live, odd, packed, even)
    everyone = lax.all_to_all(attended, "y", split_axis=0, concat_axis=0, tiled=True)
    everyone = lax.all_gather(everyone, "core", axis=0, tiled=True)
    total = jnp.einsum("hrd,hdn->rn", everyone, projection, preferred_element_type=jnp.float32)
    return total.astype(jnp.bfloat16)


def solution(mesh):
    n_slab, n_head, n_cfg = (mesh.shape[a] for a in ("slab", "head", "cfg"))
    fine = Mesh(
        mesh.devices.reshape(n_slab // 4, 4, n_head // 2, 2, n_cfg), ("z", "x", "y", "core", "cfg")
    )
    placed = (
        P(("cfg",) + SLAB, HEAD),
        P(SLAB, HEAD),
        P(SLAB, HEAD),
        P(SLAB, HEAD),
        P(HEAD, SLAB),
        P(),
        P(),
        P(HEAD, SLAB, None),
    )
    return jax.shard_map(
        on_device, mesh=fine, in_specs=placed, out_specs=P(("cfg",) + SLAB, HEAD), check_vma=False
    )
```

```python
import jax
import jax.numpy as jnp
from jax import lax
from jax.experimental import pallas as pl
from jax.experimental.pallas import tpu as pltpu
from jax.sharding import Mesh
from jax.sharding import PartitionSpec as P

HDIM = 128
TILE = 64
HEAD = ("y", "core")
SLAB = ("z", "x")
MIB = 1024 * 1024


def whole_block(array):
    rank = len(array.shape)
    return pl.BlockSpec(array.shape, lambda *_: (0,) * rank)


def params(mib):
    return pltpu.CompilerParams(vmem_limit_bytes=mib * MIB)


def normed(total, gain):
    return total * lax.rsqrt(jnp.mean(total * total, axis=-1, keepdims=True) + 1e-06) * gain


def summed(ref, low, high):
    return jnp.sum(ref[:, :, low:high].astype(jnp.float32), axis=0)


def pack_kernel(share_ref, gain_ref, out_ref):
    width = out_ref.shape[1] // 2
    for low in range(0, width, HDIM):
        total = summed(share_ref, low, low + HDIM)
        out_ref[:, low : low + HDIM] = normed(total, gain_ref[...]).astype(jnp.bfloat16)
    out_ref[:, width:] = summed(share_ref, width, 2 * width).astype(jnp.bfloat16)


def pack(share, gain):
    return pl.pallas_call(
        pack_kernel,
        out_shape=jax.ShapeDtypeStruct(share.shape[1:], jnp.bfloat16),
        compiler_params=params(16),
    )(share, gain.reshape(1, HDIM))


def turn_kernel(source_ref, out_ref):
    out_ref[...] = source_ref[...].T


def turned_over(array):
    return pl.pallas_call(
        turn_kernel,
        out_shape=jax.ShapeDtypeStruct(array.shape[::-1], array.dtype),
        compiler_params=params(16),
    )(array)


def query_kernel(share_ref, gain_ref, out_ref):
    for low in range(0, out_ref.shape[1], HDIM):
        total = summed(share_ref, low, low + HDIM)
        out_ref[:, low : low + HDIM] = normed(total, gain_ref[...]).astype(jnp.bfloat16)


def normed_query(share, gain):
    return pl.pallas_call(
        query_kernel,
        out_shape=jax.ShapeDtypeStruct(share.shape[1:], jnp.bfloat16),
        compiler_params=params(16),
    )(share, gain.reshape(1, HDIM))


def copy_kernel(source_ref, out_ref):
    out_ref[...] = source_ref[...]


def copied(array):
    return pl.pallas_call(
        copy_kernel,
        out_shape=jax.ShapeDtypeStruct(array.shape, array.dtype),
        compiler_params=params(16),
    )(array)


def attention_kernel(query_ref, live_ref, odd_ref, own_ref, even_ref, out_ref):
    rows, width = out_ref.shape[1:]
    near = (odd_ref, own_ref, even_ref)
    tiles = rows // TILE
    scale = 1.0 / HDIM**0.5
    lows = range(0, width, HDIM)

    def weight_of(low, place):
        score = lax.dot_general(
            query_ref[:, low : low + HDIM],
            near[place][:, low : low + HDIM],
            (((1,), (1,)), ((), ())),
            preferred_element_type=jnp.float32,
        )
        allowed = [
            jnp.broadcast_to(
                live_ref[pl.ds(low // HDIM * tiles + t, 1), place * rows : (place + 1) * rows],
                (TILE, rows),
            )
            for t in range(tiles)
        ]
        return jnp.where(jnp.concatenate(allowed, axis=0) > 0, jnp.exp(score * scale), 0.0)

    weights = [[weight_of(low, place) for place in range(len(near))] for low in lows]
    for low, each in zip(lows, weights):
        total = jnp.sum(sum(each), axis=1, keepdims=True)
        mixed = sum(
            jnp.dot(
                weight.astype(jnp.bfloat16),
                ref[:, width + low : width + low + HDIM],
                preferred_element_type=jnp.float32,
            )
            for weight, ref in zip(each, near)
        )
        mixed = (mixed / total).astype(jnp.bfloat16)
        for copy in range(out_ref.shape[0]):
            out_ref[copy, :, low : low + HDIM] = mixed


def attention(copies, query, live, odd, own, even):
    rows, width = query.shape
    return pl.pallas_call(
        attention_kernel,
        out_shape=jax.ShapeDtypeStruct((copies, rows, width), jnp.bfloat16),
        compiler_params=params(16),
    )(query, live, odd, own, even)


def live_rows(key_tiles, tiles_here):
    slab = lax.axis_index(SLAB)
    even_at = jnp.where(slab % 2 == 0, slab + 1, slab - 1)
    slabs = jnp.stack([2 * slab - even_at, slab, even_at])
    near_ids = slabs[:, None] * tiles_here + jnp.arange(tiles_here, dtype=jnp.int32)
    near_ids = near_ids.reshape(-1)
    live = jnp.any(key_tiles[:, :, :, None] == near_ids[None, None, None, :], axis=2)
    live = live.reshape(-1, 3 * tiles_here).astype(jnp.float32)
    return jnp.repeat(live, TILE, axis=1)


def on_device(tokens, q_weight, k_weight, v_weight, out_weight, q_gain, k_gain, key_tiles):
    rows, width = tokens.shape
    n_x, n_z, n_head = (lax.axis_size(a) for a in ("x", "z", HEAD))
    part = width // n_x

    stacked = jnp.concatenate([k_weight, v_weight, q_weight], axis=1)
    weights = lax.all_gather(stacked, "z", axis=0, tiled=True)

    n_core = lax.axis_size("core")
    rank = [h % n_core * (n_head // n_core) + h // n_core for h in range(n_head)]
    turned = [(z * n_head + h, rank[h] * n_z + z) for z in range(n_z) for h in range(n_head)]
    columns = lax.ppermute(out_weight.T, ("z",) + HEAD, turned)

    pieces = tokens.reshape(rows, n_x, part).transpose(1, 0, 2)
    pieces = lax.all_to_all(pieces, "x", split_axis=0, concat_axis=0, tiled=True)
    pieces = lax.all_gather(pieces.reshape(n_x * rows, part), HEAD, axis=0, tiled=False)
    pieces, columns = lax.optimization_barrier((pieces, columns))
    group = pieces.transpose(1, 0, 2).reshape(n_x * rows, n_head * part)

    columns = turned_over(lax.all_gather(columns, "x", axis=0, tiled=True))
    projection = lax.all_gather(columns, "z", axis=0, tiled=False)
    weights, group, _ = lax.optimization_barrier((weights, group, columns))

    def shares(piece):
        share = jnp.dot(group, piece, preferred_element_type=jnp.float32).astype(jnp.bfloat16)
        return share.reshape(n_x, rows, -1)

    key_value = shares(weights[:, : 2 * width])
    key_value = lax.all_to_all(key_value, "x", split_axis=0, concat_axis=0, tiled=True)
    query = shares(weights[:, 2 * width :])
    packed = pack(key_value, k_gain)
    query, packed = lax.optimization_barrier((query, packed))
    query = lax.all_to_all(query, "x", split_axis=0, concat_axis=0, tiled=True)
    count = lax.axis_size(SLAB)
    swaps = [
        [pair for i in range(first, count - 1, 2) for pair in ((i, i + 1), (i + 1, i))]
        for first in (1, 0)
    ]
    odd = lax.ppermute(packed, SLAB, swaps[0])
    even = lax.ppermute(copied(packed), SLAB, swaps[1])
    live = live_rows(key_tiles, rows // TILE)
    attended = attention(n_head // n_core, normed_query(query, q_gain), live, odd, packed, even)
    everyone = lax.all_to_all(attended, "y", split_axis=0, concat_axis=0, tiled=True)
    everyone = lax.all_gather(everyone, "core", axis=0, tiled=True)
    total = jnp.einsum("hrd,hdn->rn", everyone, projection, preferred_element_type=jnp.float32)
    return total.astype(jnp.bfloat16)


def solution(mesh):
    n_slab, n_head, n_cfg = (mesh.shape[a] for a in ("slab", "head", "cfg"))
    fine = Mesh(
        mesh.devices.reshape(n_slab // 4, 4, n_head // 2, 2, n_cfg), ("z", "x", "y", "core", "cfg")
    )
    placed = (
        P(("cfg",) + SLAB, HEAD),
        P(SLAB, HEAD),
        P(SLAB, HEAD),
        P(SLAB, HEAD),
        P(HEAD, SLAB),
        P(),
        P(),
        P(HEAD, SLAB, None),
    )
    return jax.shard_map(
        on_device, mesh=fine, in_specs=placed, out_specs=P(("cfg",) + SLAB, HEAD), check_vma=False
    )
```

```python
import jax
import jax.numpy as jnp
from jax import lax
from jax.experimental import pallas as pl
from jax.experimental.pallas import tpu as pltpu
from jax.sharding import Mesh
from jax.sharding import PartitionSpec as P

HDIM = 128
TILE = 64
HEAD = ("y", "core")
SLAB = ("z", "x")
MIB = 1024 * 1024


def whole_block(array):
    rank = len(array.shape)
    return pl.BlockSpec(array.shape, lambda *_: (0,) * rank)


def params(mib):
    return pltpu.CompilerParams(vmem_limit_bytes=mib * MIB)


def normed(total, gain):
    return total * lax.rsqrt(jnp.mean(total * total, axis=-1, keepdims=True) + 1e-06) * gain


def summed(ref, low, high):
    return jnp.sum(ref[:, :, low:high].astype(jnp.float32), axis=0)


def pack_kernel(share_ref, gain_ref, out_ref):
    width = out_ref.shape[1] // 2
    for low in range(0, width, HDIM):
        total = summed(share_ref, low, low + HDIM)
        out_ref[:, low : low + HDIM] = normed(total, gain_ref[...]).astype(jnp.bfloat16)
    out_ref[:, width:] = summed(share_ref, width, 2 * width).astype(jnp.bfloat16)


def pack(share, gain):
    return pl.pallas_call(
        pack_kernel,
        out_shape=jax.ShapeDtypeStruct(share.shape[1:], jnp.bfloat16),
        compiler_params=params(16),
    )(share, gain.reshape(1, HDIM))


def turn_kernel(source_ref, out_ref):
    out_ref[...] = source_ref[...].T


def turned_over(array):
    return pl.pallas_call(
        turn_kernel,
        out_shape=jax.ShapeDtypeStruct(array.shape[::-1], array.dtype),
        compiler_params=params(16),
    )(array)


def query_kernel(share_ref, gain_ref, out_ref):
    for low in range(0, out_ref.shape[1], HDIM):
        total = summed(share_ref, low, low + HDIM)
        out_ref[:, low : low + HDIM] = normed(total, gain_ref[...]).astype(jnp.bfloat16)


def normed_query(share, gain):
    return pl.pallas_call(
        query_kernel,
        out_shape=jax.ShapeDtypeStruct(share.shape[1:], jnp.bfloat16),
        compiler_params=params(16),
    )(share, gain.reshape(1, HDIM))


def copy_kernel(source_ref, out_ref):
    out_ref[...] = source_ref[...]


def copied(array):
    return pl.pallas_call(
        copy_kernel,
        out_shape=jax.ShapeDtypeStruct(array.shape, array.dtype),
        compiler_params=params(16),
    )(array)


def attention_kernel(query_ref, live_ref, odd_ref, own_ref, even_ref, out_ref):
    rows, width = out_ref.shape[1:]
    near = (odd_ref, own_ref, even_ref)
    tiles = rows // TILE
    scale = 1.0 / HDIM**0.5
    lows = range(0, width, HDIM)

    def weight_of(low, place):
        score = lax.dot_general(
            query_ref[:, low : low + HDIM],
            near[place][:, low : low + HDIM],
            (((1,), (1,)), ((), ())),
            preferred_element_type=jnp.float32,
        )
        allowed = [
            jnp.broadcast_to(
                live_ref[pl.ds(low // HDIM * tiles + t, 1), place * rows : (place + 1) * rows],
                (TILE, rows),
            )
            for t in range(tiles)
        ]
        return jnp.where(jnp.concatenate(allowed, axis=0) > 0, jnp.exp(score * scale), 0.0)

    weights = [[weight_of(low, place) for place in range(len(near))] for low in lows]
    for low, each in zip(lows, weights):
        total = jnp.sum(sum(each), axis=1, keepdims=True)
        mixed = sum(
            jnp.dot(
                weight.astype(jnp.bfloat16),
                ref[:, width + low : width + low + HDIM],
                preferred_element_type=jnp.float32,
            )
            for weight, ref in zip(each, near)
        )
        mixed = (mixed / total).astype(jnp.bfloat16)
        for copy in range(out_ref.shape[0]):
            out_ref[copy, :, low : low + HDIM] = mixed


def attention(copies, query, live, odd, own, even):
    rows, width = query.shape
    return pl.pallas_call(
        attention_kernel,
        out_shape=jax.ShapeDtypeStruct((copies, rows, width), jnp.bfloat16),
        compiler_params=params(16),
    )(query, live, odd, own, even)


def live_rows(key_tiles, tiles_here):
    slab = lax.axis_index(SLAB)
    even_at = jnp.where(slab % 2 == 0, slab + 1, slab - 1)
    slabs = jnp.stack([2 * slab - even_at, slab, even_at])
    near_ids = slabs[:, None] * tiles_here + jnp.arange(tiles_here, dtype=jnp.int32)
    near_ids = near_ids.reshape(-1)
    live = jnp.any(key_tiles[:, :, :, None] == near_ids[None, None, None, :], axis=2)
    live = live.reshape(-1, 3 * tiles_here).astype(jnp.float32)
    return jnp.repeat(live, TILE, axis=1)


def on_device(tokens, q_weight, k_weight, v_weight, out_weight, q_gain, k_gain, key_tiles):
    rows, width = tokens.shape
    n_x, n_z, n_head = (lax.axis_size(a) for a in ("x", "z", HEAD))
    part = width // n_x

    stacked = jnp.concatenate([k_weight, v_weight, q_weight], axis=1)
    weights = lax.all_gather(stacked, "z", axis=0, tiled=True)

    n_core = lax.axis_size("core")
    rank = [h % n_core * (n_head // n_core) + h // n_core for h in range(n_head)]
    turned = [(z * n_head + h, rank[h] * n_z + z) for z in range(n_z) for h in range(n_head)]
    columns = lax.ppermute(out_weight.T, ("z",) + HEAD, turned)

    pieces = tokens.reshape(rows, n_x, part).transpose(1, 0, 2)
    pieces = lax.all_to_all(pieces, "x", split_axis=0, concat_axis=0, tiled=True)
    pieces = lax.all_gather(pieces.reshape(n_x * rows, part), HEAD, axis=0, tiled=False)
    pieces, columns = lax.optimization_barrier((pieces, columns))
    group = pieces.transpose(1, 0, 2).reshape(n_x * rows, n_head * part)

    columns = jnp.broadcast_to(columns[None], (n_x,) + columns.shape)
    columns = lax.all_to_all(columns, "x", split_axis=0, concat_axis=0, tiled=True)
    columns = turned_over(columns.reshape(width, width))
    projection = lax.all_gather(columns, "z", axis=0, tiled=False)
    weights, group, _ = lax.optimization_barrier((weights, group, columns))

    def shares(piece):
        share = jnp.dot(group, piece, preferred_element_type=jnp.float32).astype(jnp.bfloat16)
        return share.reshape(n_x, rows, -1)

    key_value = shares(weights[:, : 2 * width])
    key_value = lax.all_to_all(key_value, "x", split_axis=0, concat_axis=0, tiled=True)
    query = shares(weights[:, 2 * width :])
    packed = pack(key_value, k_gain)
    query, packed = lax.optimization_barrier((query, packed))
    query = lax.all_to_all(query, "x", split_axis=0, concat_axis=0, tiled=True)
    count = lax.axis_size(SLAB)
    swaps = [
        [pair for i in range(first, count - 1, 2) for pair in ((i, i + 1), (i + 1, i))]
        for first in (1, 0)
    ]
    odd = lax.ppermute(packed, SLAB, swaps[0])
    even = lax.ppermute(copied(packed), SLAB, swaps[1])
    live = live_rows(key_tiles, rows // TILE)
    attended = attention(n_head // n_core, normed_query(query, q_gain), live, odd, packed, even)
    everyone = lax.all_to_all(attended, "y", split_axis=0, concat_axis=0, tiled=True)
    everyone = lax.all_gather(everyone, "core", axis=0, tiled=True)
    total = jnp.einsum("hrd,hdn->rn", everyone, projection, preferred_element_type=jnp.float32)
    return total.astype(jnp.bfloat16)


def solution(mesh):
    n_slab, n_head, n_cfg = (mesh.shape[a] for a in ("slab", "head", "cfg"))
    fine = Mesh(
        mesh.devices.reshape(n_slab // 4, 4, n_head // 2, 2, n_cfg), ("z", "x", "y", "core", "cfg")
    )
    placed = (
        P(("cfg",) + SLAB, HEAD),
        P(SLAB, HEAD),
        P(SLAB, HEAD),
        P(SLAB, HEAD),
        P(HEAD, SLAB),
        P(),
        P(),
        P(HEAD, SLAB, None),
    )
    return jax.shard_map(
        on_device, mesh=fine, in_specs=placed, out_specs=P(("cfg",) + SLAB, HEAD), check_vma=False
    )
```

```python
import jax
import jax.numpy as jnp
from jax import lax
from jax.experimental import pallas as pl
from jax.experimental.pallas import tpu as pltpu
from jax.sharding import Mesh
from jax.sharding import PartitionSpec as P

HDIM = 128
TILE = 64
HEAD = ("y", "core")
SLAB = ("z", "x")
MIB = 1024 * 1024


def whole_block(array):
    rank = len(array.shape)
    return pl.BlockSpec(array.shape, lambda *_: (0,) * rank)


def params(mib):
    return pltpu.CompilerParams(vmem_limit_bytes=mib * MIB)


def normed(total, gain):
    return total * lax.rsqrt(jnp.mean(total * total, axis=-1, keepdims=True) + 1e-06) * gain


def summed(ref, low, high):
    return jnp.sum(ref[:, :, low:high].astype(jnp.float32), axis=0)


def pack_kernel(share_ref, gain_ref, out_ref):
    width = out_ref.shape[1] // 2
    for low in range(0, width, HDIM):
        total = summed(share_ref, low, low + HDIM)
        out_ref[:, low : low + HDIM] = normed(total, gain_ref[...]).astype(jnp.bfloat16)
    out_ref[:, width:] = summed(share_ref, width, 2 * width).astype(jnp.bfloat16)


def pack(share, gain):
    return pl.pallas_call(
        pack_kernel,
        out_shape=jax.ShapeDtypeStruct(share.shape[1:], jnp.bfloat16),
        compiler_params=params(16),
    )(share, gain.reshape(1, HDIM))


def turn_kernel(source_ref, out_ref):
    out_ref[...] = source_ref[...].T


def turned_over(array):
    return pl.pallas_call(
        turn_kernel,
        out_shape=jax.ShapeDtypeStruct(array.shape[::-1], array.dtype),
        compiler_params=params(16),
    )(array)


def query_kernel(share_ref, gain_ref, out_ref):
    for low in range(0, out_ref.shape[1], HDIM):
        total = summed(share_ref, low, low + HDIM)
        out_ref[:, low : low + HDIM] = normed(total, gain_ref[...]).astype(jnp.bfloat16)


def normed_query(share, gain):
    return pl.pallas_call(
        query_kernel,
        out_shape=jax.ShapeDtypeStruct(share.shape[1:], jnp.bfloat16),
        compiler_params=params(16),
    )(share, gain.reshape(1, HDIM))


def copy_kernel(source_ref, out_ref):
    out_ref[...] = source_ref[...]


def copied(array):
    return pl.pallas_call(
        copy_kernel,
        out_shape=jax.ShapeDtypeStruct(array.shape, array.dtype),
        compiler_params=params(16),
    )(array)


def attention_kernel(query_ref, live_ref, odd_ref, own_ref, even_ref, out_ref):
    rows, width = out_ref.shape[1:]
    near = (odd_ref, own_ref, even_ref)
    tiles = rows // TILE
    scale = 1.0 / HDIM**0.5
    lows = range(0, width, HDIM)

    def weight_of(low, place):
        score = lax.dot_general(
            query_ref[:, low : low + HDIM],
            near[place][:, low : low + HDIM],
            (((1,), (1,)), ((), ())),
            preferred_element_type=jnp.float32,
        )
        allowed = [
            jnp.broadcast_to(
                live_ref[pl.ds(low // HDIM * tiles + t, 1), place * rows : (place + 1) * rows],
                (TILE, rows),
            )
            for t in range(tiles)
        ]
        return jnp.where(jnp.concatenate(allowed, axis=0) > 0, jnp.exp(score * scale), 0.0)

    weights = [[weight_of(low, place) for place in range(len(near))] for low in lows]
    for low, each in zip(lows, weights):
        total = jnp.sum(sum(each), axis=1, keepdims=True)
        mixed = sum(
            jnp.dot(
                weight.astype(jnp.bfloat16),
                ref[:, width + low : width + low + HDIM],
                preferred_element_type=jnp.float32,
            )
            for weight, ref in zip(each, near)
        )
        mixed = (mixed / total).astype(jnp.bfloat16)
        for copy in range(out_ref.shape[0]):
            out_ref[copy, :, low : low + HDIM] = mixed


def attention(copies, query, live, odd, own, even):
    rows, width = query.shape
    return pl.pallas_call(
        attention_kernel,
        out_shape=jax.ShapeDtypeStruct((copies, rows, width), jnp.bfloat16),
        compiler_params=params(16),
    )(query, live, odd, own, even)


def live_rows(key_tiles, tiles_here):
    slab = lax.axis_index(SLAB)
    even_at = jnp.where(slab % 2 == 0, slab + 1, slab - 1)
    slabs = jnp.stack([2 * slab - even_at, slab, even_at])
    near_ids = slabs[:, None] * tiles_here + jnp.arange(tiles_here, dtype=jnp.int32)
    near_ids = near_ids.reshape(-1)
    live = jnp.any(key_tiles[:, :, :, None] == near_ids[None, None, None, :], axis=2)
    live = live.reshape(-1, 3 * tiles_here).astype(jnp.float32)
    return jnp.repeat(live, TILE, axis=1)


def on_device(tokens, q_weight, k_weight, v_weight, out_weight, q_gain, k_gain, key_tiles):
    rows, width = tokens.shape
    n_x, n_z, n_head = (lax.axis_size(a) for a in ("x", "z", HEAD))
    part = width // n_x

    stacked = jnp.concatenate([k_weight, v_weight, q_weight], axis=1)
    weights = lax.all_gather(stacked, "z", axis=0, tiled=True)

    n_core = lax.axis_size("core")
    n_y = n_head // n_core

    def place_of(head, column):
        return head % n_core * n_y + (head // n_core ^ column // n_core)

    turned = [
        (z * n_head + h, place_of(h, z) * n_z + z) for z in range(n_z) for h in range(n_head)
    ]
    columns = lax.ppermute(out_weight.T, ("z",) + HEAD, turned)

    pieces = tokens.reshape(rows, n_x, part).transpose(1, 0, 2)
    pieces = lax.all_to_all(pieces, "x", split_axis=0, concat_axis=0, tiled=True)
    pieces = lax.all_gather(pieces.reshape(n_x * rows, part), HEAD, axis=0, tiled=False)
    pieces, columns = lax.optimization_barrier((pieces, columns))
    group = pieces.transpose(1, 0, 2).reshape(n_x * rows, n_head * part)

    columns = turned_over(lax.all_gather(columns, "x", axis=0, tiled=True))
    projection = lax.all_gather(columns, "z", axis=0, tiled=False)
    weights, group, _ = lax.optimization_barrier((weights, group, columns))

    def shares(piece):
        share = jnp.dot(group, piece, preferred_element_type=jnp.float32).astype(jnp.bfloat16)
        return share.reshape(n_x, rows, -1)

    key_value = shares(weights[:, : 2 * width])
    key_value = lax.all_to_all(key_value, "x", split_axis=0, concat_axis=0, tiled=True)
    query = shares(weights[:, 2 * width :])
    packed = pack(key_value, k_gain)
    query, packed = lax.optimization_barrier((query, packed))
    query = lax.all_to_all(query, "x", split_axis=0, concat_axis=0, tiled=True)
    count = lax.axis_size(SLAB)
    swaps = [
        [pair for i in range(first, count - 1, 2) for pair in ((i, i + 1), (i + 1, i))]
        for first in (1, 0)
    ]
    odd = lax.ppermute(packed, SLAB, swaps[0])
    even = lax.ppermute(copied(packed), SLAB, swaps[1])
    live = live_rows(key_tiles, rows // TILE)
    attended = attention(1, normed_query(query, q_gain), live, odd, packed, even)
    line = [
        lax.ppermute(attended, "y", [(i, i ^ step) for i in range(n_y)]) for step in range(1, n_y)
    ]
    everyone = jnp.concatenate([attended, *line], axis=0)
    everyone = lax.all_gather(everyone, "core", axis=0, tiled=True)
    total = jnp.einsum("hrd,hdn->rn", everyone, projection, preferred_element_type=jnp.float32)
    return total.astype(jnp.bfloat16)


def solution(mesh):
    n_slab, n_head, n_cfg = (mesh.shape[a] for a in ("slab", "head", "cfg"))
    fine = Mesh(
        mesh.devices.reshape(n_slab // 4, 4, n_head // 2, 2, n_cfg), ("z", "x", "y", "core", "cfg")
    )
    placed = (
        P(("cfg",) + SLAB, HEAD),
        P(SLAB, HEAD),
        P(SLAB, HEAD),
        P(SLAB, HEAD),
        P(HEAD, SLAB),
        P(),
        P(),
        P(HEAD, SLAB, None),
    )
    return jax.shard_map(
        on_device, mesh=fine, in_specs=placed, out_specs=P(("cfg",) + SLAB, HEAD), check_vma=False
    )
```

```python
import jax
import jax.numpy as jnp
from jax import lax
from jax.experimental import pallas as pl
from jax.experimental.pallas import tpu as pltpu
from jax.sharding import Mesh
from jax.sharding import PartitionSpec as P

HDIM = 128
TILE = 64
HEAD = ("y", "core")
SLAB = ("z", "x")
MIB = 1024 * 1024


def whole_block(array):
    rank = len(array.shape)
    return pl.BlockSpec(array.shape, lambda *_: (0,) * rank)


def params(mib):
    return pltpu.CompilerParams(vmem_limit_bytes=mib * MIB)


def normed(total, gain):
    return total * lax.rsqrt(jnp.mean(total * total, axis=-1, keepdims=True) + 1e-06) * gain


def summed(ref, low, high):
    return jnp.sum(ref[:, :, low:high].astype(jnp.float32), axis=0)


def pack_kernel(share_ref, gain_ref, out_ref):
    width = out_ref.shape[1] // 2
    for low in range(0, width, HDIM):
        total = summed(share_ref, low, low + HDIM)
        out_ref[:, low : low + HDIM] = normed(total, gain_ref[...]).astype(jnp.bfloat16)
    out_ref[:, width:] = summed(share_ref, width, 2 * width).astype(jnp.bfloat16)


def pack(share, gain):
    return pl.pallas_call(
        pack_kernel,
        out_shape=jax.ShapeDtypeStruct(share.shape[1:], jnp.bfloat16),
        compiler_params=params(16),
    )(share, gain.reshape(1, HDIM))


def turn_kernel(source_ref, out_ref):
    out_ref[...] = source_ref[...].T


def turned_over(array):
    return pl.pallas_call(
        turn_kernel,
        out_shape=jax.ShapeDtypeStruct(array.shape[::-1], array.dtype),
        compiler_params=params(16),
    )(array)


def query_kernel(share_ref, gain_ref, out_ref):
    for low in range(0, out_ref.shape[1], HDIM):
        total = summed(share_ref, low, low + HDIM)
        out_ref[:, low : low + HDIM] = normed(total, gain_ref[...]).astype(jnp.bfloat16)


def normed_query(share, gain):
    return pl.pallas_call(
        query_kernel,
        out_shape=jax.ShapeDtypeStruct(share.shape[1:], jnp.bfloat16),
        compiler_params=params(16),
    )(share, gain.reshape(1, HDIM))


def copy_kernel(source_ref, out_ref):
    out_ref[...] = source_ref[...]


def copied(array):
    return pl.pallas_call(
        copy_kernel,
        out_shape=jax.ShapeDtypeStruct(array.shape, array.dtype),
        compiler_params=params(16),
    )(array)


def attention_kernel(query_ref, live_ref, odd_ref, own_ref, even_ref, out_ref):
    rows, width = out_ref.shape[1:]
    near = (odd_ref, own_ref, even_ref)
    tiles = rows // TILE
    scale = 1.0 / HDIM**0.5
    lows = range(0, width, HDIM)

    def weight_of(low, place):
        score = lax.dot_general(
            query_ref[:, low : low + HDIM],
            near[place][:, low : low + HDIM],
            (((1,), (1,)), ((), ())),
            preferred_element_type=jnp.float32,
        )
        allowed = [
            jnp.broadcast_to(
                live_ref[pl.ds(low // HDIM * tiles + t, 1), place * rows : (place + 1) * rows],
                (TILE, rows),
            )
            for t in range(tiles)
        ]
        return jnp.where(jnp.concatenate(allowed, axis=0) > 0, jnp.exp(score * scale), 0.0)

    weights = [[weight_of(low, place) for place in range(len(near))] for low in lows]
    for low, each in zip(lows, weights):
        total = jnp.sum(sum(each), axis=1, keepdims=True)
        mixed = sum(
            jnp.dot(
                weight.astype(jnp.bfloat16),
                ref[:, width + low : width + low + HDIM],
                preferred_element_type=jnp.float32,
            )
            for weight, ref in zip(each, near)
        )
        mixed = (mixed / total).astype(jnp.bfloat16)
        for copy in range(out_ref.shape[0]):
            out_ref[copy, :, low : low + HDIM] = mixed


def attention(copies, query, live, odd, own, even):
    rows, width = query.shape
    return pl.pallas_call(
        attention_kernel,
        out_shape=jax.ShapeDtypeStruct((copies, rows, width), jnp.bfloat16),
        compiler_params=params(16),
    )(query, live, odd, own, even)


def live_rows(key_tiles, tiles_here):
    slab = lax.axis_index(SLAB)
    even_at = jnp.where(slab % 2 == 0, slab + 1, slab - 1)
    slabs = jnp.stack([2 * slab - even_at, slab, even_at])
    near_ids = slabs[:, None] * tiles_here + jnp.arange(tiles_here, dtype=jnp.int32)
    near_ids = near_ids.reshape(-1)
    live = jnp.any(key_tiles[:, :, :, None] == near_ids[None, None, None, :], axis=2)
    live = live.reshape(-1, 3 * tiles_here).astype(jnp.float32)
    return jnp.repeat(live, TILE, axis=1)


def on_device(tokens, q_weight, k_weight, v_weight, out_weight, q_gain, k_gain, key_tiles):
    rows, width = tokens.shape
    n_x, n_z, n_head = (lax.axis_size(a) for a in ("x", "z", HEAD))
    part = width // n_x

    stacked = jnp.concatenate([k_weight, v_weight, q_weight], axis=1)
    weights = lax.all_gather(stacked, "z", axis=0, tiled=True)

    n_core = lax.axis_size("core")
    rank = [h % n_core * (n_head // n_core) + h // n_core for h in range(n_head)]
    turned = [(z * n_head + h, rank[h] * n_z + z) for z in range(n_z) for h in range(n_head)]
    columns = lax.ppermute(out_weight.T, ("z",) + HEAD, turned)

    pieces = tokens.reshape(rows, n_x, part).transpose(1, 0, 2)
    pieces = lax.all_to_all(pieces, "x", split_axis=0, concat_axis=0, tiled=True)
    pieces = lax.all_gather(pieces.reshape(n_x * rows, part), HEAD, axis=0, tiled=False)
    pieces, columns = lax.optimization_barrier((pieces, columns))
    group = copied(pieces.transpose(1, 0, 2).reshape(n_x * rows, n_head * part))

    columns = jnp.broadcast_to(columns[None], (n_x,) + columns.shape)
    columns = lax.all_to_all(columns, "x", split_axis=0, concat_axis=0, tiled=True)
    columns = turned_over(columns.reshape(width, width))
    projection = lax.all_gather(columns, "z", axis=0, tiled=False)
    weights, group, _ = lax.optimization_barrier((weights, group, columns))

    def shares(piece):
        share = jnp.dot(group, piece, preferred_element_type=jnp.float32).astype(jnp.bfloat16)
        return share.reshape(n_x, rows, -1)

    key_value = shares(weights[:, : 2 * width])
    key_value = lax.all_to_all(key_value, "x", split_axis=0, concat_axis=0, tiled=True)
    query = shares(weights[:, 2 * width :])
    packed = pack(key_value, k_gain)
    query, packed = lax.optimization_barrier((query, packed))
    query = lax.all_to_all(query, "x", split_axis=0, concat_axis=0, tiled=True)
    count = lax.axis_size(SLAB)
    swaps = [
        [pair for i in range(first, count - 1, 2) for pair in ((i, i + 1), (i + 1, i))]
        for first in (1, 0)
    ]
    odd = lax.ppermute(packed, SLAB, swaps[0])
    even = lax.ppermute(copied(packed), SLAB, swaps[1])
    live = live_rows(key_tiles, rows // TILE)
    attended = attention(n_head // n_core, normed_query(query, q_gain), live, odd, packed, even)
    everyone = lax.all_to_all(attended, "y", split_axis=0, concat_axis=0, tiled=True)
    everyone = lax.all_gather(everyone, "core", axis=0, tiled=True)
    total = jnp.einsum("hrd,hdn->rn", everyone, projection, preferred_element_type=jnp.float32)
    return total.astype(jnp.bfloat16)


def solution(mesh):
    n_slab, n_head, n_cfg = (mesh.shape[a] for a in ("slab", "head", "cfg"))
    fine = Mesh(
        mesh.devices.reshape(n_slab // 4, 4, n_head // 2, 2, n_cfg), ("z", "x", "y", "core", "cfg")
    )
    placed = (
        P(("cfg",) + SLAB, HEAD),
        P(SLAB, HEAD),
        P(SLAB, HEAD),
        P(SLAB, HEAD),
        P(HEAD, SLAB),
        P(),
        P(),
        P(HEAD, SLAB, None),
    )
    return jax.shard_map(
        on_device, mesh=fine, in_specs=placed, out_specs=P(("cfg",) + SLAB, HEAD), check_vma=False
    )
```

```python
import jax
import jax.numpy as jnp
from jax import lax
from jax.experimental import pallas as pl
from jax.experimental.pallas import tpu as pltpu
from jax.sharding import Mesh
from jax.sharding import PartitionSpec as P

HDIM = 128
TILE = 64
HEAD = ("y", "core")
SLAB = ("z", "x")
MIB = 1024 * 1024


def whole_block(array):
    rank = len(array.shape)
    return pl.BlockSpec(array.shape, lambda *_: (0,) * rank)


def params(mib):
    return pltpu.CompilerParams(vmem_limit_bytes=mib * MIB)


def normed(total, gain):
    return total * lax.rsqrt(jnp.mean(total * total, axis=-1, keepdims=True) + 1e-06) * gain


def summed(ref, low, high):
    return jnp.sum(ref[:, :, low:high].astype(jnp.float32), axis=0)


def pack_kernel(share_ref, gain_ref, out_ref):
    width = out_ref.shape[1] // 2
    for low in range(0, width, HDIM):
        total = summed(share_ref, low, low + HDIM)
        out_ref[:, low : low + HDIM] = normed(total, gain_ref[...]).astype(jnp.bfloat16)
    out_ref[:, width:] = summed(share_ref, width, 2 * width).astype(jnp.bfloat16)


def pack(share, gain):
    return pl.pallas_call(
        pack_kernel,
        out_shape=jax.ShapeDtypeStruct(share.shape[1:], jnp.bfloat16),
        compiler_params=params(16),
    )(share, gain.reshape(1, HDIM))


def turn_kernel(source_ref, out_ref):
    out_ref[...] = source_ref[...].T


def turned_over(array):
    return pl.pallas_call(
        turn_kernel,
        out_shape=jax.ShapeDtypeStruct(array.shape[::-1], array.dtype),
        compiler_params=params(16),
    )(array)


def query_kernel(share_ref, gain_ref, out_ref):
    for low in range(0, out_ref.shape[1], HDIM):
        total = summed(share_ref, low, low + HDIM)
        out_ref[:, low : low + HDIM] = normed(total, gain_ref[...]).astype(jnp.bfloat16)


def normed_query(share, gain):
    return pl.pallas_call(
        query_kernel,
        out_shape=jax.ShapeDtypeStruct(share.shape[1:], jnp.bfloat16),
        compiler_params=params(16),
    )(share, gain.reshape(1, HDIM))


def copy_kernel(source_ref, out_ref):
    out_ref[...] = source_ref[...]


def copied(array):
    return pl.pallas_call(
        copy_kernel,
        out_shape=jax.ShapeDtypeStruct(array.shape, array.dtype),
        compiler_params=params(16),
    )(array)


def attention_kernel(query_ref, live_ref, odd_ref, own_ref, even_ref, out_ref):
    rows, width = out_ref.shape[1:]
    near = (odd_ref, own_ref, even_ref)
    tiles = rows // TILE
    scale = 1.0 / HDIM**0.5
    lows = range(0, width, HDIM)

    def weight_of(low, place):
        score = lax.dot_general(
            query_ref[:, low : low + HDIM],
            near[place][:, low : low + HDIM],
            (((1,), (1,)), ((), ())),
            preferred_element_type=jnp.float32,
        )
        allowed = [
            jnp.broadcast_to(
                live_ref[pl.ds(low // HDIM * tiles + t, 1), place * rows : (place + 1) * rows],
                (TILE, rows),
            )
            for t in range(tiles)
        ]
        return jnp.where(jnp.concatenate(allowed, axis=0) > 0, jnp.exp(score * scale), 0.0)

    weights = [[weight_of(low, place) for place in range(len(near))] for low in lows]
    for low, each in zip(lows, weights):
        total = jnp.sum(sum(each), axis=1, keepdims=True)
        mixed = sum(
            jnp.dot(
                weight.astype(jnp.bfloat16),
                ref[:, width + low : width + low + HDIM],
                preferred_element_type=jnp.float32,
            )
            for weight, ref in zip(each, near)
        )
        mixed = (mixed / total).astype(jnp.bfloat16)
        for copy in range(out_ref.shape[0]):
            out_ref[copy, :, low : low + HDIM] = mixed


def attention(copies, query, live, odd, own, even):
    rows, width = query.shape
    return pl.pallas_call(
        attention_kernel,
        out_shape=jax.ShapeDtypeStruct((copies, rows, width), jnp.bfloat16),
        compiler_params=params(16),
    )(query, live, odd, own, even)


def live_rows(key_tiles, tiles_here):
    slab = lax.axis_index(SLAB)
    even_at = jnp.where(slab % 2 == 0, slab + 1, slab - 1)
    slabs = jnp.stack([2 * slab - even_at, slab, even_at])
    near_ids = slabs[:, None] * tiles_here + jnp.arange(tiles_here, dtype=jnp.int32)
    near_ids = near_ids.reshape(-1)
    live = jnp.any(key_tiles[:, :, :, None] == near_ids[None, None, None, :], axis=2)
    live = live.reshape(-1, 3 * tiles_here).astype(jnp.float32)
    return jnp.repeat(live, TILE, axis=1)


def on_device(tokens, q_weight, k_weight, v_weight, out_weight, q_gain, k_gain, key_tiles):
    rows, width = tokens.shape
    n_x, n_z, n_head = (lax.axis_size(a) for a in ("x", "z", HEAD))
    part = width // n_x

    stacked = jnp.concatenate([k_weight, v_weight, q_weight], axis=1)
    weights = lax.all_gather(stacked, "z", axis=0, tiled=True)

    n_core = lax.axis_size("core")
    n_y = n_head // n_core

    def place_of(head, column):
        return (head + column) % n_core * n_y + head // n_core

    turned = [
        (z * n_head + h, place_of(h, z) * n_z + z) for z in range(n_z) for h in range(n_head)
    ]
    columns = lax.ppermute(out_weight.T, ("z",) + HEAD, turned)

    pieces = tokens.reshape(rows, n_x, part).transpose(1, 0, 2)
    pieces = lax.all_to_all(pieces, "x", split_axis=0, concat_axis=0, tiled=True)
    pieces = lax.all_gather(pieces.reshape(n_x * rows, part), HEAD, axis=0, tiled=False)
    pieces, columns = lax.optimization_barrier((pieces, columns))
    group = copied(pieces.transpose(1, 0, 2).reshape(n_x * rows, n_head * part))

    columns = jnp.broadcast_to(columns[None], (n_x,) + columns.shape)
    columns = lax.all_to_all(columns, "x", split_axis=0, concat_axis=0, tiled=True)
    columns = turned_over(columns.reshape(width, width))
    projection = lax.all_gather(columns, "z", axis=0, tiled=False)
    weights, group, _ = lax.optimization_barrier((weights, group, columns))

    def shares(piece):
        share = jnp.dot(group, piece, preferred_element_type=jnp.float32).astype(jnp.bfloat16)
        return share.reshape(n_x, rows, -1)

    key_value = shares(weights[:, : 2 * width])
    key_value = lax.all_to_all(key_value, "x", split_axis=0, concat_axis=0, tiled=True)
    query = shares(weights[:, 2 * width :])
    packed = pack(key_value, k_gain)
    query, packed = lax.optimization_barrier((query, packed))
    query = lax.all_to_all(query, "x", split_axis=0, concat_axis=0, tiled=True)
    count = lax.axis_size(SLAB)
    swaps = [
        [pair for i in range(first, count - 1, 2) for pair in ((i, i + 1), (i + 1, i))]
        for first in (1, 0)
    ]
    odd = lax.ppermute(packed, SLAB, swaps[0])
    even = lax.ppermute(copied(packed), SLAB, swaps[1])
    live = live_rows(key_tiles, rows // TILE)
    attended = attention(n_head // n_core, normed_query(query, q_gain), live, odd, packed, even)
    everyone = lax.all_to_all(attended, "y", split_axis=0, concat_axis=0, tiled=True)
    other = lax.ppermute(everyone, "core", [(i, (i + 1) % n_core) for i in range(n_core)])
    everyone = jnp.concatenate([everyone, other], axis=0)
    total = jnp.einsum("hrd,hdn->rn", everyone, projection, preferred_element_type=jnp.float32)
    return total.astype(jnp.bfloat16)


def solution(mesh):
    n_slab, n_head, n_cfg = (mesh.shape[a] for a in ("slab", "head", "cfg"))
    fine = Mesh(
        mesh.devices.reshape(n_slab // 4, 4, n_head // 2, 2, n_cfg), ("z", "x", "y", "core", "cfg")
    )
    placed = (
        P(("cfg",) + SLAB, HEAD),
        P(SLAB, HEAD),
        P(SLAB, HEAD),
        P(SLAB, HEAD),
        P(HEAD, SLAB),
        P(),
        P(),
        P(HEAD, SLAB, None),
    )
    return jax.shard_map(
        on_device, mesh=fine, in_specs=placed, out_specs=P(("cfg",) + SLAB, HEAD), check_vma=False
    )
```

```python
import jax
import jax.numpy as jnp
from jax import lax
from jax.experimental import pallas as pl
from jax.experimental.pallas import tpu as pltpu
from jax.sharding import Mesh
from jax.sharding import PartitionSpec as P

HDIM = 128
TILE = 64
HEAD = ("y", "core")
SLAB = ("z", "x")
MIB = 1024 * 1024


def whole_block(array):
    rank = len(array.shape)
    return pl.BlockSpec(array.shape, lambda *_: (0,) * rank)


def params(mib):
    return pltpu.CompilerParams(vmem_limit_bytes=mib * MIB)


def normed(total, gain):
    return total * lax.rsqrt(jnp.mean(total * total, axis=-1, keepdims=True) + 1e-06) * gain


def summed(ref, low, high):
    return jnp.sum(ref[:, :, low:high].astype(jnp.float32), axis=0)


def pack_kernel(share_ref, gain_ref, out_ref):
    width = out_ref.shape[1] // 2
    for low in range(0, width, HDIM):
        total = summed(share_ref, low, low + HDIM)
        out_ref[:, low : low + HDIM] = normed(total, gain_ref[...]).astype(jnp.bfloat16)
    out_ref[:, width:] = summed(share_ref, width, 2 * width).astype(jnp.bfloat16)


def pack(share, gain):
    return pl.pallas_call(
        pack_kernel,
        out_shape=jax.ShapeDtypeStruct(share.shape[1:], jnp.bfloat16),
        compiler_params=params(16),
    )(share, gain.reshape(1, HDIM))


def turn_kernel(source_ref, out_ref):
    out_ref[...] = source_ref[...].T


def turned_over(array):
    return pl.pallas_call(
        turn_kernel,
        out_shape=jax.ShapeDtypeStruct(array.shape[::-1], array.dtype),
        compiler_params=params(16),
    )(array)


def query_kernel(share_ref, gain_ref, out_ref):
    for low in range(0, out_ref.shape[1], HDIM):
        total = summed(share_ref, low, low + HDIM)
        out_ref[:, low : low + HDIM] = normed(total, gain_ref[...]).astype(jnp.bfloat16)


def normed_query(share, gain):
    return pl.pallas_call(
        query_kernel,
        out_shape=jax.ShapeDtypeStruct(share.shape[1:], jnp.bfloat16),
        compiler_params=params(16),
    )(share, gain.reshape(1, HDIM))


def copy_kernel(source_ref, out_ref):
    out_ref[...] = source_ref[...]


def copied(array):
    return pl.pallas_call(
        copy_kernel,
        out_shape=jax.ShapeDtypeStruct(array.shape, array.dtype),
        compiler_params=params(16),
    )(array)


def attention_kernel(query_ref, live_ref, odd_ref, own_ref, even_ref, out_ref):
    rows, width = out_ref.shape[1:]
    near = (odd_ref, own_ref, even_ref)
    tiles = rows // TILE
    scale = 1.0 / HDIM**0.5
    lows = range(0, width, HDIM)

    def weight_of(low, place):
        score = lax.dot_general(
            query_ref[:, low : low + HDIM],
            near[place][:, low : low + HDIM],
            (((1,), (1,)), ((), ())),
            preferred_element_type=jnp.float32,
        )
        allowed = [
            jnp.broadcast_to(
                live_ref[pl.ds(low // HDIM * tiles + t, 1), place * rows : (place + 1) * rows],
                (TILE, rows),
            )
            for t in range(tiles)
        ]
        return jnp.where(jnp.concatenate(allowed, axis=0) > 0, jnp.exp(score * scale), 0.0)

    weights = [[weight_of(low, place) for place in range(len(near))] for low in lows]
    for low, each in zip(lows, weights):
        total = jnp.sum(sum(each), axis=1, keepdims=True)
        mixed = sum(
            jnp.dot(
                weight.astype(jnp.bfloat16),
                ref[:, width + low : width + low + HDIM],
                preferred_element_type=jnp.float32,
            )
            for weight, ref in zip(each, near)
        )
        mixed = (mixed / total).astype(jnp.bfloat16)
        for copy in range(out_ref.shape[0]):
            out_ref[copy, :, low : low + HDIM] = mixed


def attention(copies, query, live, odd, own, even):
    rows, width = query.shape
    return pl.pallas_call(
        attention_kernel,
        out_shape=jax.ShapeDtypeStruct((copies, rows, width), jnp.bfloat16),
        compiler_params=params(16),
    )(query, live, odd, own, even)


def live_rows(key_tiles, tiles_here):
    slab = lax.axis_index(SLAB)
    even_at = jnp.where(slab % 2 == 0, slab + 1, slab - 1)
    slabs = jnp.stack([2 * slab - even_at, slab, even_at])
    near_ids = slabs[:, None] * tiles_here + jnp.arange(tiles_here, dtype=jnp.int32)
    near_ids = near_ids.reshape(-1)
    live = jnp.any(key_tiles[:, :, :, None] == near_ids[None, None, None, :], axis=2)
    live = live.reshape(-1, 3 * tiles_here).astype(jnp.float32)
    return jnp.repeat(live, TILE, axis=1)


def on_device(tokens, q_weight, k_weight, v_weight, out_weight, q_gain, k_gain, key_tiles):
    rows, width = tokens.shape
    n_x, n_z, n_head = (lax.axis_size(a) for a in ("x", "z", HEAD))
    part = width // n_x

    stacked = jnp.concatenate([k_weight, v_weight, q_weight], axis=1)
    weights = lax.all_gather(stacked, "z", axis=0, tiled=True)

    n_core = lax.axis_size("core")
    rank = [h % n_core * (n_head // n_core) + h // n_core for h in range(n_head)]
    turned = [(z * n_head + h, rank[h] * n_z + z) for z in range(n_z) for h in range(n_head)]
    columns = lax.ppermute(out_weight.T, ("z",) + HEAD, turned)

    pieces = tokens.reshape(rows, n_x, part).transpose(1, 0, 2)
    pieces = lax.all_to_all(pieces, "x", split_axis=0, concat_axis=0, tiled=True)
    pieces = lax.all_gather(pieces.reshape(n_x * rows, part), HEAD, axis=0, tiled=False)
    group = copied(pieces.transpose(1, 0, 2).reshape(n_x * rows, n_head * part))

    columns = jnp.broadcast_to(columns[None], (n_x,) + columns.shape)
    columns = lax.all_to_all(columns, "x", split_axis=0, concat_axis=0, tiled=True)
    columns = turned_over(columns.reshape(width, width))
    projection = lax.all_gather(columns, "z", axis=0, tiled=False)
    weights, group, _ = lax.optimization_barrier((weights, group, columns))

    def shares(piece):
        share = jnp.dot(group, piece, preferred_element_type=jnp.float32).astype(jnp.bfloat16)
        return share.reshape(n_x, rows, -1)

    key_value = shares(weights[:, : 2 * width])
    key_value = lax.all_to_all(key_value, "x", split_axis=0, concat_axis=0, tiled=True)
    query = shares(weights[:, 2 * width :])
    packed = pack(key_value, k_gain)
    query, packed = lax.optimization_barrier((query, packed))
    query = lax.all_to_all(query, "x", split_axis=0, concat_axis=0, tiled=True)
    count = lax.axis_size(SLAB)
    swaps = [
        [pair for i in range(first, count - 1, 2) for pair in ((i, i + 1), (i + 1, i))]
        for first in (1, 0)
    ]
    odd = lax.ppermute(packed, SLAB, swaps[0])
    even = lax.ppermute(copied(packed), SLAB, swaps[1])
    live = live_rows(key_tiles, rows // TILE)
    attended = attention(n_head // n_core, normed_query(query, q_gain), live, odd, packed, even)
    everyone = lax.all_to_all(attended, "y", split_axis=0, concat_axis=0, tiled=True)
    everyone = lax.all_gather(everyone, "core", axis=0, tiled=True)
    total = jnp.einsum("hrd,hdn->rn", everyone, projection, preferred_element_type=jnp.float32)
    return total.astype(jnp.bfloat16)


def solution(mesh):
    n_slab, n_head, n_cfg = (mesh.shape[a] for a in ("slab", "head", "cfg"))
    fine = Mesh(
        mesh.devices.reshape(n_slab // 4, 4, n_head // 2, 2, n_cfg), ("z", "x", "y", "core", "cfg")
    )
    placed = (
        P(("cfg",) + SLAB, HEAD),
        P(SLAB, HEAD),
        P(SLAB, HEAD),
        P(SLAB, HEAD),
        P(HEAD, SLAB),
        P(),
        P(),
        P(HEAD, SLAB, None),
    )
    return jax.shard_map(
        on_device, mesh=fine, in_specs=placed, out_specs=P(("cfg",) + SLAB, HEAD), check_vma=False
    )
```
